32 devices in a mesh: rep: 8 (over z, core), shard: 4 (over y, x).
Axes of the slice: x: 2, y: 2, z: 4, core: 2. Of those that a mesh axis runs over, the one named last changes fastest.
Arguments:
- tokens_in: bfloat16 [8192, 1024], P(('rep', 'shard')), may hold values from -6 to 6
- cotangent: bfloat16 [8192, 1024], P(('rep', 'shard')), may hold values from -6 to 6
- deal_order: int32 [8192], replicated, may hold values from 0 to 8191, as said below
- lengths: int32 [8], replicated, may hold values from 1 to 2048, 8192 in all
- decay_rates: float32 [8], replicated, may hold values from 0.00012207031 to 0.03
- w_query: bfloat16 [1024, 1024], P('shard'), may hold values from -0.1875 to 0.1875
- w_key: bfloat16 [1024, 1024], P('shard'), may hold values from -0.1875 to 0.1875
- w_value: bfloat16 [1024, 1024], P('shard'), may hold values from -0.1875 to 0.1875
- w_ugate: bfloat16 [1024, 1024], P('shard'), may hold values from -0.1875 to 0.1875
- w_out: bfloat16 [1024, 1024], P('shard'), may hold values from -0.1875 to 0.1875
- w_ffin: bfloat16 [1024, 5632], P('shard'), may hold values from -0.1875 to 0.1875
- w_ffdown: bfloat16 [2816, 1024], P('shard'), may hold values from -0.109375 to 0.109375
Outputs:
- output: bfloat16 [8192, 1024], P(('rep', 'shard'))
- input_grad: bfloat16 [8192, 1024], P(('rep', 'shard'))
- grad_query: float32 [1024, 1024], P('shard')
- grad_key: float32 [1024, 1024], P('shard')
- grad_value: float32 [1024, 1024], P('shard')
- grad_ugate: float32 [1024, 1024], P('shard')
- grad_out: float32 [1024, 1024], P('shard')
- grad_ffin: float32 [1024, 5632], P('shard')
- grad_ffdown: float32 [2816, 1024], P('shard')
The draws below stay inside these ranges and needn't reach their ends.
Inputs may be any that keep to these rules, and one draw needn't show every extreme that they name: deal_order holds each row once; every 256 consecutive entries hold exactly 8 rows of each block of 256 rows of the given order. The lengths sum to 8192.
All inputs are finite; a program needn't handle non-finite values.
Results may differ from the reference program's by a relative error of at most 0.022.
Values may be sent and summed in bfloat16 or wider, within the bound.
No kernel may reach another device: no remote copies, remote signals or barrier semaphores. Data moves between devices by JAX's collectives and lax.ppermute only.
A program may use at most 256 MiB of HBM per device.

```python
import math
from functools import partial
import jax
import jax.numpy as jnp
import numpy as np
from jax import lax

D = 1024
HEADS = 8
HEAD = 128
FF = 2816
BLOCK = 256
TOK_DEV = 256
TOKENS = 8192
NSEQ = 8
MAXLEN = 2048


def draw_deal_order(key, part):
    blocks = TOKENS // TOK_DEV
    src_keys = jax.random.split(jax.random.fold_in(key, 11), blocks)
    dst_keys = jax.random.split(jax.random.fold_in(key, 12), blocks)
    shuffled = jax.vmap(lambda one_key: jax.random.permutation(one_key, TOK_DEV))(src_keys).astype(jnp.int32)
    shuffled = shuffled + (jnp.arange(blocks, dtype=jnp.int32) * TOK_DEV)[:, None]
    grouped = shuffled.reshape(blocks, blocks, TOK_DEV // blocks).transpose(1, 0, 2).reshape(blocks, TOK_DEV)
    mixing = jax.vmap(lambda one_key: jax.random.permutation(one_key, TOK_DEV))(dst_keys).astype(jnp.int32)
    dealt_rows = jnp.take_along_axis(grouped, mixing, axis=1)
    return dealt_rows.reshape(TOKENS).astype(jnp.int32)


def block_levels(stream_key, extent, shards, low, high):
    loudness = 1.0
    for dim, blocks in shards:
        heights = jax.random.uniform(jax.random.fold_in(jax.random.fold_in(stream_key, 6), dim), (blocks,), jnp.float32, low / len(shards), high / len(shards))
        loudness = loudness * jnp.repeat(jnp.exp(heights), extent[dim] // blocks).reshape((-1,) + (1,) * (len(extent) - 1 - dim))
    return loudness


def profile(number_of, total, bound, skew):
    portions = [(1 << 20) // math.isqrt(standing ** skew) + 1 for standing in range(2, number_of + 1)]
    rest, holding = total - bound - (number_of - 1), [1] * (number_of - 1)
    while rest > 0:
        free = [i for i in range(number_of - 1) if holding[i] < bound]
        pool, budget = sum([portions[i] for i in free]), rest
        for i in free:
            more = min(bound - holding[i], max(1, budget * portions[i] // pool), rest)
            holding[i] = holding[i] + more
            rest = rest - more
    return np.array([bound] + holding)


def uneven_parts(own_key, number_of, total, reach, slope):
    if number_of == 2:
        one = jax.random.randint(own_key, (), max(1, total - reach), min(reach, total - 1) + 1)
        return jnp.stack([one, total - one])
    tallies = jnp.asarray(profile(number_of, total, reach, slope), jnp.int32)
    twos = (number_of - 1) // 2
    donor, sink = tallies[1:1 + 2 * twos:2], tallies[2:2 + 2 * twos:2]
    slack = jnp.minimum(donor - 1, reach - sink)
    moved = jax.random.randint(jax.random.fold_in(own_key, 1), (twos,), 0, 1 << 20) % (slack + 1)
    tallies = tallies.at[1:1 + 2 * twos:2].set(donor - moved).at[2:2 + 2 * twos:2].set(sink + moved)
    return tallies[jax.random.permutation(jax.random.fold_in(own_key, 2), number_of)]


def normal_values(own_key, shape, width, most, cuts=(), held_as=jnp.bfloat16):
    entries = width * jax.random.normal(own_key, shape, jnp.float32)
    if cuts:
        entries = entries * block_levels(own_key, shape, cuts, -0.22, 0.18)
    return jnp.clip(entries, -most, most).astype(held_as)


def setup_inputs(seed: int = 0) -> dict:
    key_list = jax.random.split(jax.random.key(seed), 13)
    return {
        "tokens_in": normal_values(key_list[0], (TOKENS, D), 1.0, 6.0, ((0, 32),)),
        "cotangent": normal_values(key_list[1], (TOKENS, D), 1.0, 6.0, ((0, 32),)),
        "deal_order": draw_deal_order(jax.random.fold_in(key_list[12], 71), 0),
        "lengths": uneven_parts(key_list[3], NSEQ, TOKENS, MAXLEN, 2).astype(jnp.int32),
        "decay_rates": jnp.clip(jnp.exp(jax.random.uniform(key_list[4], (HEADS,), jnp.float32, math.log(0.00012207031), math.log(0.03))), 0.00012207031, 0.03),
        "w_query": normal_values(key_list[5], (D, D), D ** -0.5, 0.1875, ((0, 4),)),
        "w_key": normal_values(key_list[6], (D, D), D ** -0.5, 0.1875, ((0, 4),)),
        "w_value": normal_values(key_list[7], (D, D), D ** -0.5, 0.1875, ((0, 4),)),
        "w_ugate": normal_values(key_list[8], (D, D), D ** -0.5, 0.1875, ((0, 4),)),
        "w_out": normal_values(key_list[9], (D, D), D ** -0.5, 0.1875, ((0, 4),)),
        "w_ffin": normal_values(key_list[10], (D, 2 * FF), D ** -0.5, 0.1875, ((0, 4),)),
        "w_ffdown": normal_values(key_list[11], (FF, D), FF ** -0.5, 0.109375, ((0, 4),)),
    }


@jax.custom_vjp
def low(v):
    return lax.optimization_barrier(v.astype(jnp.bfloat16)).astype(jnp.float32)

@jax.custom_vjp
def low_back(v):
    return v

def low_keep(v):
    return (low(v), None)

def low_pass(kept, grad):
    return (grad,)

def back_keep(v):
    return (v, None)

def back_low(kept, grad):
    return (low(grad),)
low.defvjp(low_keep, low_pass)
low_back.defvjp(back_keep, back_low)
epsilon = 1e-06
highest = lax.Precision.HIGHEST

def simple_norm(values):
    return values * lax.rsqrt(lax.optimization_barrier(jnp.mean(values * values, axis=-1, keepdims=True)) + epsilon)

def matmul_high(left, right):
    return jnp.dot(left, right, precision=highest, preferred_element_type=jnp.float32)

def block_masks(rates, seg_block, seg_prev):
    block_len = seg_block.shape[0]
    indices = jnp.arange(block_len).astype(jnp.float32)
    distance = indices[:, None] - indices[None, :]
    allowed = (seg_block[:, None] == seg_block[None, :]) & (distance >= 0)
    decay_mask = jnp.where(allowed[None], jnp.exp(-rates[:, None, None] * jnp.maximum(distance, 0.0)[None]), 0.0)
    carried = (seg_block == seg_prev).astype(jnp.float32)
    query_scale = jnp.exp(-(indices + 1.0)[:, None] * rates[None, :]) * carried[:, None]
    last_seg = seg_block[-1]
    passing = (last_seg == seg_prev).astype(jnp.float32) * jnp.exp(-rates * block_len)
    key_scale = jnp.exp(-(block_len - 1.0 - indices)[:, None] * rates[None, :]) * (seg_block == last_seg).astype(jnp.float32)[:, None]
    return (decay_mask, query_scale, passing, key_scale)

def attend_block(rates, kv_state, block_item):
    queries, keys_rows, values, seg_block, seg_prev = block_item
    decay_mask, query_scale, passing, key_scale = block_masks(rates, seg_block, seg_prev)
    raw_scores = low_back(jnp.einsum('ihe,jhe->hij', queries, keys_rows, precision=highest))
    mixing = low(raw_scores * decay_mask)
    mixed = jnp.einsum('hij,jhe->ihe', mixing, values, precision=highest)
    mixed = mixed + jnp.einsum('ihe,hef->ihf', queries * query_scale[:, :, None], kv_state, precision=highest)
    new_state = passing[:, None, None] * kv_state + jnp.einsum('jhe,jhf->hef', keys_rows * key_scale[:, :, None], values, precision=highest)
    return (new_state, mixed)

def span_step(weight_list, rates, kv_state, span_item):
    w_query, w_key, w_value, w_ugate, w_out, w_ffin, w_ffdown = weight_list
    rows_in, seg_rows, seg_first = span_item
    span_len = rows_in.shape[0]
    normed = low(simple_norm(rows_in))
    pre_query = low_back(matmul_high(normed, w_query))
    pre_key = low_back(matmul_high(normed, w_key))
    pre_value = low_back(matmul_high(normed, w_value))
    pre_ugate = low_back(matmul_high(normed, w_ugate))
    block_shape = (span_len // BLOCK, BLOCK, HEADS, HEAD)
    queries = low(jax.nn.silu(pre_query)).reshape(block_shape)
    keys_rows = low(jax.nn.silu(pre_key)).reshape(block_shape)
    values = low(pre_value).reshape(block_shape)
    prev_rows = jnp.concatenate([seg_first[None], seg_rows[:-1]])
    seg_blocks = seg_rows.reshape(-1, BLOCK)
    prev_blocks = prev_rows.reshape(-1, BLOCK)[:, 0]
    kv_state, mixed = lax.scan(jax.checkpoint(partial(attend_block, rates)), kv_state, (queries, keys_rows, values, seg_blocks, prev_blocks))
    mixed = low_back(mixed.reshape(span_len, HEADS, HEAD))
    gated = low(pre_ugate * simple_norm(mixed).reshape(span_len, D))
    attended = low_back(matmul_high(gated, w_out))
    hidden_state = rows_in + attended
    normed_two = low(simple_norm(hidden_state))
    joined = low_back(matmul_high(normed_two, w_ffin))
    product = low(joined[:, :FF] * joined[:, FF:])
    mlp_out = low_back(matmul_high(product, w_ffdown))
    return (kv_state, hidden_state + mlp_out)

def reference(tokens_in, cotangent, deal_order, lengths, decay_rates, w_query, w_key, w_value, w_ugate, w_out, w_ffin, w_ffdown):
    seq_ends = jnp.cumsum(lengths).astype(jnp.int32)
    positions = jnp.arange(TOKENS).astype(jnp.int32)
    seg_all = lax.optimization_barrier(jnp.sum((positions[:, None] >= seq_ends[None, :]).astype(jnp.int32), axis=1)).astype(jnp.int32)
    seg_prev_all = jnp.concatenate([jnp.full((1,), -1, jnp.int32), seg_all[:-1]])
    span_rows = math.gcd(TOKENS, 4096)
    span_count = TOKENS // span_rows
    seg_spans = seg_all.reshape(span_count, span_rows)
    prev_spans = seg_prev_all.reshape(span_count, span_rows)[:, 0]
    packed = tokens_in.astype(jnp.float32)[deal_order]
    grad_packed = cotangent.astype(jnp.float32)[deal_order]
    weights_f = tuple((weight.astype(jnp.float32) for weight in (w_query, w_key, w_value, w_ugate, w_out, w_ffin, w_ffdown)))

    def layer_forward(rows_all, wq_f, wk_f, wv_f, wu_f, wo_f, wf_f, wd_f):
        step_fn = jax.checkpoint(partial(span_step, (wq_f, wk_f, wv_f, wu_f, wo_f, wf_f, wd_f), decay_rates))
        zero_state = jnp.zeros((HEADS, HEAD, HEAD), jnp.float32)
        unused, result = lax.scan(step_fn, zero_state, (rows_all.reshape(span_count, span_rows, D), seg_spans, prev_spans))
        return result.reshape(TOKENS, D)
    result, pullback = jax.vjp(layer_forward, packed, weights_f[0], weights_f[1], weights_f[2], weights_f[3], weights_f[4], weights_f[5], weights_f[6])
    gradients = pullback(grad_packed)
    restore = jnp.argsort(deal_order)
    return (result[restore].astype(jnp.bfloat16), gradients[0][restore].astype(jnp.bfloat16), gradients[1], gradients[2], gradients[3], gradients[4], gradients[5], gradients[6], gradients[7])
```

```python
import jax
import jax.numpy as jnp
from jax import lax
from jax.sharding import Mesh, PartitionSpec as P

HEAD = 128
BLOCK = 256
TEAM = 4
EPS = 1e-06
BF = jnp.bfloat16
F32 = jnp.float32
ALL = ("zh", "zl", "core", "shard")


def send(value, axis, mask):
    size = lax.axis_size(axis)
    return lax.ppermute(value, axis, [(i, i ^ mask) for i in range(size)])


def dot(a, b, dims=((1,), (0,))):
    return lax.dot_general(a, b, (dims, ((), ())), preferred_element_type=F32)


def norm_scale(values):
    return lax.rsqrt(jnp.mean(values * values, axis=-1, keepdims=True) + EPS)


def norm_back(values, grad):
    scale = norm_scale(values)
    return scale * grad - values * (scale**3) * jnp.mean(values * grad, axis=-1, keepdims=True)


def in_order(pieces, index):
    pieces = list(pieces)
    bit = 1
    while bit < len(pieces):
        flip = (index & bit) != 0
        pieces = [jnp.where(flip, pieces[j ^ bit], pieces[j]) for j in range(len(pieces))]
        bit *= 2
    return pieces


def gather_shard(part):
    size = lax.axis_size("shard")
    if size != 4:
        every = lax.all_gather(part, "shard", axis=0)
        return [every[j] for j in range(size)]
    half = part.shape[0] // 2
    by_x, by_y = send(part, "shard", 1), send(part, "shard", 2)
    far = jnp.concatenate([send(by_x[:half], "shard", 2), send(by_y[half:], "shard", 1)], 0)
    return in_order([part, by_x, by_y, far], lax.axis_index("shard"))


def scatter_shard(parts):
    size = lax.axis_size("shard")
    if size != 4:
        return lax.psum_scatter(jnp.stack(parts), "shard", scatter_dimension=0, tiled=False)
    rel = in_order(parts, lax.axis_index("shard"))
    total = rel[0].astype(F32)
    for j in (1, 2, 3):
        total = total + send(rel[j].astype(BF), "shard", j).astype(F32)
    return total


def sum_zh(part):
    size = lax.axis_size("zh")
    part = part.astype(BF)
    if size != 2:
        return lax.psum(part.astype(F32), "zh").astype(BF)
    return (part.astype(F32) + send(part, "zh", 1).astype(F32)).astype(BF)


def team_gather(own):
    pair = send(own, "zl", 1)
    return [own, send(own, "core", 1), pair, send(pair, "core", 1)]


def team_reduce(parts):
    low = [p.astype(BF) for p in parts]
    here = parts[0] + send(low[1], "core", 1).astype(F32)
    there = parts[2] + send(low[3], "core", 1).astype(F32)
    return here + send(there.astype(BF), "zl", 1).astype(F32)


def place_mix(state, weights):
    groups = lax.axis_size("zh") * lax.axis_size("shard")
    mine = lax.axis_index("zh") * lax.axis_size("shard") + lax.axis_index("shard")
    low = state.astype(BF)
    if groups != 8:
        every = lax.all_gather(low, ("zh", "shard"), axis=0).astype(F32)
        return jnp.sum(every * weights[:, :, None, None], axis=0)
    total = jnp.zeros_like(state)
    for j in range(1, groups):
        got = lax.ppermute(low, ("zh", "shard"), [(i, i ^ j) for i in range(groups)])
        factor = lax.dynamic_index_in_dim(weights, mine ^ j, 0, keepdims=False)
        total = total + factor[:, None, None] * got.astype(F32)
    return total


def after(value, *others):
    return lax.optimization_barrier((value, *others))[0]


def body(tokens_in, cotangent, deal_order, lengths, decay_rates, w_query, w_key, w_value, w_ugate, w_out, w_ffin, w_ffdown):
    rows, width = tokens_in.shape
    n_zh, n_shard = lax.axis_size("zh"), lax.axis_size("shard")
    groups = n_zh * n_shard
    devices = groups * TEAM
    zh, zl, core, shard = (lax.axis_index(a) for a in ALL)
    me = zl * 2 + core
    group = zh * n_shard + shard
    device = (zh * TEAM + me) * n_shard + shard
    heads = width // HEAD // TEAM
    cols = heads * HEAD
    depth = w_query.shape[0]
    ff = w_ffin.shape[1] // 2
    ff_shard = w_ffdown.shape[0]
    ff_own = ff_shard // TEAM
    per_peer = rows // devices
    span = rows * TEAM

    by_device = deal_order.reshape(n_zh, n_shard, TEAM, rows).transpose(0, 2, 1, 3).reshape(-1)
    row_ids = jnp.arange(rows, dtype=jnp.int32)
    key = jnp.sum(
        jnp.where(
            by_device[:, None] == device * rows + row_ids[None, :],
            jnp.arange(by_device.shape[0], dtype=jnp.int32)[:, None],
            0,
        ),
        axis=0,
    )
    rank = jnp.sum((key[:, None] < key[None, :]).astype(jnp.int32), axis=0)
    leave = (row_ids[:, None] == rank[None, :]).astype(BF)
    sent_x = dot(leave, tokens_in).astype(BF)
    sent_g = dot(leave, cotangent).astype(BF)
    got_x = lax.all_to_all(sent_x, ALL, split_axis=0, concat_axis=0, tiled=True)
    own_block = lax.dynamic_slice_in_dim(by_device, device * rows, rows)
    source = own_block // rows
    earlier = row_ids[None, :] < row_ids[:, None]
    own_rank = jnp.sum(((source[:, None] == source[None, :]) & earlier).astype(jnp.int32), axis=1)
    slot = source * per_peer + own_rank
    enter = (slot[:, None] == row_ids[None, :]).astype(BF)
    x_own = dot(enter, got_x).astype(BF)
    got_g = lax.all_to_all(after(sent_g, got_x), ALL, split_axis=0, concat_axis=0, tiled=True)
    g_own = dot(enter, got_g).astype(BF)

    def quarter(w):
        return lax.dynamic_slice_in_dim(w, me * cols, cols, axis=1)

    qkvu_part = jnp.concatenate([quarter(w) for w in (w_query, w_key, w_value, w_ugate)], 1)
    w_qkvu = jnp.concatenate(gather_shard(qkvu_part), 0)
    out_all = jnp.concatenate(gather_shard(after(w_out, w_qkvu)), 0)
    w_o = lax.dynamic_slice_in_dim(out_all, me * cols, cols)
    fin = w_ffin.reshape(depth, 2, n_shard, TEAM, ff_own)
    fin = lax.dynamic_index_in_dim(fin, me, 3, keepdims=False)
    fin = fin.transpose(1, 0, 2, 3).reshape(2 * depth, n_shard * ff_own)
    fin_parts = gather_shard(after(fin, out_all))
    w_gate = jnp.concatenate([p[:depth] for p in fin_parts], 0)
    w_up = jnp.concatenate([p[depth:] for p in fin_parts], 0)
    fdown = lax.dynamic_slice_in_dim(w_ffdown, me * ff_own, ff_own)
    w_down = jnp.concatenate(gather_shard(after(fdown, w_up)), 0)

    ends = jnp.sum(jnp.where(jnp.arange(8)[None, :] <= jnp.arange(8)[:, None], lengths[None, :], 0), axis=1)
    all_last = jnp.arange(1, groups + 1) * span - 1
    last_seg = jnp.sum((all_last[:, None] >= ends[None, :]).astype(jnp.int32), axis=1)
    before_seg = jnp.concatenate([jnp.full((1,), -1, jnp.int32), last_seg[:-1]])
    positions = group * span + jnp.arange(span)
    seg = jnp.sum((positions[:, None] >= ends[None, :]).astype(jnp.int32), axis=1)
    seg_before = before_seg[group]
    blocks = span // BLOCK
    seg_b = seg.reshape(blocks, BLOCK)
    prev_b = jnp.concatenate([seg_before[None], seg_b[:-1, -1]])
    rates = lax.dynamic_slice_in_dim(decay_rates, me * heads, heads)
    idx = jnp.arange(BLOCK).astype(F32)
    dist = idx[:, None] - idx[None, :]
    decay = jnp.where(dist >= 0, jnp.exp(-rates[:, None, None] * jnp.maximum(dist, 0.0)), 0.0)
    same = (seg_b[:, :, None] == seg_b[:, None, :]).astype(F32)
    mask = same[:, None] * decay[None]
    carry = (seg_b == prev_b[:, None]).astype(F32)
    q_scale = jnp.exp(-(idx + 1.0)[None, :, None] * rates) * carry[:, :, None]
    k_scale = jnp.exp(-(BLOCK - 1.0 - idx)[None, :, None] * rates) * (seg_b == seg_b[:, -1:]).astype(F32)[:, :, None]
    passing = (seg_b[:, -1] == prev_b).astype(F32)[:, None] * jnp.exp(-rates * BLOCK)[None]
    ids = jnp.arange(groups)
    gap = jnp.maximum(jnp.abs(ids - group) - 1, 0).astype(F32) * span
    into = (ids < group) & (last_seg == seg_before)
    outof = (ids > group) & (before_seg == last_seg[group])
    fade = jnp.exp(-gap[:, None] * rates[None, :])
    w_into = jnp.where(into[:, None], fade, 0.0)
    w_outof = jnp.where(outof[:, None], fade, 0.0)

    x = in_order(team_gather(x_own), me)
    x_all = jnp.concatenate(x, 0)
    xf = x_all.astype(F32)
    normed = (xf * norm_scale(xf)).astype(BF)
    pre = dot(normed, w_qkvu)
    pre_q, pre_k, pre_v, pre_u = (pre[:, i * cols : (i + 1) * cols] for i in range(4))
    shape = (blocks, BLOCK, heads, HEAD)
    q = jax.nn.silu(pre_q).astype(BF).reshape(shape)
    k = jax.nn.silu(pre_k).astype(BF).reshape(shape)
    v = pre_v.astype(BF).reshape(shape)

    def ein(text, a, b):
        return jnp.einsum(text, a, b, preferred_element_type=F32)

    ks = (k.astype(F32) * k_scale[..., None]).astype(BF)
    qs = (q.astype(F32) * q_scale[..., None]).astype(BF)
    kv = ein("bjhe,bjhf->bhef", ks, v)
    state = jnp.zeros((heads, HEAD, HEAD), F32)
    for b in range(blocks):
        state = passing[b][:, None, None] * state + kv[b]
    state_in = place_mix(state, w_into)
    scores = ein("bihe,bjhe->bhij", q, k)
    mixing = (scores * mask).astype(BF)
    mixed = ein("bhij,bjhf->bihf", mixing, v)
    states = []
    state = state_in
    for b in range(blocks):
        states.append(state)
        state = passing[b][:, None, None] * state + kv[b]
    states = jnp.stack(states).astype(BF)
    mixed = mixed + ein("bihe,bhef->bihf", qs, states)
    m_norm = (mixed * norm_scale(mixed)).reshape(span, cols)
    gated = (pre_u * m_norm).astype(BF)
    part = dot(gated, w_o).reshape(TEAM, rows, width)
    att = team_reduce(in_order([part[j] for j in range(TEAM)], me))
    att = jnp.concatenate(in_order(team_gather(att.astype(BF)), me), 0)
    hidden = xf + att.astype(F32)

    g_all = jnp.concatenate(in_order(team_gather(g_own), me), 0)
    n2 = (hidden * norm_scale(hidden)).astype(BF)
    gate, up = dot(n2, w_gate), dot(n2, w_up)
    product = (gate * up).astype(BF)
    res = dot(product, w_down).reshape(TEAM, rows, width)
    g_product = dot(g_all, w_down, ((1,), (1,)))
    g_gate, g_up = (g_product * up).astype(BF), (g_product * gate).astype(BF)
    gn2 = dot(g_gate, w_gate, ((1,), (1,))) + dot(g_up, w_up, ((1,), (1,)))
    gn2 = gn2.reshape(TEAM, rows, width)
    gn2 = team_reduce(in_order([gn2[j] for j in range(TEAM)], me))
    gn2 = jnp.concatenate(in_order(team_gather(gn2.astype(BF)), me), 0)
    g_hidden = g_all.astype(F32) + norm_back(hidden, gn2.astype(F32))
    ga = g_hidden.astype(BF)

    res = team_reduce(in_order([res[j] for j in range(TEAM)], me))
    my_rows = lambda a: lax.dynamic_slice_in_dim(a, me * rows, rows)
    result = (my_rows(hidden) + res).astype(BF)

    g_gated = dot(ga, w_o, ((1,), (1,)))
    g_pre_u = (g_gated * m_norm).astype(BF)
    gm = norm_back(mixed, (g_gated * pre_u).reshape(shape)).astype(BF)
    qg = ein("bihe,bihf->bhef", qs, gm)
    gs = jnp.zeros((heads, HEAD, HEAD), F32)
    for b in reversed(range(blocks)):
        gs = passing[b][:, None, None] * gs + qg[b]
    gs = place_mix(gs, w_outof)
    g_states = [None] * blocks
    for b in reversed(range(blocks)):
        g_states[b] = gs
        gs = passing[b][:, None, None] * gs + qg[b]
    g_states = jnp.stack(g_states).astype(BF)
    g_mixing = ein("bihf,bjhf->bhij", gm, v)
    g_scores = (g_mixing * mask).astype(BF)
    g_q = ein("bhij,bjhe->bihe", g_scores, k) + q_scale[..., None] * ein("bihf,bhef->bihe", gm, states)
    g_k = ein("bhij,bihe->bjhe", g_scores, q) + k_scale[..., None] * ein("bhef,bjhf->bjhe", g_states, v)
    g_v = ein("bhij,bihf->bjhf", mixing, gm) + ein("bjhe,bhef->bjhf", ks, g_states)

    def silu_back(pre_rows, grad):
        sig = jax.nn.sigmoid(pre_rows)
        return (grad * (sig * (1.0 + pre_rows * (1.0 - sig)))).astype(BF)

    g_pre = jnp.concatenate(
        [
            silu_back(pre_q, g_q.reshape(span, cols)),
            silu_back(pre_k, g_k.reshape(span, cols)),
            g_v.reshape(span, cols).astype(BF),
            g_pre_u,
        ],
        1,
    )
    gn = dot(g_pre, w_qkvu, ((1,), (1,))).reshape(TEAM, rows, width)
    gn = team_reduce(in_order([gn[j] for j in range(TEAM)], me))
    grad_x = (my_rows(g_hidden) + norm_back(x_own.astype(F32), gn)).astype(BF)

    def give_back(rows_own):
        ordered = dot(enter, rows_own, ((0,), (0,))).astype(BF)
        back = lax.all_to_all(ordered, ALL, split_axis=0, concat_axis=0, tiled=True)
        return dot(leave, back, ((0,), (0,))).astype(BF)

    output, input_grad = give_back(result), give_back(grad_x)

    def by_place(grad):
        return list(grad.astype(BF).reshape(n_shard, -1, grad.shape[-1]))

    d_down = dot(product, g_all, ((0,), (0,)))
    d_gate, d_up = dot(n2, g_gate, ((0,), (0,))), dot(n2, g_up, ((0,), (0,)))
    d_out = dot(gated, ga, ((0,), (0,)))
    d_qkvu = dot(normed, g_pre, ((0,), (0,)))

    def collect(parts):
        return in_order(team_gather(sum_zh(scatter_shard(parts))), me)

    down = collect(by_place(d_down))
    grad_down = jnp.concatenate(down, 0).astype(F32)
    fin_grad = [jnp.concatenate([a, b], 0) for a, b in zip(by_place(d_gate), by_place(d_up))]
    fin_grad = jnp.stack(collect(fin_grad), 0).reshape(TEAM, 2, depth, n_shard, ff_own)
    grad_fin = fin_grad.transpose(2, 1, 3, 0, 4).reshape(depth, 2 * ff).astype(F32)
    out_cols = width // n_shard
    d_out_cols = [d_out[:, j * out_cols : (j + 1) * out_cols].astype(BF) for j in range(n_shard)]
    d_out_rows = jnp.concatenate(collect(d_out_cols), 0)
    d_out_rows = lax.all_to_all(
        d_out_rows.reshape(n_shard, depth, out_cols), "shard", split_axis=0, concat_axis=0, tiled=True
    )
    grad_out = d_out_rows.transpose(1, 0, 2).reshape(depth, width).astype(F32)
    qkvu = collect(by_place(d_qkvu))
    grads = [
        jnp.concatenate([p[:, i * cols : (i + 1) * cols] for p in qkvu], 1).astype(F32) for i in range(4)
    ]
    return (output, input_grad, *grads, grad_out, grad_fin, grad_down)


def solution(mesh):
    rep, shard = mesh.shape["rep"], mesh.shape["shard"]
    team = Mesh(mesh.devices.reshape(rep // TEAM, 2, 2, shard), ALL)
    token, weight = P(ALL, None), P("shard", None)
    return jax.shard_map(
        body,
        mesh=team,
        in_specs=(token, token, P(), P(), P(), *([weight] * 7)),
        out_specs=(token, token, *([weight] * 7)),
        check_vma=False,
    )
```

```python
import functools

import jax
import jax.numpy as jnp
from jax import lax
from jax.experimental import pallas as pl
from jax.experimental.pallas import tpu as pltpu
from jax.sharding import Mesh, PartitionSpec as P

HEAD = 128
BLOCK = 256
TEAM = 4
EPS = 1e-06
BF = jnp.bfloat16
F32 = jnp.float32
ALL = ("zh", "zl", "core", "shard")


def send(value, axis, mask):
    size = lax.axis_size(axis)
    return lax.ppermute(value, axis, [(i, i ^ mask) for i in range(size)])


def dot(a, b, dims=((1,), (0,))):
    return lax.dot_general(a, b, (dims, ((), ())), preferred_element_type=F32)


def norm_scale(values):
    return lax.rsqrt(jnp.mean(values * values, axis=-1, keepdims=True) + EPS)


def norm_back(values, grad):
    scale = norm_scale(values)
    return scale * grad - values * (scale**3) * jnp.mean(values * grad, axis=-1, keepdims=True)


def in_order(pieces, index):
    pieces = list(pieces)
    bit = 1
    while bit < len(pieces):
        flip = (index & bit) != 0
        pieces = [jnp.where(flip, pieces[j ^ bit], pieces[j]) for j in range(len(pieces))]
        bit *= 2
    return pieces


def gather_shard(part):
    size = lax.axis_size("shard")
    if size != 4:
        every = lax.all_gather(part, "shard", axis=0)
        return [every[j] for j in range(size)]
    half = part.shape[0] // 2
    by_x, by_y = send(part, "shard", 1), send(part, "shard", 2)
    far = jnp.concatenate([send(by_x[:half], "shard", 2), send(by_y[half:], "shard", 1)], 0)
    return in_order([part, by_x, by_y, far], lax.axis_index("shard"))


def scatter_shard(parts):
    size = lax.axis_size("shard")
    if size != 4:
        return lax.psum_scatter(jnp.stack(parts), "shard", scatter_dimension=0, tiled=False)
    rel = in_order(parts, lax.axis_index("shard"))
    total = rel[0].astype(F32)
    for j in (1, 2, 3):
        total = total + send(rel[j].astype(BF), "shard", j).astype(F32)
    return total


def sum_zh(part):
    size = lax.axis_size("zh")
    part = part.astype(BF)
    if size != 2:
        return lax.psum(part.astype(F32), "zh").astype(BF)
    return (part.astype(F32) + send(part, "zh", 1).astype(F32)).astype(BF)


def team_gather(own):
    pair = send(own, "zl", 1)
    return [own, send(own, "core", 1), pair, send(pair, "core", 1)]


def team_reduce(parts):
    low = [p.astype(BF) for p in parts]
    here = parts[0] + send(low[1], "core", 1).astype(F32)
    there = parts[2] + send(low[3], "core", 1).astype(F32)
    return here + send(there.astype(BF), "zl", 1).astype(F32)


def place_mix(state, weights):
    groups = lax.axis_size("zh") * lax.axis_size("shard")
    mine = lax.axis_index("zh") * lax.axis_size("shard") + lax.axis_index("shard")
    low = state.astype(BF)
    if groups != 8:
        every = lax.all_gather(low, ("zh", "shard"), axis=0).astype(F32)
        return jnp.sum(every * weights[:, :, None, None], axis=0)
    total = jnp.zeros_like(state)
    for j in range(1, groups):
        got = lax.ppermute(low, ("zh", "shard"), [(i, i ^ j) for i in range(groups)])
        factor = lax.dynamic_index_in_dim(weights, mine ^ j, 0, keepdims=False)
        total = total + factor[:, None, None] * got.astype(F32)
    return total


def after(value, *others):
    return lax.optimization_barrier((value, *others))[0]


def general_body(tokens_in, cotangent, deal_order, lengths, decay_rates, w_query, w_key, w_value, w_ugate, w_out, w_ffin, w_ffdown):
    rows, width = tokens_in.shape
    n_zh, n_shard = lax.axis_size("zh"), lax.axis_size("shard")
    groups = n_zh * n_shard
    devices = groups * TEAM
    zh, zl, core, shard = (lax.axis_index(a) for a in ALL)
    me = zl * 2 + core
    group = zh * n_shard + shard
    device = (zh * TEAM + me) * n_shard + shard
    heads = width // HEAD // TEAM
    cols = heads * HEAD
    depth = w_query.shape[0]
    ff = w_ffin.shape[1] // 2
    ff_shard = w_ffdown.shape[0]
    ff_own = ff_shard // TEAM
    per_peer = rows // devices
    span = rows * TEAM

    by_device = deal_order.reshape(n_zh, n_shard, TEAM, rows).transpose(0, 2, 1, 3).reshape(-1)
    row_ids = jnp.arange(rows, dtype=jnp.int32)
    key = jnp.sum(
        jnp.where(
            by_device[:, None] == device * rows + row_ids[None, :],
            jnp.arange(by_device.shape[0], dtype=jnp.int32)[:, None],
            0,
        ),
        axis=0,
    )
    rank = jnp.sum((key[:, None] < key[None, :]).astype(jnp.int32), axis=0)
    leave = (row_ids[:, None] == rank[None, :]).astype(BF)
    sent_x = dot(leave, tokens_in).astype(BF)
    sent_g = dot(leave, cotangent).astype(BF)
    got_x = lax.all_to_all(sent_x, ALL, split_axis=0, concat_axis=0, tiled=True)
    own_block = lax.dynamic_slice_in_dim(by_device, device * rows, rows)
    source = own_block // rows
    earlier = row_ids[None, :] < row_ids[:, None]
    own_rank = jnp.sum(((source[:, None] == source[None, :]) & earlier).astype(jnp.int32), axis=1)
    slot = source * per_peer + own_rank
    enter = (slot[:, None] == row_ids[None, :]).astype(BF)
    x_own = dot(enter, got_x).astype(BF)
    got_g = lax.all_to_all(after(sent_g, got_x), ALL, split_axis=0, concat_axis=0, tiled=True)
    g_own = dot(enter, got_g).astype(BF)

    def quarter(w):
        return lax.dynamic_slice_in_dim(w, me * cols, cols, axis=1)

    qkvu_part = jnp.concatenate([quarter(w) for w in (w_query, w_key, w_value, w_ugate)], 1)
    w_qkvu = jnp.concatenate(gather_shard(qkvu_part), 0)
    out_all = jnp.concatenate(gather_shard(after(w_out, w_qkvu)), 0)
    w_o = lax.dynamic_slice_in_dim(out_all, me * cols, cols)
    fin = w_ffin.reshape(depth, 2, n_shard, TEAM, ff_own)
    fin = lax.dynamic_index_in_dim(fin, me, 3, keepdims=False)
    fin = fin.transpose(1, 0, 2, 3).reshape(2 * depth, n_shard * ff_own)
    fin_parts = gather_shard(after(fin, out_all))
    w_gate = jnp.concatenate([p[:depth] for p in fin_parts], 0)
    w_up = jnp.concatenate([p[depth:] for p in fin_parts], 0)
    fdown = lax.dynamic_slice_in_dim(w_ffdown, me * ff_own, ff_own)
    w_down = jnp.concatenate(gather_shard(after(fdown, w_up)), 0)

    ends = jnp.sum(jnp.where(jnp.arange(8)[None, :] <= jnp.arange(8)[:, None], lengths[None, :], 0), axis=1)
    all_last = jnp.arange(1, groups + 1) * span - 1
    last_seg = jnp.sum((all_last[:, None] >= ends[None, :]).astype(jnp.int32), axis=1)
    before_seg = jnp.concatenate([jnp.full((1,), -1, jnp.int32), last_seg[:-1]])
    positions = group * span + jnp.arange(span)
    seg = jnp.sum((positions[:, None] >= ends[None, :]).astype(jnp.int32), axis=1)
    seg_before = before_seg[group]
    blocks = span // BLOCK
    seg_b = seg.reshape(blocks, BLOCK)
    prev_b = jnp.concatenate([seg_before[None], seg_b[:-1, -1]])
    rates = lax.dynamic_slice_in_dim(decay_rates, me * heads, heads)
    idx = jnp.arange(BLOCK).astype(F32)
    dist = idx[:, None] - idx[None, :]
    decay = jnp.where(dist >= 0, jnp.exp(-rates[:, None, None] * jnp.maximum(dist, 0.0)), 0.0)
    same = (seg_b[:, :, None] == seg_b[:, None, :]).astype(F32)
    mask = same[:, None] * decay[None]
    carry = (seg_b == prev_b[:, None]).astype(F32)
    q_scale = jnp.exp(-(idx + 1.0)[None, :, None] * rates) * carry[:, :, None]
    k_scale = jnp.exp(-(BLOCK - 1.0 - idx)[None, :, None] * rates) * (seg_b == seg_b[:, -1:]).astype(F32)[:, :, None]
    passing = (seg_b[:, -1] == prev_b).astype(F32)[:, None] * jnp.exp(-rates * BLOCK)[None]
    ids = jnp.arange(groups)
    gap = jnp.maximum(jnp.abs(ids - group) - 1, 0).astype(F32) * span
    into = (ids < group) & (last_seg == seg_before)
    outof = (ids > group) & (before_seg == last_seg[group])
    fade = jnp.exp(-gap[:, None] * rates[None, :])
    w_into = jnp.where(into[:, None], fade, 0.0)
    w_outof = jnp.where(outof[:, None], fade, 0.0)

    x = in_order(team_gather(x_own), me)
    x_all = jnp.concatenate(x, 0)
    xf = x_all.astype(F32)
    normed = (xf * norm_scale(xf)).astype(BF)
    pre = dot(normed, w_qkvu)
    pre_q, pre_k, pre_v, pre_u = (pre[:, i * cols : (i + 1) * cols] for i in range(4))
    shape = (blocks, BLOCK, heads, HEAD)
    q = jax.nn.silu(pre_q).astype(BF).reshape(shape)
    k = jax.nn.silu(pre_k).astype(BF).reshape(shape)
    v = pre_v.astype(BF).reshape(shape)

    def ein(text, a, b):
        return jnp.einsum(text, a, b, preferred_element_type=F32)

    ks = (k.astype(F32) * k_scale[..., None]).astype(BF)
    qs = (q.astype(F32) * q_scale[..., None]).astype(BF)
    kv = ein("bjhe,bjhf->bhef", ks, v)
    state = jnp.zeros((heads, HEAD, HEAD), F32)
    for b in range(blocks):
        state = passing[b][:, None, None] * state + kv[b]
    state_in = place_mix(state, w_into)
    scores = ein("bihe,bjhe->bhij", q, k)
    mixing = (scores * mask).astype(BF)
    mixed = ein("bhij,bjhf->bihf", mixing, v)
    states = []
    state = state_in
    for b in range(blocks):
        states.append(state)
        state = passing[b][:, None, None] * state + kv[b]
    states = jnp.stack(states).astype(BF)
    mixed = mixed + ein("bihe,bhef->bihf", qs, states)
    m_norm = (mixed * norm_scale(mixed)).reshape(span, cols)
    gated = (pre_u * m_norm).astype(BF)
    part = dot(gated, w_o).reshape(TEAM, rows, width)
    att = team_reduce(in_order([part[j] for j in range(TEAM)], me))
    att = jnp.concatenate(in_order(team_gather(att.astype(BF)), me), 0)
    hidden = xf + att.astype(F32)

    g_all = jnp.concatenate(in_order(team_gather(g_own), me), 0)
    n2 = (hidden * norm_scale(hidden)).astype(BF)
    gate, up = dot(n2, w_gate), dot(n2, w_up)
    product = (gate * up).astype(BF)
    res = dot(product, w_down).reshape(TEAM, rows, width)
    g_product = dot(g_all, w_down, ((1,), (1,)))
    g_gate, g_up = (g_product * up).astype(BF), (g_product * gate).astype(BF)
    gn2 = dot(g_gate, w_gate, ((1,), (1,))) + dot(g_up, w_up, ((1,), (1,)))
    gn2 = gn2.reshape(TEAM, rows, width)
    gn2 = team_reduce(in_order([gn2[j] for j in range(TEAM)], me))
    gn2 = jnp.concatenate(in_order(team_gather(gn2.astype(BF)), me), 0)
    g_hidden = g_all.astype(F32) + norm_back(hidden, gn2.astype(F32))
    ga = g_hidden.astype(BF)

    res = team_reduce(in_order([res[j] for j in range(TEAM)], me))
    my_rows = lambda a: lax.dynamic_slice_in_dim(a, me * rows, rows)
    result = (my_rows(hidden) + res).astype(BF)

    g_gated = dot(ga, w_o, ((1,), (1,)))
    g_pre_u = (g_gated * m_norm).astype(BF)
    gm = norm_back(mixed, (g_gated * pre_u).reshape(shape)).astype(BF)
    qg = ein("bihe,bihf->bhef", qs, gm)
    gs = jnp.zeros((heads, HEAD, HEAD), F32)
    for b in reversed(range(blocks)):
        gs = passing[b][:, None, None] * gs + qg[b]
    gs = place_mix(gs, w_outof)
    g_states = [None] * blocks
    for b in reversed(range(blocks)):
        g_states[b] = gs
        gs = passing[b][:, None, None] * gs + qg[b]
    g_states = jnp.stack(g_states).astype(BF)
    g_mixing = ein("bihf,bjhf->bhij", gm, v)
    g_scores = (g_mixing * mask).astype(BF)
    g_q = ein("bhij,bjhe->bihe", g_scores, k) + q_scale[..., None] * ein("bihf,bhef->bihe", gm, states)
    g_k = ein("bhij,bihe->bjhe", g_scores, q) + k_scale[..., None] * ein("bhef,bjhf->bjhe", g_states, v)
    g_v = ein("bhij,bihf->bjhf", mixing, gm) + ein("bjhe,bhef->bjhf", ks, g_states)

    def silu_back(pre_rows, grad):
        sig = jax.nn.sigmoid(pre_rows)
        return (grad * (sig * (1.0 + pre_rows * (1.0 - sig)))).astype(BF)

    g_pre = jnp.concatenate(
        [
            silu_back(pre_q, g_q.reshape(span, cols)),
            silu_back(pre_k, g_k.reshape(span, cols)),
            g_v.reshape(span, cols).astype(BF),
            g_pre_u,
        ],
        1,
    )
    gn = dot(g_pre, w_qkvu, ((1,), (1,))).reshape(TEAM, rows, width)
    gn = team_reduce(in_order([gn[j] for j in range(TEAM)], me))
    grad_x = (my_rows(g_hidden) + norm_back(x_own.astype(F32), gn)).astype(BF)

    def give_back(rows_own):
        ordered = dot(enter, rows_own, ((0,), (0,))).astype(BF)
        back = lax.all_to_all(ordered, ALL, split_axis=0, concat_axis=0, tiled=True)
        return dot(leave, back, ((0,), (0,))).astype(BF)

    output, input_grad = give_back(result), give_back(grad_x)

    def by_place(grad):
        return list(grad.astype(BF).reshape(n_shard, -1, grad.shape[-1]))

    d_down = dot(product, g_all, ((0,), (0,)))
    d_gate, d_up = dot(n2, g_gate, ((0,), (0,))), dot(n2, g_up, ((0,), (0,)))
    d_out = dot(gated, ga, ((0,), (0,)))
    d_qkvu = dot(normed, g_pre, ((0,), (0,)))

    def collect(parts):
        return in_order(team_gather(sum_zh(scatter_shard(parts))), me)

    down = collect(by_place(d_down))
    grad_down = jnp.concatenate(down, 0).astype(F32)
    fin_grad = [jnp.concatenate([a, b], 0) for a, b in zip(by_place(d_gate), by_place(d_up))]
    fin_grad = jnp.stack(collect(fin_grad), 0).reshape(TEAM, 2, depth, n_shard, ff_own)
    grad_fin = fin_grad.transpose(2, 1, 3, 0, 4).reshape(depth, 2 * ff).astype(F32)
    out_cols = width // n_shard
    d_out_cols = [d_out[:, j * out_cols : (j + 1) * out_cols].astype(BF) for j in range(n_shard)]
    d_out_rows = jnp.concatenate(collect(d_out_cols), 0)
    d_out_rows = lax.all_to_all(
        d_out_rows.reshape(n_shard, depth, out_cols), "shard", split_axis=0, concat_axis=0, tiled=True
    )
    grad_out = d_out_rows.transpose(1, 0, 2).reshape(depth, width).astype(F32)
    qkvu = collect(by_place(d_qkvu))
    grads = [
        jnp.concatenate([p[:, i * cols : (i + 1) * cols] for p in qkvu], 1).astype(F32) for i in range(4)
    ]
    return (output, input_grad, *grads, grad_out, grad_fin, grad_down)


N_SHARD = 4
ROWS = 256
WIDTH = 1024
COLS = 256
HEADS_OWN = 2
FF_PART = 176
FF_OWN = 704
SLOTS = 8
DEVICES = 32
TN = ((0,), (0,))
NT = ((1,), (1,))
NN = ((1,), (0,))
GLOBAL = pl.BlockSpec(memory_space=pltpu.VMEM)


def far(*values):
    return tuple(pltpu.with_memory_space_constraint(v, pltpu.HBM) for v in values)


def rel_of(i):
    return (i & 1) * 2 + (i >> 1)


def hbm(shape, dtype=BF):
    return pltpu.HBM(shape, dtype)


def sds(shape, dtype=BF):
    return jax.ShapeDtypeStruct(shape, dtype)


def run(kernel, out, prefetch, args, grid=None, in_specs=None, out_specs=None, scratch=(), mib=16, flops=0, nbytes=0):
    return pl.pallas_call(
        kernel,
        out_shape=out,
        grid_spec=pltpu.PrefetchScalarGridSpec(
            num_scalar_prefetch=len(prefetch),
            grid=grid or (1,),
            in_specs=in_specs,
            out_specs=out_specs,
            scratch_shapes=list(scratch),
        ),
        compiler_params=pltpu.CompilerParams(
            vmem_limit_bytes=mib << 20, dimension_semantics=("arbitrary",) * len(grid or (1,))
        ),
        cost_estimate=pl.CostEstimate(flops=0, bytes_accessed=0, transcendentals=0),
    )(*prefetch, *args)


def full(*shape):
    return pl.BlockSpec(shape, lambda *_: (0,) * len(shape))


def place(info, j):
    return info[1] ^ j


def block_abs(i, info):
    return info[0] ^ rel_of(i)


def seg_scalar(p, ends):
    total = jnp.int32(0)
    for n in range(8):
        total = total + jnp.where(p >= ends[n], 1, 0)
    return jnp.where(p < 0, -1, total)


def seg_vector(base, shape, dim, ends):
    p = base + lax.broadcasted_iota(jnp.int32, shape, dim)
    total = jnp.zeros(shape, jnp.int32)
    for n in range(8):
        total = total + jnp.where(p >= ends[n], 1, 0)
    return total


def scales(a, info, ends, rates, h):
    base = info[2] + a * BLOCK
    prev = seg_scalar(base - 1, ends)
    last = seg_scalar(base + BLOCK - 1, ends)
    seg = seg_vector(base, (BLOCK, HEAD), 0, ends)
    idx = lax.broadcasted_iota(jnp.int32, (BLOCK, HEAD), 0).astype(F32)
    r = rates[info[0] * HEADS_OWN + h]
    q_scale = jnp.where(seg == prev, jnp.exp(-(idx + 1.0) * r), 0.0)
    k_scale = jnp.where(seg == last, jnp.exp(-(BLOCK - 1.0 - idx) * r), 0.0)
    return q_scale, k_scale, passing(a, info, ends, rates, h)


def passing(a, info, ends, rates, h):
    base = info[2] + a * BLOCK
    same = seg_scalar(base - 1, ends) == seg_scalar(base + BLOCK - 1, ends)
    r = rates[info[0] * HEADS_OWN + h]
    return jnp.exp(jnp.full((1, HEAD), -float(BLOCK), F32) * r) * jnp.where(same, 1.0, 0.0)


def decay_masks(info, rates, out):
    dist = lax.broadcasted_iota(jnp.int32, (BLOCK, BLOCK), 0) - lax.broadcasted_iota(jnp.int32, (BLOCK, BLOCK), 1)
    away = jnp.maximum(dist, 0).astype(F32)
    for h in range(HEADS_OWN):
        r = rates[info[0] * HEADS_OWN + h]
        out[h] = jnp.where(dist >= 0, jnp.exp(-away * r), 0.0)


def same_seg(a, info, ends):
    base = info[2] + a * BLOCK
    return seg_vector(base, (BLOCK, 1), 0, ends) == seg_vector(base, (1, BLOCK), 1, ends)


def rms(v):
    return v * lax.rsqrt(jnp.mean(v * v, axis=-1, keepdims=True) + EPS)


def rms_back(v, g):
    s = lax.rsqrt(jnp.mean(v * v, axis=-1, keepdims=True) + EPS)
    return s * g - v * ((s * s * s) * jnp.mean(v * g, axis=-1, keepdims=True))


def lanes(j, info):
    return pl.ds(pl.multiple_of(place(info, j) * 256, 256), 256)


def rows_kernel(info, deal, tok, cot, leave, enter, sent_x, sent_g):
    dev = info[3]
    d = deal[...]
    owner = lax.shift_right_logical(d, 8)
    mine = owner == dev
    r_i = lax.broadcasted_iota(jnp.int32, (ROWS, ROWS), 0)
    c_i = lax.broadcasted_iota(jnp.int32, (ROWS, ROWS), 1)
    upper = jnp.where(r_i < c_i, 1.0, 0.0).astype(BF)
    count = dot(jnp.where(mine, 1.0, 0.0).astype(BF), upper)
    local = (d - dev * ROWS).astype(F32)
    lane8 = lax.broadcasted_iota(jnp.int32, (DEVICES, 128), 1)
    picked = jnp.zeros((DEVICES, 128), F32)
    for slot in range(SLOTS):
        row = jnp.sum(jnp.where(mine & (count == float(slot)), local, 0.0), axis=1, keepdims=True)
        picked = jnp.where(lane8 == slot, row, picked)
    k_r = lax.broadcasted_iota(jnp.int32, (ROWS, DEVICES), 0)
    k_c = lax.broadcasted_iota(jnp.int32, (ROWS, DEVICES), 1)
    spread = jnp.where(lax.shift_right_logical(k_r, 3) == k_c, 1.0, 0.0).astype(BF)
    wide = dot(spread, picked.astype(BF))
    k8 = lax.broadcasted_iota(jnp.int32, (ROWS, 128), 0) & 7
    l8 = lax.broadcasted_iota(jnp.int32, (ROWS, 128), 1)
    column = jnp.sum(jnp.where(k8 == l8, wide, 0.0), axis=1, keepdims=True)
    lv = jnp.where(column == c_i.astype(F32), 1.0, 0.0).astype(BF)
    leave[...] = lv
    sent_x[...] = dot(lv, tok[...]).astype(BF)
    sent_g[...] = dot(lv, cot[...]).astype(BF)
    for i in range(TEAM):
        a = info[0] ^ rel_of(i)
        at = (info[4] * TEAM + a) * N_SHARD + info[1]
        src = lax.shift_right_logical(deal[pl.ds(at, 1), :], 8)
        src_f = src.astype(F32)
        src_col = jnp.sum(jnp.where(r_i == c_i, src_f, 0.0), axis=1, keepdims=True)
        alike = jnp.where((src_col == src_f) & (c_i < r_i), 1.0, 0.0)
        rank = jnp.sum(alike, axis=1, keepdims=True)
        slot = src_col * float(SLOTS) + rank
        enter[i] = jnp.where(slot == c_i.astype(F32), 1.0, 0.0).astype(BF)


def exchange_rows(info, by_device, tokens_in, cotangent):
    return run(
        rows_kernel,
        (sds((ROWS, ROWS)), sds((TEAM, ROWS, ROWS)), sds((ROWS, WIDTH)), sds((ROWS, WIDTH))),
        (info,),
        (by_device, tokens_in, cotangent),
        in_specs=[full(DEVICES, ROWS), full(ROWS, WIDTH), full(ROWS, WIDTH)],
        out_specs=[full(ROWS, ROWS), full(TEAM, ROWS, ROWS), full(ROWS, WIDTH), full(ROWS, WIDTH)],
        flops=4 << 28,
        nbytes=3 << 20,
    )


def quarter_kernel(info, wq, wk, wv, wu, out):
    for t, w in enumerate((wq, wk, wv, wu)):
        out[t * COLS : (t + 1) * COLS] = w[...]


def take_quarter(info, *weights):
    spec = pl.BlockSpec((256, COLS), lambda i, info: (0, info[0]))
    return run(
        quarter_kernel,
        sds((4 * COLS, COLS)),
        (info,),
        weights,
        in_specs=[spec] * 4,
        out_specs=full(4 * COLS, COLS),
        nbytes=1 << 20,
    )


def ff_bundle_kernel(info, fin, down, out, turned):
    me = info[0]
    unit = jnp.where(
        lax.broadcasted_iota(jnp.int32, (256, 256), 0) == lax.broadcasted_iota(jnp.int32, (256, 256), 1), 1.0, 0.0
    ).astype(BF)
    for n in range(11):
        turned[n * 512 : (n + 1) * 512] = dot(fin[:, n * 512 : (n + 1) * 512], unit, TN).astype(BF)
    for n in range(2 * N_SHARD):
        start = pl.multiple_of(n * FF_OWN + me * FF_PART, 16)
        out[n * FF_PART : (n + 1) * FF_PART] = turned[pl.ds(start, FF_PART)]
    for c in range(4):
        rows = pl.ds(pl.multiple_of(me * FF_PART, 16), FF_PART)
        at = 2 * FF_OWN + c * FF_PART
        out[at : at + FF_PART] = down[rows, c * 256 : (c + 1) * 256]


def ff_bundle(info, fin, down):
    return run(
        ff_bundle_kernel,
        sds((3 * FF_OWN, 256)),
        (info,),
        (fin, down),
        in_specs=[full(*fin.shape), full(*down.shape)],
        out_specs=full(3 * FF_OWN, 256),
        scratch=[pltpu.VMEM((8 * FF_OWN, 256), BF)],
        flops=1 << 30,
        nbytes=6 << 20,
    )


def gather_pieces(part):
    return [part] + [send(part, "shard", j) for j in (1, 2, 3)]


def gather_out(w_out, me, shard):
    axes = ("zl", "core", "shard")
    rel = me ^ shard
    wo = w_out
    for j in (1, 2, 3):
        pairs = [(m * N_SHARD + m, m * N_SHARD + (m ^ j)) for m in range(TEAM)]
        wo = jnp.where(rel == j, lax.ppermute(w_out, axes, pairs), wo)
    return wo


def weight_at(refs, j, t):
    return refs[j][t * 256 : (t + 1) * 256]


def project_kernel(info, ends, rates, enter, r0, r1, r2, r3, w0, w1, w2, w3,
                   x, normed, pq, pk, pu, q, k, v, kv, state, scr):
    i = pl.program_id(0)
    a = block_abs(i, info)
    for t, raw in enumerate((r0, r1, r2, r3)):

        @pl.when(i == t)
        def _():
            x[0] = dot(enter[0], raw[...]).astype(BF)

    scr[...] = rms(x[0].astype(F32)).astype(BF)
    normed[0] = scr[...]
    refs = (w0, w1, w2, w3)
    pre = []
    for t in range(4):
        total = dot(scr[:, lanes(0, info)], weight_at(refs, 0, t))
        for j in (1, 2, 3):
            total = total + dot(scr[:, lanes(j, info)], weight_at(refs, j, t))
        pre.append(total)
    pq[0], pk[0], pu[0] = pre[0], pre[1], pre[3]
    qb = (pre[0] * jax.nn.sigmoid(pre[0])).astype(BF)
    kb = (pre[1] * jax.nn.sigmoid(pre[1])).astype(BF)
    vb = pre[2].astype(BF)
    q[0], k[0], v[0] = qb, kb, vb
    for h in range(HEADS_OWN):
        at = slice(h * HEAD, (h + 1) * HEAD)
        _, k_scale, _ = scales(a, info, ends, rates, h)
        ks = (kb[:, at].astype(F32) * k_scale).astype(BF)
        kv[a, h] = dot(ks, vb[:, at], TN)

    @pl.when(i == TEAM - 1)
    def _():
        for h in range(HEADS_OWN):
            total = kv[0, h]
            for b in range(1, TEAM):
                total = passing(b, info, ends, rates, h) * total + kv[b, h]
            state[h] = total.astype(BF)


def project(scal, enter, raws, pieces):
    info = scal[0]
    by_abs = pl.BlockSpec((1, ROWS, COLS), lambda i, info, *_: (block_abs(i, info), 0, 0))
    by_abs_wide = pl.BlockSpec((1, ROWS, WIDTH), lambda i, info, *_: (block_abs(i, info), 0, 0))
    by_i = pl.BlockSpec((1, ROWS, ROWS), lambda i, *_: (i, 0, 0))
    by_i_wide = pl.BlockSpec((1, ROWS, WIDTH), lambda i, *_: (i, 0, 0))
    f32_block, bf_block = sds((TEAM, ROWS, COLS), F32), sds((TEAM, ROWS, COLS))
    return run(
        project_kernel,
        (
            hbm((TEAM, ROWS, WIDTH)), hbm((TEAM, ROWS, WIDTH)), hbm((TEAM, ROWS, COLS), F32), hbm((TEAM, ROWS, COLS), F32),
            f32_block, bf_block, bf_block,
            bf_block, sds((TEAM, HEADS_OWN, HEAD, HEAD), F32), sds((HEADS_OWN, HEAD, HEAD)),
        ),
        scal,
        (enter, *raws, *pieces),
        grid=(TEAM,),
        in_specs=[by_i, *[full(ROWS, WIDTH)] * 4, *[full(*p.shape) for p in pieces]],
        out_specs=[
            by_i_wide, by_abs_wide, *[by_abs] * 6, full(TEAM, HEADS_OWN, HEAD, HEAD), full(HEADS_OWN, HEAD, HEAD),
        ],
        scratch=[pltpu.VMEM((ROWS, WIDTH), BF)],
        flops=3 << 30,
        nbytes=14 << 20,
    )


def local_kernel(info, ends, rates, q, k, v, mixed, dec):
    b = pl.program_id(0)

    @pl.when(b == 0)
    def _():
        decay_masks(info, rates, dec)

    same = same_seg(b, info, ends)
    for h in range(HEADS_OWN):
        at = slice(h * HEAD, (h + 1) * HEAD)
        scores = dot(q[0, :, at], k[0, :, at], NT)
        mixing = jnp.where(same, scores * dec[h], 0.0).astype(BF)
        mixed[0, :, at] = dot(mixing, v[0, :, at])


BLOCK_SPEC = pl.BlockSpec((1, ROWS, COLS), lambda i, *_: (i, 0, 0))


def attend_local(scal, q, k, v):
    return run(
        local_kernel,
        sds((TEAM, ROWS, COLS), F32),
        scal,
        (q, k, v),
        grid=(TEAM,),
        in_specs=[BLOCK_SPEC] * 3,
        out_specs=BLOCK_SPEC,
        scratch=[pltpu.VMEM((HEADS_OWN, BLOCK, BLOCK), F32)],
        flops=1 << 28,
        nbytes=3 << 20,
    )


def run_states(start, step, out, info, ends, rates, order):
    for h in range(HEADS_OWN):
        now = start[h]
        for b in order:
            out[b, h] = now.astype(BF)
            now = passing(b, info, ends, rates, h) * now + step[b, h]


def halves(i, value, keep, give):
    @pl.when(i < 2)
    def _():
        keep[0] = value

    @pl.when(i >= 2)
    def _():
        give[0] = value


def carry_kernel(info, ends, rates, local, q, pu, kv, s_in, wo, mixed, gated, keep, give, states):
    i = pl.program_id(0)
    a = block_abs(i, info)

    @pl.when(i == 0)
    def _():
        run_states(s_in, kv, states, info, ends, rates, range(TEAM))

    for h in range(HEADS_OWN):
        at = slice(h * HEAD, (h + 1) * HEAD)
        q_scale, _, _ = scales(a, info, ends, rates, h)
        qs = (q[0, :, at].astype(F32) * q_scale).astype(BF)
        m = local[0, :, at] + dot(qs, states[a, h])
        mixed[0, :, at] = m
        gated[0, :, at] = (pu[0, :, at] * rms(m)).astype(BF)
    halves(i, dot(gated[0], wo[...]).astype(BF), keep, give)


KEEP = pl.BlockSpec((1, ROWS, WIDTH), lambda i, *_: (jnp.minimum(i, 1), 0, 0))
GIVE = pl.BlockSpec((1, ROWS, WIDTH), lambda i, *_: (jnp.maximum(i - 2, 0), 0, 0))
BY_ABS = pl.BlockSpec((1, ROWS, COLS), lambda i, info, *_: (block_abs(i, info), 0, 0))
BY_ABS_WIDE = pl.BlockSpec((1, ROWS, WIDTH), lambda i, info, *_: (block_abs(i, info), 0, 0))
BY_I = pl.BlockSpec((1, ROWS, ROWS), lambda i, *_: (i, 0, 0))
BY_I_WIDE = pl.BlockSpec((1, ROWS, WIDTH), lambda i, *_: (i, 0, 0))
PAIR = sds((2, ROWS, WIDTH))


def carry_in(scal, local, q, pu, kv, s_in, wo):
    return run(
        carry_kernel,
        (sds((TEAM, ROWS, COLS), F32), sds((TEAM, ROWS, COLS)), PAIR, PAIR),
        scal,
        (local, q, pu, kv, s_in, wo),
        grid=(TEAM,),
        in_specs=[BY_ABS, BY_ABS, BY_ABS, full(*kv.shape), full(*s_in.shape), full(*wo.shape)],
        out_specs=[BY_ABS, BY_ABS, KEEP, GIVE],
        scratch=[pltpu.VMEM((TEAM, HEADS_OWN, HEAD, HEAD), BF)],
        flops=1 << 29,
        nbytes=8 << 20,
    )


def sglu_kernel(info, enter, x, ta, tb, g0, g1, g2, g3, w,
                g, n2, product, gg, gu, r_keep, r_give, n_keep, n_give, wd, scr, back):
    i = pl.program_id(0)
    pieces = [w.at[p] for p in range(N_SHARD)]

    @pl.when(i == 0)
    def _():
        for p in range(N_SHARD):
            for c in range(4):
                at = 2 * FF_OWN + c * FF_PART
                wd[p * FF_PART : (p + 1) * FF_PART, c * 256 : (c + 1) * 256] = w[p, at : at + FF_PART]

    for t, raw in enumerate((g0, g1, g2, g3)):

        @pl.when(i == t)
        def _():
            g[0] = dot(enter[0], raw[...]).astype(BF)

    att = jnp.where(i < 2, ta[0].astype(F32), tb[0].astype(F32))
    scr[...] = rms(x[0].astype(F32) + att).astype(BF)
    n2[0] = scr[...]
    gate = up = None
    for j in range(N_SHARD):
        rows = scr[:, j * 256 : (j + 1) * 256]
        one, two = dot(rows, pieces[j][:FF_OWN], NT), dot(rows, pieces[j][FF_OWN : 2 * FF_OWN], NT)
        gate, up = (one, two) if j == 0 else (gate + one, up + two)
    prod = (gate * up).astype(BF)
    product[0] = prod
    g_prod = dot(g[0], wd[...], NT)
    one, two = (g_prod * up).astype(BF), (g_prod * gate).astype(BF)
    gg[0], gu[0] = one, two
    for j in range(N_SHARD):
        back[:, j * 256 : (j + 1) * 256] = (dot(one, pieces[j][:FF_OWN]) + dot(two, pieces[j][FF_OWN : 2 * FF_OWN])).astype(BF)
    halves(i, back[...], n_keep, n_give)
    halves(i, dot(prod, wd[...]).astype(BF), r_keep, r_give)


def sglu(info, enter, x, ta, tb, raws, w_ff):
    hid = pl.BlockSpec((1, ROWS, FF_OWN), lambda i, *_: (i, 0, 0))
    hid_out = sds((TEAM, ROWS, FF_OWN))
    wide = sds((TEAM, ROWS, WIDTH))
    return run(
        sglu_kernel,
        (wide, wide, hid_out, hid_out, hid_out, PAIR, PAIR, PAIR, PAIR),
        (info,),
        (enter, x, ta, tb, *raws, w_ff),
        grid=(TEAM,),
        in_specs=[BY_I, BY_I_WIDE, KEEP, GIVE, *[full(ROWS, WIDTH)] * 4, full(*w_ff.shape)],
        out_specs=[BY_I_WIDE, BY_I_WIDE, hid, hid, hid, KEEP, GIVE, KEEP, GIVE],
        scratch=[
            pltpu.VMEM((FF_OWN, WIDTH), BF),
            pltpu.VMEM((ROWS, WIDTH), BF),
            pltpu.VMEM((ROWS, WIDTH), BF),
        ],
        mib=34,
        flops=12 << 30,
        nbytes=28 << 20,
    )


def flat(v):
    return v.reshape(-1, v.shape[-1])


def turn(i, first):
    return rel_of(i) if first == 1 else i


def grads_call(kernel, info, rows, args, specs, scratch=(), nbytes=0):
    shape = (2, rows, 256)
    return run(
        kernel,
        (sds(shape), sds(shape)),
        (info,),
        args,
        grid=(N_SHARD,),
        in_specs=specs,
        out_specs=[
            pl.BlockSpec((1, rows, 256), lambda i, *_: (jnp.minimum(i, 1), 0, 0)),
            pl.BlockSpec((1, rows, 256), lambda i, *_: (jnp.maximum(i - 2, 0), 0, 0)),
        ],
        scratch=scratch,
        nbytes=nbytes,
    )


def hidden_grads_kernel(info, n2, grad, keep, give):
    halves(pl.program_id(0), dot(grad[...], n2[...], TN).astype(BF), keep, give)


def hidden_grads(info, n2, grad, first):
    span = TEAM * ROWS
    specs = [
        pl.BlockSpec((span, 256), lambda i, info: (0, place(info, turn(i, first)))),
        full(span, FF_OWN),
    ]
    return grads_call(hidden_grads_kernel, info, FF_OWN, (flat(n2), flat(grad)), specs)


def down_grads(info, g, product, first):
    span = TEAM * ROWS

    def kernel(info, g, product, keep, give, dd):
        i = pl.program_id(0)

        @pl.when(i == 0)
        def _():
            for c in range(4):
                dd[c] = dot(product[...], g[:, c * 256 : (c + 1) * 256], TN).astype(BF)

        rows = pl.ds(pl.multiple_of(place(info, turn(i, first)) * FF_PART, 16), FF_PART)
        for c in range(4):
            at = slice(c * FF_PART, (c + 1) * FF_PART)

            @pl.when(i < 2)
            def _():
                keep[0, at] = dd[c, rows]

            @pl.when(i >= 2)
            def _():
                give[0, at] = dd[c, rows]

    specs = [full(span, WIDTH), full(span, FF_OWN)]
    return grads_call(
        kernel, info, FF_OWN, (flat(g), flat(product)), specs, scratch=[pltpu.VMEM((4, FF_OWN, 256), BF)]
    )


def hidden_back_kernel(info, ends, rates, x, ta, tb, ua, ub, g, wo, mixed, pu, q,
                       ga, gpu, gm, qg, gh, state):
    i = pl.program_id(0)
    a = block_abs(i, info)
    att = jnp.where(i < 2, ta[0].astype(F32), tb[0].astype(F32))
    gn2 = jnp.where(i < 2, ua[0].astype(F32), ub[0].astype(F32))
    grad = g[0].astype(F32) + rms_back(x[0].astype(F32) + att, gn2)
    ga[0] = grad.astype(BF)

    @pl.when(i == 0)
    def _():
        gh[...] = grad

    g_gated = dot(ga[0], wo[...], NT)
    for h in range(HEADS_OWN):
        at = slice(h * HEAD, (h + 1) * HEAD)
        m = mixed[0, :, at]
        gpu[0, :, at] = (g_gated[:, at] * rms(m)).astype(BF)
        gmb = rms_back(m, g_gated[:, at] * pu[0, :, at]).astype(BF)
        gm[0, :, at] = gmb
        q_scale, _, _ = scales(a, info, ends, rates, h)
        qs = (q[0, :, at].astype(F32) * q_scale).astype(BF)
        qg[a, h] = dot(qs, gmb, TN)

    @pl.when(i == TEAM - 1)
    def _():
        for h in range(HEADS_OWN):
            total = qg[TEAM - 1, h]
            for b in reversed(range(TEAM - 1)):
                total = passing(b, info, ends, rates, h) * total + qg[b, h]
            state[h] = total.astype(BF)


def hidden_back(scal, x, ta, tb, ua, ub, g, wo, mixed, pu, q):
    block = sds((TEAM, ROWS, COLS))
    return run(
        hidden_back_kernel,
        (
            sds((TEAM, ROWS, WIDTH)), block, block, sds((TEAM, HEADS_OWN, HEAD, HEAD), F32), sds((ROWS, WIDTH), F32),
            sds((HEADS_OWN, HEAD, HEAD)),
        ),
        scal,
        (x, ta, tb, ua, ub, g, wo, mixed, pu, q),
        grid=(TEAM,),
        in_specs=[BY_I_WIDE, KEEP, GIVE, KEEP, GIVE, BY_I_WIDE, full(*wo.shape), BY_ABS, BY_ABS, BY_ABS],
        out_specs=[
            BY_ABS_WIDE, BY_ABS, BY_ABS, full(TEAM, HEADS_OWN, HEAD, HEAD), full(ROWS, WIDTH), full(HEADS_OWN, HEAD, HEAD),
        ],
        flops=1 << 30,
        nbytes=14 << 20,
    )


def scores_back_kernel(info, ends, rates, q, k, v, gm, kv, s_in, gq, gk, gv, dec, states):
    b = pl.program_id(0)

    @pl.when(b == 0)
    def _():
        decay_masks(info, rates, dec)
        run_states(s_in, kv, states, info, ends, rates, range(TEAM))

    same = same_seg(b, info, ends)
    for h in range(HEADS_OWN):
        at = slice(h * HEAD, (h + 1) * HEAD)
        qh, kh, vh, gh = q[0, :, at], k[0, :, at], v[0, :, at], gm[0, :, at]
        q_scale, _, _ = scales(b, info, ends, rates, h)
        mixing = jnp.where(same, dot(qh, kh, NT) * dec[h], 0.0).astype(BF)
        g_scores = jnp.where(same, dot(gh, vh, NT) * dec[h], 0.0).astype(BF)
        gq[0, :, at] = dot(g_scores, kh) + q_scale * dot(gh, states[b, h], NT)
        gk[0, :, at] = dot(g_scores, qh, TN)
        gv[0, :, at] = dot(mixing, gh, TN)


def scores_back(scal, q, k, v, gm, kv, s_in):
    block = sds((TEAM, ROWS, COLS), F32)
    return run(
        scores_back_kernel,
        (block, block, block),
        scal,
        (q, k, v, gm, kv, s_in),
        grid=(TEAM,),
        in_specs=[*[BLOCK_SPEC] * 4, full(*kv.shape), full(*s_in.shape)],
        out_specs=[BLOCK_SPEC] * 3,
        scratch=[
            pltpu.VMEM((HEADS_OWN, BLOCK, BLOCK), F32),
            pltpu.VMEM((TEAM, HEADS_OWN, HEAD, HEAD), BF),
        ],
        flops=3 << 28,
        nbytes=6 << 20,
    )


def silu_slope(p):
    s = jax.nn.sigmoid(p)
    return s * (1.0 + p * (1.0 - s))


def project_back_kernel(info, ends, rates, gq, gk, gv, pq, pk, k, v, gpu, qg, g_in, w0, w1, w2, w3,
                        dqkv, keep, give, states, back):
    i = pl.program_id(0)
    a = block_abs(i, info)

    @pl.when(i == 0)
    def _():
        run_states(g_in, qg, states, info, ends, rates, (3, 2, 1, 0))

    dqkv[0, :, :COLS] = (gq[0] * silu_slope(pq[0])).astype(BF)
    for h in range(HEADS_OWN):
        at = slice(h * HEAD, (h + 1) * HEAD)
        _, k_scale, _ = scales(a, info, ends, rates, h)
        kh, vh = k[0, :, at], v[0, :, at]
        ks = (kh.astype(F32) * k_scale).astype(BF)
        g_k = gk[0, :, at] + k_scale * dot(vh, states[a, h], NT)
        to_k = slice(COLS + h * HEAD, COLS + (h + 1) * HEAD)
        to_v = slice(2 * COLS + h * HEAD, 2 * COLS + (h + 1) * HEAD)
        dqkv[0, :, to_k] = (g_k * silu_slope(pk[0, :, at])).astype(BF)
        dqkv[0, :, to_v] = (gv[0, :, at] + dot(ks, states[a, h])).astype(BF)
    refs = (w0, w1, w2, w3)
    grads = (dqkv[0, :, :COLS], dqkv[0, :, COLS : 2 * COLS], dqkv[0, :, 2 * COLS :], gpu[0])
    for j in range(N_SHARD):
        total = dot(grads[0], weight_at(refs, j, 0), NT)
        for t in (1, 2, 3):
            total = total + dot(grads[t], weight_at(refs, j, t), NT)
        back[:, lanes(j, info)] = total.astype(BF)
    halves(i, back[...], keep, give)


def project_back(scal, gq, gk, gv, pq, pk, k, v, gpu, qg, g_in, pieces):
    return run(
        project_back_kernel,
        (sds((TEAM, ROWS, 3 * COLS)), PAIR, PAIR),
        scal,
        (gq, gk, gv, pq, pk, k, v, gpu, qg, g_in, *pieces),
        grid=(TEAM,),
        in_specs=[*[BY_ABS] * 8, full(*qg.shape), full(*g_in.shape), *[full(*p.shape) for p in pieces]],
        out_specs=[pl.BlockSpec((1, ROWS, 3 * COLS), lambda i, info, *_: (block_abs(i, info), 0, 0)), KEEP, GIVE],
        scratch=[pltpu.VMEM((TEAM, HEADS_OWN, HEAD, HEAD), BF), pltpu.VMEM((ROWS, WIDTH), BF)],
        flops=5 << 29,
        nbytes=14 << 20,
    )


def column_grads(info, pairs, first):
    span = TEAM * ROWS
    args, specs = [], []
    for pair in pairs:
        for v in pair:
            args.append(v.reshape(span, v.shape[-1]))
            wide = v.shape[-1] == WIDTH
            cut = (lambda i, info: (0, place(info, turn(i, first)))) if wide else (lambda i, info: (0, 0))
            specs.append(pl.BlockSpec((span, 256 if wide else v.shape[-1]), cut))
    n = sum(1 if b.shape[-1] == WIDTH else b.shape[-1] // 256 for _, b in pairs)

    def kernel(info, *refs):
        i = pl.program_id(0)
        values = []
        for t in range(len(pairs)):
            value = dot(refs[2 * t][...], refs[2 * t + 1][...], TN).astype(BF)
            values += [value[:, c * 256 : (c + 1) * 256] for c in range(value.shape[1] // 256)]
        for t, value in enumerate(values):
            at = slice(t * 256, (t + 1) * 256)

            @pl.when(i < 2)
            def _():
                refs[-2][0, at] = value

            @pl.when(i >= 2)
            def _():
                refs[-1][0, at] = value

    return grads_call(kernel, info, n * 256, tuple(args), specs)


def hop(parts, first, hold=()):
    keep, give = parts
    got = send(give, "shard", first)
    if hold:
        got = after(got, *hold)
    total = keep.astype(F32) + got.astype(F32)
    return total[0].astype(BF), total[1].astype(BF)


def hop_two(own, other, first, hold=(), hold_send=()):
    got = send(after(other, *hold_send) if hold_send else other, "shard", 3 - first)
    if hold:
        got = after(got, *hold)
    return (own.astype(F32) + got.astype(F32)).astype(BF)


def over_zh(part, hold=(), hold_send=()):
    if hold_send:
        part = after(part, *hold_send)
    got = send(part, "zh", 1)
    if hold:
        got = after(got, *hold)
    return (part.astype(F32) + got.astype(F32)).astype(BF)


def fin_out_kernel(info, p0, p1, p2, p3, u0, u1, u2, u3, fin, stack):
    unit = jnp.where(
        lax.broadcasted_iota(jnp.int32, (256, 256), 0) == lax.broadcasted_iota(jnp.int32, (256, 256), 1), 1.0, 0.0
    ).astype(BF)
    for j, both in enumerate(((p0, u0), (p1, u1), (p2, u2), (p3, u3))):
        q = info[0] ^ j
        for n in range(2 * N_SHARD):
            start = pl.multiple_of(n * FF_OWN + q * FF_PART, 16)
            m = n % N_SHARD
            stack[pl.ds(start, FF_PART)] = both[n // N_SHARD][m * FF_PART : (m + 1) * FF_PART]
    for n in range(11):
        fin[:, n * 512 : (n + 1) * 512] = dot(unit, stack[n * 512 : (n + 1) * 512], NT)


def fin_out(info, pieces):
    return run(
        fin_out_kernel,
        sds((256, 8 * FF_OWN), F32),
        (info,),
        tuple(pieces),
        in_specs=[full(FF_OWN, 256)] * 8,
        out_specs=full(256, 8 * FF_OWN),
        scratch=[pltpu.VMEM((8 * FF_OWN, 256), BF)],
        mib=24,
        flops=1 << 30,
        nbytes=9 << 20,
    )


def down_out_kernel(info, p0, p1, p2, p3, down):
    for j, p in enumerate((p0, p1, p2, p3)):
        rows = pl.ds(pl.multiple_of((info[0] ^ j) * FF_PART, 16), FF_PART)
        for c in range(4):
            down[rows, c * 256 : (c + 1) * 256] = p[c * FF_PART : (c + 1) * FF_PART].astype(F32)


def down_out(info, pieces):
    return run(
        down_out_kernel,
        sds((FF_OWN, WIDTH), F32),
        (info,),
        tuple(pieces),
        in_specs=[full(FF_OWN, 256)] * 4,
        out_specs=full(FF_OWN, WIDTH),
        nbytes=5 << 20,
    )


def columns_out_kernel(info, *refs):
    pieces, outs = refs[:4], refs[4:]
    for j, p in enumerate(pieces):
        at = pl.ds(pl.multiple_of((info[0] ^ j) * 256, 256), 256)
        for t, out in enumerate(outs):
            out[:, at] = p[t * 256 : (t + 1) * 256].astype(F32)


def columns_out(info, pieces, n):
    return run(
        columns_out_kernel,
        (sds((256, WIDTH), F32),) * n,
        (info,),
        tuple(pieces),
        in_specs=[full(*p.shape) for p in pieces],
        out_specs=[full(256, WIDTH)] * n,
        nbytes=(3 * n) << 19,
    )


def out_grad_kernel(info, o0, o1, o2, o3, p0, p1, p2, p3, g_out, g_u):
    for j, (o, p) in enumerate(zip((o0, o1, o2, o3), (p0, p1, p2, p3))):
        g_out[:, lanes(j, info)] = o[...].astype(F32)
        g_u[:, pl.ds(pl.multiple_of((info[0] ^ j) * 256, 256), 256)] = p[256:].astype(F32)


def finish_kernel(x, gh, here, got, enter, out):
    gn = here[...] + got[...].astype(F32)
    grad = (gh[...] + rms_back(x[0].astype(F32), gn)).astype(BF)
    out[...] = dot(enter[0], grad, TN).astype(BF)


def result_kernel(x, att, here, got, enter, out):
    result = (x[0].astype(F32) + att[0].astype(F32) + here[...] + got[...].astype(F32)).astype(BF)
    out[...] = dot(enter[0], result, TN).astype(BF)


def finish(kernel, x, second, here, got, enter):
    first = lambda v: pl.BlockSpec((1, *v.shape[1:]), lambda _: (0,) * v.ndim) if v.ndim == 3 else full(*v.shape)
    args = (x, second, here, got, enter)
    return run(
        kernel,
        sds((ROWS, WIDTH)),
        (),
        args,
        in_specs=[first(v) for v in args],
        out_specs=full(ROWS, WIDTH),
        flops=1 << 28,
        nbytes=4 << 20,
    )


def unsort_kernel(leave, rows, out):
    out[...] = dot(leave[...], rows[...], TN).astype(BF)


def unsort(leave, rows):
    return run(
        unsort_kernel,
        sds((ROWS, WIDTH)),
        (),
        (leave, rows),
        in_specs=[full(ROWS, ROWS), full(ROWS, WIDTH)],
        out_specs=full(ROWS, WIDTH),
        flops=1 << 28,
        nbytes=2 << 20,
    )


def exchange(rows):
    return lax.all_to_all(rows, ALL, split_axis=0, concat_axis=0, tiled=True)


def team_raw(own):
    pair = send(own, "zl", 1)
    return [own, pair, send(own, "core", 1), send(pair, "core", 1)]


def team_sum(keep, give, hold=()):
    got = send(give, "core", 1)
    half = (keep.astype(F32) + got.astype(F32)).astype(BF)
    other = send(half, "zl", 1)
    if hold:
        other = after(other, *hold)
    ours = (half.astype(F32) + other[::-1].astype(F32)).astype(BF)
    return ours, send(ours, "core", 1), half


def team_own(keep, give, *behind):
    got = send(give, "core", 1)
    here = keep[0].astype(F32) + got[0].astype(F32)
    there = (keep[1].astype(F32) + got[1].astype(F32)).astype(BF)
    if behind:
        there = after(there, *behind)
    return here, send(there, "zl", 1), there


def state_in(state, near, whole, cross):
    low = [state] + [lax.ppermute(state, "shard", [(i, i ^ j) for i in range(4)]) for j in (1, 2, 3)]
    wide = [v.astype(F32) for v in low]
    hand = sum(whole[j][:, None, None] * wide[j] for j in range(4)).astype(BF)
    got = send(hand, "zh", 1)
    here = sum(near[j][:, None, None] * wide[j] for j in (1, 2, 3))
    return here + cross[:, None, None] * got.astype(F32), hand


def fast_body(tokens_in, cotangent, deal_order, lengths, decay_rates, w_query, w_key, w_value, w_ugate, w_out, w_ffin, w_ffdown):
    zh, zl, core, shard = (lax.axis_index(a) for a in ALL)
    me = zl * 2 + core
    group = zh * N_SHARD + shard
    device = (zh * TEAM + me) * N_SHARD + shard
    span = TEAM * ROWS
    info = jnp.stack([me, shard, group * span, device, zh, jnp.int32(0), jnp.int32(0), jnp.int32(0)]).astype(jnp.int32)
    ends = jnp.sum(jnp.where(jnp.arange(8)[None, :] <= jnp.arange(8)[:, None], lengths[None, :], 0), axis=1).astype(jnp.int32)
    scal = (info, ends, decay_rates)
    by_device = deal_order.reshape(2, N_SHARD, TEAM, ROWS).transpose(0, 2, 1, 3).reshape(DEVICES, ROWS)

    leave, enter, sent_x, sent_g = exchange_rows(info, by_device, *far(tokens_in, cotangent))
    raw_x = exchange(sent_x)
    quarter = take_quarter(after(info, sent_x), *far(w_query, w_key, w_value, w_ugate))
    w_proj = gather_pieces(quarter)
    w_ff = lax.all_gather(after(ff_bundle(after(info, quarter), *far(w_ffin, w_ffdown)), raw_x), "shard", axis=0)
    wo = gather_out(w_out, me, shard)
    x_raws = team_raw(raw_x)
    raw_g = exchange(after(sent_g, raw_x))
    g_raws = team_raw(raw_g)

    ids = jnp.arange(8)
    last = jnp.sum(((ids[:, None] + 1) * span - 1 >= ends[None, :]).astype(jnp.int32), axis=1)
    before = jnp.where(ids == 0, -1, jnp.sum((ids[:, None] * span - 1 >= ends[None, :]).astype(jnp.int32), axis=1))
    rates = lax.dynamic_slice_in_dim(decay_rates, me * HEADS_OWN, HEADS_OWN)

    def weigh(flag, gap):
        return jnp.where(flag[..., None], jnp.exp(-(jnp.maximum(gap, 0) * span).astype(F32)[..., None] * rates), 0.0)

    js = jnp.arange(4)
    peers = zh * N_SHARD + (shard ^ js)
    my_last, my_before = last[group], before[group]
    f_near = weigh((peers < group) & (last[peers] == my_before), group - 1 - peers)
    end = zh * N_SHARD + 3
    f_whole = weigh(last[peers] == last[end], end - peers)
    f_cross = weigh((zh == 1) & (last[3] == my_before), shard)
    b_near = weigh((peers > group) & (before[peers] == my_last), peers - 1 - group)
    start = zh * N_SHARD
    b_whole = weigh(before[peers] == before[start], peers - start)
    b_cross = weigh((zh == 0) & (before[4] == my_last), 3 - shard)

    x, normed, pq, pk, pu, q, k, v, kv, state = project(scal, enter, far(*x_raws), far(*w_proj))
    s_in, _ = state_in(state, f_near, f_whole, f_cross)
    local = attend_local(scal, q, k, v)
    mixed, gated, a_keep, a_give = carry_in((after(info, g_raws[1]), *scal[1:]), local, q, pu, kv, s_in, wo)
    ta, tb, _ = team_sum(a_keep, a_give)
    g, n2, product, gg, gu, r_keep, r_give, n_keep, n_give = sglu(info, enter, x, ta, tb, far(*g_raws), *far(w_ff))
    n_got = send(n_give, "core", 1)
    n_half = (n_keep.astype(F32) + n_got.astype(F32)).astype(BF)
    n_other = send(n_half, "zl", 1)
    d_gate = hidden_grads(after(info, n_half), n2, gg, 1)
    d_up = hidden_grads(after(info, d_gate[1]), n2, gu, 2)
    d_down = down_grads(after(info, d_up[1]), g, product, 1)
    n_other = after(n_other, d_down[1])
    ua = (n_half.astype(F32) + n_other[::-1].astype(F32)).astype(BF)
    ub = send(ua, "core", 1)
    gate_own, gate_other = hop(d_gate, 1, hold=(ua,))
    up_own, up_other = hop(d_up, 2, hold=(ua,))
    gate = hop_two(gate_own, gate_other, 1, hold=(gate_other,))

    ga, gpu, gm, qg, gh, g_state = hidden_back((after(info, gate_other, up_other), *scal[1:]), x, ta, tb, ua, ub, g, wo, mixed, pu, q)
    g_in, handed = state_in(g_state, b_near, b_whole, b_cross)
    gq, gk, gv = scores_back((after(info, gate), *scal[1:]), q, k, v, gm, kv, s_in)
    d_ou = column_grads(after(info, gq), [(gated, ga), (normed, gpu)], 2)
    up = hop_two(up_own, up_other, 2, hold=(handed,))
    r_here, r_there, r_sent = team_own(r_keep, r_give, ub)
    sent_back = finish(result_kernel, x, ta, r_here, r_there, after(enter, gq))
    dqkv, p_keep, p_give = project_back(
        (after(info, d_ou[1], sent_back), *scal[1:]), gq, gk, gv, pq, pk, k, v, gpu, qg, g_in, far(*w_proj)
    )
    here, there, p_sent = team_own(p_keep, p_give)
    d_qkv = column_grads(after(info, p_sent), [(normed, dqkv)], 1)
    qkv_own, qkv_other = hop(d_qkv, 1, hold=(p_sent,))
    last_sent = finish(finish_kernel, x, gh, here, there, enter)
    input_grad = unsort(leave, exchange(last_sent))
    output = unsort(leave, exchange(after(sent_back, last_sent)))

    gate_sum = over_zh(gate, hold=(p_sent,), hold_send=(gq,))
    up_sum = over_zh(up, hold=(p_sent,), hold_send=(gq,))
    down = hop_two(*hop(d_down, 1, hold=(p_sent,)), 1, hold=(p_sent,))
    ou = hop_two(*hop(d_ou, 2, hold=(p_sent,)), 2, hold=(p_sent,))
    down_sum = over_zh(down)
    ou_sum = over_zh(ou)
    qkv_sum = over_zh(hop_two(qkv_own, qkv_other, 1))
    grad_fin = fin_out(info, (*far(*team_gather(gate_sum)), *far(*team_gather(up_sum))))
    grad_down = down_out(info, far(*team_gather(down_sum)))
    ou = team_gather(ou_sum)
    outs = []
    for j in range(4):
        pick = me ^ shard ^ j
        top = [p[:256] for p in ou]
        piece = jnp.where(pick < 2, jnp.where(pick == 0, top[0], top[1]), jnp.where(pick == 2, top[2], top[3]))
        outs.append(piece if j == 0 else send(piece, "shard", j))
    grad_out, grad_u = run(
        out_grad_kernel,
        (sds((256, WIDTH), F32),) * 2,
        (info,),
        far(*outs, *ou),
        in_specs=[*[full(256, 256)] * 4, *[full(512, 256)] * 4],
        out_specs=[full(256, WIDTH)] * 2,
        nbytes=3 << 20,
    )
    grad_q, grad_k, grad_v = columns_out(info, far(*team_gather(qkv_sum)), 3)
    return (output, input_grad, grad_q, grad_k, grad_v, grad_u, grad_out, grad_fin, grad_down)


def solution(mesh):
    rep, shard = mesh.shape["rep"], mesh.shape["shard"]
    team = Mesh(mesh.devices.reshape(rep // TEAM, 2, 2, shard), ALL)
    token, weight = P(ALL, None), P("shard", None)
    return jax.shard_map(
        fast_body if (rep, shard) == (8, 4) else general_body,
        mesh=team,
        in_specs=(token, token, P(), P(), P(), *([weight] * 7)),
        out_specs=(token, token, *([weight] * 7)),
        check_vma=False,
    )
```

```python
import functools

import jax
import jax.numpy as jnp
from jax import lax
from jax.experimental import pallas as pl
from jax.experimental.pallas import tpu as pltpu
from jax.sharding import Mesh, PartitionSpec as P

HEAD = 128
BLOCK = 256
TEAM = 4
EPS = 1e-06
BF = jnp.bfloat16
F32 = jnp.float32
ALL = ("zh", "zl", "core", "shard")


def send(value, axis, mask):
    size = lax.axis_size(axis)
    return lax.ppermute(value, axis, [(i, i ^ mask) for i in range(size)])


def dot(a, b, dims=((1,), (0,))):
    return lax.dot_general(a, b, (dims, ((), ())), preferred_element_type=F32)


def norm_scale(values):
    return lax.rsqrt(jnp.mean(values * values, axis=-1, keepdims=True) + EPS)


def norm_back(values, grad):
    scale = norm_scale(values)
    return scale * grad - values * (scale**3) * jnp.mean(values * grad, axis=-1, keepdims=True)


def in_order(pieces, index):
    pieces = list(pieces)
    bit = 1
    while bit < len(pieces):
        flip = (index & bit) != 0
        pieces = [jnp.where(flip, pieces[j ^ bit], pieces[j]) for j in range(len(pieces))]
        bit *= 2
    return pieces


def gather_shard(part):
    size = lax.axis_size("shard")
    if size != 4:
        every = lax.all_gather(part, "shard", axis=0)
        return [every[j] for j in range(size)]
    half = part.shape[0] // 2
    by_x, by_y = send(part, "shard", 1), send(part, "shard", 2)
    far = jnp.concatenate([send(by_x[:half], "shard", 2), send(by_y[half:], "shard", 1)], 0)
    return in_order([part, by_x, by_y, far], lax.axis_index("shard"))


def scatter_shard(parts):
    size = lax.axis_size("shard")
    if size != 4:
        return lax.psum_scatter(jnp.stack(parts), "shard", scatter_dimension=0, tiled=False)
    rel = in_order(parts, lax.axis_index("shard"))
    total = rel[0].astype(F32)
    for j in (1, 2, 3):
        total = total + send(rel[j].astype(BF), "shard", j).astype(F32)
    return total


def sum_zh(part):
    size = lax.axis_size("zh")
    part = part.astype(BF)
    if size != 2:
        return lax.psum(part.astype(F32), "zh").astype(BF)
    return (part.astype(F32) + send(part, "zh", 1).astype(F32)).astype(BF)


def team_gather(own):
    pair = send(own, "zl", 1)
    return [own, send(own, "core", 1), pair, send(pair, "core", 1)]


def team_reduce(parts):
    low = [p.astype(BF) for p in parts]
    here = parts[0] + send(low[1], "core", 1).astype(F32)
    there = parts[2] + send(low[3], "core", 1).astype(F32)
    return here + send(there.astype(BF), "zl", 1).astype(F32)


def place_mix(state, weights):
    groups = lax.axis_size("zh") * lax.axis_size("shard")
    mine = lax.axis_index("zh") * lax.axis_size("shard") + lax.axis_index("shard")
    low = state.astype(BF)
    if groups != 8:
        every = lax.all_gather(low, ("zh", "shard"), axis=0).astype(F32)
        return jnp.sum(every * weights[:, :, None, None], axis=0)
    total = jnp.zeros_like(state)
    for j in range(1, groups):
        got = lax.ppermute(low, ("zh", "shard"), [(i, i ^ j) for i in range(groups)])
        factor = lax.dynamic_index_in_dim(weights, mine ^ j, 0, keepdims=False)
        total = total + factor[:, None, None] * got.astype(F32)
    return total


def after(value, *others):
    return lax.optimization_barrier((value, *others))[0]


def general_body(tokens_in, cotangent, deal_order, lengths, decay_rates, w_query, w_key, w_value, w_ugate, w_out, w_ffin, w_ffdown):
    rows, width = tokens_in.shape
    n_zh, n_shard = lax.axis_size("zh"), lax.axis_size("shard")
    groups = n_zh * n_shard
    devices = groups * TEAM
    zh, zl, core, shard = (lax.axis_index(a) for a in ALL)
    me = zl * 2 + core
    group = zh * n_shard + shard
    device = (zh * TEAM + me) * n_shard + shard
    heads = width // HEAD // TEAM
    cols = heads * HEAD
    depth = w_query.shape[0]
    ff = w_ffin.shape[1] // 2
    ff_shard = w_ffdown.shape[0]
    ff_own = ff_shard // TEAM
    per_peer = rows // devices
    span = rows * TEAM

    by_device = deal_order.reshape(n_zh, n_shard, TEAM, rows).transpose(0, 2, 1, 3).reshape(-1)
    row_ids = jnp.arange(rows, dtype=jnp.int32)
    key = jnp.sum(
        jnp.where(
            by_device[:, None] == device * rows + row_ids[None, :],
            jnp.arange(by_device.shape[0], dtype=jnp.int32)[:, None],
            0,
        ),
        axis=0,
    )
    rank = jnp.sum((key[:, None] < key[None, :]).astype(jnp.int32), axis=0)
    leave = (row_ids[:, None] == rank[None, :]).astype(BF)
    sent_x = dot(leave, tokens_in).astype(BF)
    sent_g = dot(leave, cotangent).astype(BF)
    got_x = lax.all_to_all(sent_x, ALL, split_axis=0, concat_axis=0, tiled=True)
    own_block = lax.dynamic_slice_in_dim(by_device, device * rows, rows)
    source = own_block // rows
    earlier = row_ids[None, :] < row_ids[:, None]
    own_rank = jnp.sum(((source[:, None] == source[None, :]) & earlier).astype(jnp.int32), axis=1)
    slot = source * per_peer + own_rank
    enter = (slot[:, None] == row_ids[None, :]).astype(BF)
    x_own = dot(enter, got_x).astype(BF)
    got_g = lax.all_to_all(after(sent_g, got_x), ALL, split_axis=0, concat_axis=0, tiled=True)
    g_own = dot(enter, got_g).astype(BF)

    def quarter(w):
        return lax.dynamic_slice_in_dim(w, me * cols, cols, axis=1)

    qkvu_part = jnp.concatenate([quarter(w) for w in (w_query, w_key, w_value, w_ugate)], 1)
    w_qkvu = jnp.concatenate(gather_shard(qkvu_part), 0)
    out_all = jnp.concatenate(gather_shard(after(w_out, w_qkvu)), 0)
    w_o = lax.dynamic_slice_in_dim(out_all, me * cols, cols)
    fin = w_ffin.reshape(depth, 2, n_shard, TEAM, ff_own)
    fin = lax.dynamic_index_in_dim(fin, me, 3, keepdims=False)
    fin = fin.transpose(1, 0, 2, 3).reshape(2 * depth, n_shard * ff_own)
    fin_parts = gather_shard(after(fin, out_all))
    w_gate = jnp.concatenate([p[:depth] for p in fin_parts], 0)
    w_up = jnp.concatenate([p[depth:] for p in fin_parts], 0)
    fdown = lax.dynamic_slice_in_dim(w_ffdown, me * ff_own, ff_own)
    w_down = jnp.concatenate(gather_shard(after(fdown, w_up)), 0)

    ends = jnp.sum(jnp.where(jnp.arange(8)[None, :] <= jnp.arange(8)[:, None], lengths[None, :], 0), axis=1)
    all_last = jnp.arange(1, groups + 1) * span - 1
    last_seg = jnp.sum((all_last[:, None] >= ends[None, :]).astype(jnp.int32), axis=1)
    before_seg = jnp.concatenate([jnp.full((1,), -1, jnp.int32), last_seg[:-1]])
    positions = group * span + jnp.arange(span)
    seg = jnp.sum((positions[:, None] >= ends[None, :]).astype(jnp.int32), axis=1)
    seg_before = before_seg[group]
    blocks = span // BLOCK
    seg_b = seg.reshape(blocks, BLOCK)
    prev_b = jnp.concatenate([seg_before[None], seg_b[:-1, -1]])
    rates = lax.dynamic_slice_in_dim(decay_rates, me * heads, heads)
    idx = jnp.arange(BLOCK).astype(F32)
    dist = idx[:, None] - idx[None, :]
    decay = jnp.where(dist >= 0, jnp.exp(-rates[:, None, None] * jnp.maximum(dist, 0.0)), 0.0)
    same = (seg_b[:, :, None] == seg_b[:, None, :]).astype(F32)
    mask = same[:, None] * decay[None]
    carry = (seg_b == prev_b[:, None]).astype(F32)
    q_scale = jnp.exp(-(idx + 1.0)[None, :, None] * rates) * carry[:, :, None]
    k_scale = jnp.exp(-(BLOCK - 1.0 - idx)[None, :, None] * rates) * (seg_b == seg_b[:, -1:]).astype(F32)[:, :, None]
    passing = (seg_b[:, -1] == prev_b).astype(F32)[:, None] * jnp.exp(-rates * BLOCK)[None]
    ids = jnp.arange(groups)
    gap = jnp.maximum(jnp.abs(ids - group) - 1, 0).astype(F32) * span
    into = (ids < group) & (last_seg == seg_before)
    outof = (ids > group) & (before_seg == last_seg[group])
    fade = jnp.exp(-gap[:, None] * rates[None, :])
    w_into = jnp.where(into[:, None], fade, 0.0)
    w_outof = jnp.where(outof[:, None], fade, 0.0)

    x = in_order(team_gather(x_own), me)
    x_all = jnp.concatenate(x, 0)
    xf = x_all.astype(F32)
    normed = (xf * norm_scale(xf)).astype(BF)
    pre = dot(normed, w_qkvu)
    pre_q, pre_k, pre_v, pre_u = (pre[:, i * cols : (i + 1) * cols] for i in range(4))
    shape = (blocks, BLOCK, heads, HEAD)
    q = jax.nn.silu(pre_q).astype(BF).reshape(shape)
    k = jax.nn.silu(pre_k).astype(BF).reshape(shape)
    v = pre_v.astype(BF).reshape(shape)

    def ein(text, a, b):
        return jnp.einsum(text, a, b, preferred_element_type=F32)

    ks = (k.astype(F32) * k_scale[..., None]).astype(BF)
    qs = (q.astype(F32) * q_scale[..., None]).astype(BF)
    kv = ein("bjhe,bjhf->bhef", ks, v)
    state = jnp.zeros((heads, HEAD, HEAD), F32)
    for b in range(blocks):
        state = passing[b][:, None, None] * state + kv[b]
    state_in = place_mix(state, w_into)
    scores = ein("bihe,bjhe->bhij", q, k)
    mixing = (scores * mask).astype(BF)
    mixed = ein("bhij,bjhf->bihf", mixing, v)
    states = []
    state = state_in
    for b in range(blocks):
        states.append(state)
        state = passing[b][:, None, None] * state + kv[b]
    states = jnp.stack(states).astype(BF)
    mixed = mixed + ein("bihe,bhef->bihf", qs, states)
    m_norm = (mixed * norm_scale(mixed)).reshape(span, cols)
    gated = (pre_u * m_norm).astype(BF)
    part = dot(gated, w_o).reshape(TEAM, rows, width)
    att = team_reduce(in_order([part[j] for j in range(TEAM)], me))
    att = jnp.concatenate(in_order(team_gather(att.astype(BF)), me), 0)
    hidden = xf + att.astype(F32)

    g_all = jnp.concatenate(in_order(team_gather(g_own), me), 0)
    n2 = (hidden * norm_scale(hidden)).astype(BF)
    gate, up = dot(n2, w_gate), dot(n2, w_up)
    product = (gate * up).astype(BF)
    res = dot(product, w_down).reshape(TEAM, rows, width)
    g_product = dot(g_all, w_down, ((1,), (1,)))
    g_gate, g_up = (g_product * up).astype(BF), (g_product * gate).astype(BF)
    gn2 = dot(g_gate, w_gate, ((1,), (1,))) + dot(g_up, w_up, ((1,), (1,)))
    gn2 = gn2.reshape(TEAM, rows, width)
    gn2 = team_reduce(in_order([gn2[j] for j in range(TEAM)], me))
    gn2 = jnp.concatenate(in_order(team_gather(gn2.astype(BF)), me), 0)
    g_hidden = g_all.astype(F32) + norm_back(hidden, gn2.astype(F32))
    ga = g_hidden.astype(BF)

    res = team_reduce(in_order([res[j] for j in range(TEAM)], me))
    my_rows = lambda a: lax.dynamic_slice_in_dim(a, me * rows, rows)
    result = (my_rows(hidden) + res).astype(BF)

    g_gated = dot(ga, w_o, ((1,), (1,)))
    g_pre_u = (g_gated * m_norm).astype(BF)
    gm = norm_back(mixed, (g_gated * pre_u).reshape(shape)).astype(BF)
    qg = ein("bihe,bihf->bhef", qs, gm)
    gs = jnp.zeros((heads, HEAD, HEAD), F32)
    for b in reversed(range(blocks)):
        gs = passing[b][:, None, None] * gs + qg[b]
    gs = place_mix(gs, w_outof)
    g_states = [None] * blocks
    for b in reversed(range(blocks)):
        g_states[b] = gs
        gs = passing[b][:, None, None] * gs + qg[b]
    g_states = jnp.stack(g_states).astype(BF)
    g_mixing = ein("bihf,bjhf->bhij", gm, v)
    g_scores = (g_mixing * mask).astype(BF)
    g_q = ein("bhij,bjhe->bihe", g_scores, k) + q_scale[..., None] * ein("bihf,bhef->bihe", gm, states)
    g_k = ein("bhij,bihe->bjhe", g_scores, q) + k_scale[..., None] * ein("bhef,bjhf->bjhe", g_states, v)
    g_v = ein("bhij,bihf->bjhf", mixing, gm) + ein("bjhe,bhef->bjhf", ks, g_states)

    def silu_back(pre_rows, grad):
        sig = jax.nn.sigmoid(pre_rows)
        return (grad * (sig * (1.0 + pre_rows * (1.0 - sig)))).astype(BF)

    g_pre = jnp.concatenate(
        [
            silu_back(pre_q, g_q.reshape(span, cols)),
            silu_back(pre_k, g_k.reshape(span, cols)),
            g_v.reshape(span, cols).astype(BF),
            g_pre_u,
        ],
        1,
    )
    gn = dot(g_pre, w_qkvu, ((1,), (1,))).reshape(TEAM, rows, width)
    gn = team_reduce(in_order([gn[j] for j in range(TEAM)], me))
    grad_x = (my_rows(g_hidden) + norm_back(x_own.astype(F32), gn)).astype(BF)

    def give_back(rows_own):
        ordered = dot(enter, rows_own, ((0,), (0,))).astype(BF)
        back = lax.all_to_all(ordered, ALL, split_axis=0, concat_axis=0, tiled=True)
        return dot(leave, back, ((0,), (0,))).astype(BF)

    output, input_grad = give_back(result), give_back(grad_x)

    def by_place(grad):
        return list(grad.astype(BF).reshape(n_shard, -1, grad.shape[-1]))

    d_down = dot(product, g_all, ((0,), (0,)))
    d_gate, d_up = dot(n2, g_gate, ((0,), (0,))), dot(n2, g_up, ((0,), (0,)))
    d_out = dot(gated, ga, ((0,), (0,)))
    d_qkvu = dot(normed, g_pre, ((0,), (0,)))

    def collect(parts):
        return in_order(team_gather(sum_zh(scatter_shard(parts))), me)

    down = collect(by_place(d_down))
    grad_down = jnp.concatenate(down, 0).astype(F32)
    fin_grad = [jnp.concatenate([a, b], 0) for a, b in zip(by_place(d_gate), by_place(d_up))]
    fin_grad = jnp.stack(collect(fin_grad), 0).reshape(TEAM, 2, depth, n_shard, ff_own)
    grad_fin = fin_grad.transpose(2, 1, 3, 0, 4).reshape(depth, 2 * ff).astype(F32)
    out_cols = width // n_shard
    d_out_cols = [d_out[:, j * out_cols : (j + 1) * out_cols].astype(BF) for j in range(n_shard)]
    d_out_rows = jnp.concatenate(collect(d_out_cols), 0)
    d_out_rows = lax.all_to_all(
        d_out_rows.reshape(n_shard, depth, out_cols), "shard", split_axis=0, concat_axis=0, tiled=True
    )
    grad_out = d_out_rows.transpose(1, 0, 2).reshape(depth, width).astype(F32)
    qkvu = collect(by_place(d_qkvu))
    grads = [
        jnp.concatenate([p[:, i * cols : (i + 1) * cols] for p in qkvu], 1).astype(F32) for i in range(4)
    ]
    return (output, input_grad, *grads, grad_out, grad_fin, grad_down)


N_SHARD = 4
ROWS = 256
WIDTH = 1024
COLS = 256
HEADS_OWN = 2
FF_PART = 176
FF_OWN = 704
SLOTS = 8
DEVICES = 32
TN = ((0,), (0,))
NT = ((1,), (1,))
NN = ((1,), (0,))
GLOBAL = pl.BlockSpec(memory_space=pltpu.VMEM)


def far(*values):
    return tuple(pltpu.with_memory_space_constraint(v, pltpu.HBM) for v in values)


def rel_of(i):
    return (i & 1) * 2 + (i >> 1)


def hbm(shape, dtype=BF):
    return pltpu.HBM(shape, dtype)


def sds(shape, dtype=BF):
    return jax.ShapeDtypeStruct(shape, dtype)


def run(kernel, out, prefetch, args, grid=None, in_specs=None, out_specs=None, scratch=(), mib=16, flops=0, nbytes=0):
    return pl.pallas_call(
        kernel,
        out_shape=out,
        grid_spec=pltpu.PrefetchScalarGridSpec(
            num_scalar_prefetch=len(prefetch),
            grid=grid or (1,),
            in_specs=in_specs,
            out_specs=out_specs,
            scratch_shapes=list(scratch),
        ),
        compiler_params=pltpu.CompilerParams(
            vmem_limit_bytes=mib << 20, dimension_semantics=("arbitrary",) * len(grid or (1,))
        ),
        cost_estimate=pl.CostEstimate(flops=0, bytes_accessed=0, transcendentals=0),
    )(*prefetch, *args)


def full(*shape):
    return pl.BlockSpec(shape, lambda *_: (0,) * len(shape))


def place(info, j):
    return info[1] ^ j


def block_abs(i, info):
    return info[0] ^ rel_of(i)


def seg_scalar(p, ends):
    total = jnp.int32(0)
    for n in range(8):
        total = total + jnp.where(p >= ends[n], 1, 0)
    return jnp.where(p < 0, -1, total)


def seg_vector(base, shape, dim, ends):
    p = base + lax.broadcasted_iota(jnp.int32, shape, dim)
    total = jnp.zeros(shape, jnp.int32)
    for n in range(8):
        total = total + jnp.where(p >= ends[n], 1, 0)
    return total


def scales(a, info, ends, rates, h):
    base = info[2] + a * BLOCK
    prev = seg_scalar(base - 1, ends)
    last = seg_scalar(base + BLOCK - 1, ends)
    seg = seg_vector(base, (BLOCK, HEAD), 0, ends)
    idx = lax.broadcasted_iota(jnp.int32, (BLOCK, HEAD), 0).astype(F32)
    r = rates[info[0] * HEADS_OWN + h]
    q_scale = jnp.where(seg == prev, jnp.exp(-(idx + 1.0) * r), 0.0)
    k_scale = jnp.where(seg == last, jnp.exp(-(BLOCK - 1.0 - idx) * r), 0.0)
    return q_scale, k_scale, passing(a, info, ends, rates, h)


def passing(a, info, ends, rates, h):
    base = info[2] + a * BLOCK
    same = seg_scalar(base - 1, ends) == seg_scalar(base + BLOCK - 1, ends)
    r = rates[info[0] * HEADS_OWN + h]
    return jnp.exp(jnp.full((1, HEAD), -float(BLOCK), F32) * r) * jnp.where(same, 1.0, 0.0)


def decay_masks(info, rates, out):
    dist = lax.broadcasted_iota(jnp.int32, (BLOCK, BLOCK), 0) - lax.broadcasted_iota(jnp.int32, (BLOCK, BLOCK), 1)
    away = jnp.maximum(dist, 0).astype(F32)
    for h in range(HEADS_OWN):
        r = rates[info[0] * HEADS_OWN + h]
        out[h] = jnp.where(dist >= 0, jnp.exp(-away * r), 0.0)


def same_seg(a, info, ends):
    base = info[2] + a * BLOCK
    return seg_vector(base, (BLOCK, 1), 0, ends) == seg_vector(base, (1, BLOCK), 1, ends)


def rms(v):
    return v * lax.rsqrt(jnp.mean(v * v, axis=-1, keepdims=True) + EPS)


def rms_back(v, g):
    s = lax.rsqrt(jnp.mean(v * v, axis=-1, keepdims=True) + EPS)
    return s * g - v * ((s * s * s) * jnp.mean(v * g, axis=-1, keepdims=True))


def lanes(j, info):
    return pl.ds(pl.multiple_of(place(info, j) * 256, 256), 256)


def rows_kernel(info, deal, tok, cot, leave, enter, sent_x, sent_g):
    dev = info[3]
    d = deal[...]
    owner = lax.shift_right_logical(d, 8)
    mine = owner == dev
    r_i = lax.broadcasted_iota(jnp.int32, (ROWS, ROWS), 0)
    c_i = lax.broadcasted_iota(jnp.int32, (ROWS, ROWS), 1)
    upper = jnp.where(r_i < c_i, 1.0, 0.0).astype(BF)
    count = dot(jnp.where(mine, 1.0, 0.0).astype(BF), upper)
    local = (d - dev * ROWS).astype(F32)
    lane8 = lax.broadcasted_iota(jnp.int32, (DEVICES, 128), 1)
    picked = jnp.zeros((DEVICES, 128), F32)
    for slot in range(SLOTS):
        row = jnp.sum(jnp.where(mine & (count == float(slot)), local, 0.0), axis=1, keepdims=True)
        picked = jnp.where(lane8 == slot, row, picked)
    k_r = lax.broadcasted_iota(jnp.int32, (ROWS, DEVICES), 0)
    k_c = lax.broadcasted_iota(jnp.int32, (ROWS, DEVICES), 1)
    spread = jnp.where(lax.shift_right_logical(k_r, 3) == k_c, 1.0, 0.0).astype(BF)
    wide = dot(spread, picked.astype(BF))
    k8 = lax.broadcasted_iota(jnp.int32, (ROWS, 128), 0) & 7
    l8 = lax.broadcasted_iota(jnp.int32, (ROWS, 128), 1)
    column = jnp.sum(jnp.where(k8 == l8, wide, 0.0), axis=1, keepdims=True)
    lv = jnp.where(column == c_i.astype(F32), 1.0, 0.0).astype(BF)
    leave[...] = lv
    sent_x[...] = dot(lv, tok[...]).astype(BF)
    sent_g[...] = dot(lv, cot[...]).astype(BF)
    for i in range(TEAM):
        a = info[0] ^ rel_of(i)
        at = (info[4] * TEAM + a) * N_SHARD + info[1]
        src = lax.shift_right_logical(deal[pl.ds(at, 1), :], 8)
        src_f = src.astype(F32)
        src_col = jnp.sum(jnp.where(r_i == c_i, src_f, 0.0), axis=1, keepdims=True)
        alike = jnp.where((src_col == src_f) & (c_i < r_i), 1.0, 0.0)
        rank = jnp.sum(alike, axis=1, keepdims=True)
        slot = src_col * float(SLOTS) + rank
        enter[i] = jnp.where(slot == c_i.astype(F32), 1.0, 0.0).astype(BF)


def exchange_rows(info, by_device, tokens_in, cotangent):
    return run(
        rows_kernel,
        (sds((ROWS, ROWS)), sds((TEAM, ROWS, ROWS)), sds((ROWS, WIDTH)), sds((ROWS, WIDTH))),
        (info,),
        (by_device, tokens_in, cotangent),
        in_specs=[full(DEVICES, ROWS), full(ROWS, WIDTH), full(ROWS, WIDTH)],
        out_specs=[full(ROWS, ROWS), full(TEAM, ROWS, ROWS), full(ROWS, WIDTH), full(ROWS, WIDTH)],
        flops=4 << 28,
        nbytes=3 << 20,
    )


def quarter_kernel(info, wq, wk, wv, wu, out):
    for t, w in enumerate((wq, wk, wv, wu)):
        out[t * COLS : (t + 1) * COLS] = w[...]


def take_quarter(info, *weights):
    spec = pl.BlockSpec((256, COLS), lambda i, info: (0, info[0]))
    return run(
        quarter_kernel,
        sds((4 * COLS, COLS)),
        (info,),
        weights,
        in_specs=[spec] * 4,
        out_specs=full(4 * COLS, COLS),
        nbytes=1 << 20,
    )


def ff_bundle_kernel(info, fin, down, out, turned):
    me = info[0]
    unit = jnp.where(
        lax.broadcasted_iota(jnp.int32, (256, 256), 0) == lax.broadcasted_iota(jnp.int32, (256, 256), 1), 1.0, 0.0
    ).astype(BF)
    for n in range(11):
        turned[n * 512 : (n + 1) * 512] = dot(fin[:, n * 512 : (n + 1) * 512], unit, TN).astype(BF)
    for n in range(2 * N_SHARD):
        start = pl.multiple_of(n * FF_OWN + me * FF_PART, 16)
        out[n * FF_PART : (n + 1) * FF_PART] = turned[pl.ds(start, FF_PART)]
    for c in range(4):
        rows = pl.ds(pl.multiple_of(me * FF_PART, 16), FF_PART)
        at = 2 * FF_OWN + c * FF_PART
        out[at : at + FF_PART] = down[rows, c * 256 : (c + 1) * 256]


def ff_bundle(info, fin, down):
    return run(
        ff_bundle_kernel,
        sds((3 * FF_OWN, 256)),
        (info,),
        (fin, down),
        in_specs=[full(*fin.shape), full(*down.shape)],
        out_specs=full(3 * FF_OWN, 256),
        scratch=[pltpu.VMEM((8 * FF_OWN, 256), BF)],
        flops=1 << 30,
        nbytes=6 << 20,
    )


def gather_pieces(part):
    return [part] + [send(part, "shard", j) for j in (1, 2, 3)]


def gather_out(w_out, me, shard):
    axes = ("zl", "core", "shard")
    rel = me ^ shard
    wo = w_out
    for j in (1, 2, 3):
        pairs = [(m * N_SHARD + m, m * N_SHARD + (m ^ j)) for m in range(TEAM)]
        wo = jnp.where(rel == j, lax.ppermute(w_out, axes, pairs), wo)
    return wo


def weight_at(refs, j, t):
    return refs[j][t * 256 : (t + 1) * 256]


def project_kernel(info, ends, rates, enter, r0, r1, r2, r3, w0, w1, w2, w3,
                   x, normed, pq, pk, pu, q, k, v, kv, state, scr):
    i = pl.program_id(0)
    a = block_abs(i, info)
    for t, raw in enumerate((r0, r1, r2, r3)):

        @pl.when(i == t)
        def _():
            x[0] = dot(enter[0], raw[...]).astype(BF)

    scr[...] = rms(x[0].astype(F32)).astype(BF)
    normed[0] = scr[...]
    refs = (w0, w1, w2, w3)
    pre = []
    for t in range(4):
        total = dot(scr[:, lanes(0, info)], weight_at(refs, 0, t))
        for j in (1, 2, 3):
            total = total + dot(scr[:, lanes(j, info)], weight_at(refs, j, t))
        pre.append(total)
    pq[0], pk[0], pu[0] = pre[0], pre[1], pre[3]
    qb = (pre[0] * jax.nn.sigmoid(pre[0])).astype(BF)
    kb = (pre[1] * jax.nn.sigmoid(pre[1])).astype(BF)
    vb = pre[2].astype(BF)
    q[0], k[0], v[0] = qb, kb, vb
    for h in range(HEADS_OWN):
        at = slice(h * HEAD, (h + 1) * HEAD)
        _, k_scale, _ = scales(a, info, ends, rates, h)
        ks = (kb[:, at].astype(F32) * k_scale).astype(BF)
        kv[a, h] = dot(ks, vb[:, at], TN)

    @pl.when(i == TEAM - 1)
    def _():
        for h in range(HEADS_OWN):
            total = kv[0, h]
            for b in range(1, TEAM):
                total = passing(b, info, ends, rates, h) * total + kv[b, h]
            state[h] = total.astype(BF)


def project(scal, enter, raws, pieces):
    info = scal[0]
    by_abs = pl.BlockSpec((1, ROWS, COLS), lambda i, info, *_: (block_abs(i, info), 0, 0))
    by_abs_wide = pl.BlockSpec((1, ROWS, WIDTH), lambda i, info, *_: (block_abs(i, info), 0, 0))
    by_i = pl.BlockSpec((1, ROWS, ROWS), lambda i, *_: (i, 0, 0))
    by_i_wide = pl.BlockSpec((1, ROWS, WIDTH), lambda i, *_: (i, 0, 0))
    f32_block, bf_block = sds((TEAM, ROWS, COLS), F32), sds((TEAM, ROWS, COLS))
    return run(
        project_kernel,
        (
            hbm((TEAM, ROWS, WIDTH)), hbm((TEAM, ROWS, WIDTH)), hbm((TEAM, ROWS, COLS), F32), hbm((TEAM, ROWS, COLS), F32),
            f32_block, bf_block, bf_block,
            bf_block, sds((TEAM, HEADS_OWN, HEAD, HEAD), F32), sds((HEADS_OWN, HEAD, HEAD)),
        ),
        scal,
        (enter, *raws, *pieces),
        grid=(TEAM,),
        in_specs=[by_i, *[full(ROWS, WIDTH)] * 4, *[full(*p.shape) for p in pieces]],
        out_specs=[
            by_i_wide, by_abs_wide, *[by_abs] * 6, full(TEAM, HEADS_OWN, HEAD, HEAD), full(HEADS_OWN, HEAD, HEAD),
        ],
        scratch=[pltpu.VMEM((ROWS, WIDTH), BF)],
        flops=3 << 30,
        nbytes=14 << 20,
    )


def local_kernel(info, ends, rates, q, k, v, mixed, dec):
    b = pl.program_id(0)

    @pl.when(b == 0)
    def _():
        decay_masks(info, rates, dec)

    same = same_seg(b, info, ends)
    for h in range(HEADS_OWN):
        at = slice(h * HEAD, (h + 1) * HEAD)
        scores = dot(q[0, :, at], k[0, :, at], NT)
        mixing = jnp.where(same, scores * dec[h], 0.0).astype(BF)
        mixed[0, :, at] = dot(mixing, v[0, :, at])


BLOCK_SPEC = pl.BlockSpec((1, ROWS, COLS), lambda i, *_: (i, 0, 0))


def attend_local(scal, q, k, v):
    return run(
        local_kernel,
        sds((TEAM, ROWS, COLS), F32),
        scal,
        (q, k, v),
        grid=(TEAM,),
        in_specs=[BLOCK_SPEC] * 3,
        out_specs=BLOCK_SPEC,
        scratch=[pltpu.VMEM((HEADS_OWN, BLOCK, BLOCK), F32)],
        flops=1 << 28,
        nbytes=3 << 20,
    )


def run_states(start, step, out, info, ends, rates, order):
    for h in range(HEADS_OWN):
        now = start[h]
        for b in order:
            out[b, h] = now.astype(BF)
            now = passing(b, info, ends, rates, h) * now + step[b, h]


def halves(i, value, keep, give):
    @pl.when(i < 2)
    def _():
        keep[0] = value

    @pl.when(i >= 2)
    def _():
        give[0] = value


def carry_kernel(info, ends, rates, local, q, pu, kv, s_in, wo, mixed, gated, keep, give, states):
    i = pl.program_id(0)
    a = block_abs(i, info)

    @pl.when(i == 0)
    def _():
        run_states(s_in, kv, states, info, ends, rates, range(TEAM))

    for h in range(HEADS_OWN):
        at = slice(h * HEAD, (h + 1) * HEAD)
        q_scale, _, _ = scales(a, info, ends, rates, h)
        qs = (q[0, :, at].astype(F32) * q_scale).astype(BF)
        m = local[0, :, at] + dot(qs, states[a, h])
        mixed[0, :, at] = m
        gated[0, :, at] = (pu[0, :, at] * rms(m)).astype(BF)
    halves(i, dot(gated[0], wo[...]).astype(BF), keep, give)


KEEP = pl.BlockSpec((1, ROWS, WIDTH), lambda i, *_: (jnp.minimum(i, 1), 0, 0))
GIVE = pl.BlockSpec((1, ROWS, WIDTH), lambda i, *_: (jnp.maximum(i - 2, 0), 0, 0))
BY_ABS = pl.BlockSpec((1, ROWS, COLS), lambda i, info, *_: (block_abs(i, info), 0, 0))
BY_ABS_WIDE = pl.BlockSpec((1, ROWS, WIDTH), lambda i, info, *_: (block_abs(i, info), 0, 0))
BY_I = pl.BlockSpec((1, ROWS, ROWS), lambda i, *_: (i, 0, 0))
BY_I_WIDE = pl.BlockSpec((1, ROWS, WIDTH), lambda i, *_: (i, 0, 0))
PAIR = sds((2, ROWS, WIDTH))


def carry_in(scal, local, q, pu, kv, s_in, wo):
    return run(
        carry_kernel,
        (sds((TEAM, ROWS, COLS), F32), sds((TEAM, ROWS, COLS)), PAIR, PAIR),
        scal,
        (local, q, pu, kv, s_in, wo),
        grid=(TEAM,),
        in_specs=[BY_ABS, BY_ABS, BY_ABS, full(*kv.shape), full(*s_in.shape), full(*wo.shape)],
        out_specs=[BY_ABS, BY_ABS, KEEP, GIVE],
        scratch=[pltpu.VMEM((TEAM, HEADS_OWN, HEAD, HEAD), BF)],
        flops=1 << 29,
        nbytes=8 << 20,
    )


def sglu_kernel(info, enter, x, ta, tb, g0, g1, g2, g3, w,
                g, n2, product, gg, gu, r_keep, r_give, n_keep, n_give, wd, scr, back):
    i = pl.program_id(0)
    pieces = [w.at[p] for p in range(N_SHARD)]

    @pl.when(i == 0)
    def _():
        for p in range(N_SHARD):
            for c in range(4):
                at = 2 * FF_OWN + c * FF_PART
                wd[p * FF_PART : (p + 1) * FF_PART, c * 256 : (c + 1) * 256] = w[p, at : at + FF_PART]

    for t, raw in enumerate((g0, g1, g2, g3)):

        @pl.when(i == t)
        def _():
            g[0] = dot(enter[0], raw[...]).astype(BF)

    att = jnp.where(i < 2, ta[0].astype(F32), tb[0].astype(F32))
    scr[...] = rms(x[0].astype(F32) + att).astype(BF)
    n2[0] = scr[...]
    gate = up = None
    for j in range(N_SHARD):
        rows = scr[:, j * 256 : (j + 1) * 256]
        one, two = dot(rows, pieces[j][:FF_OWN], NT), dot(rows, pieces[j][FF_OWN : 2 * FF_OWN], NT)
        gate, up = (one, two) if j == 0 else (gate + one, up + two)
    prod = (gate * up).astype(BF)
    product[0] = prod
    g_prod = dot(g[0], wd[...], NT)
    one, two = (g_prod * up).astype(BF), (g_prod * gate).astype(BF)
    gg[0], gu[0] = one, two
    for j in range(N_SHARD):
        back[:, j * 256 : (j + 1) * 256] = (dot(one, pieces[j][:FF_OWN]) + dot(two, pieces[j][FF_OWN : 2 * FF_OWN])).astype(BF)
    halves(i, back[...], n_keep, n_give)
    halves(i, dot(prod, wd[...]).astype(BF), r_keep, r_give)


def sglu(info, enter, x, ta, tb, raws, w_ff):
    hid = pl.BlockSpec((1, ROWS, FF_OWN), lambda i, *_: (i, 0, 0))
    hid_out = sds((TEAM, ROWS, FF_OWN))
    wide = sds((TEAM, ROWS, WIDTH))
    return run(
        sglu_kernel,
        (wide, wide, hid_out, hid_out, hid_out, PAIR, PAIR, PAIR, PAIR),
        (info,),
        (enter, x, ta, tb, *raws, w_ff),
        grid=(TEAM,),
        in_specs=[BY_I, BY_I_WIDE, KEEP, GIVE, *[full(ROWS, WIDTH)] * 4, full(*w_ff.shape)],
        out_specs=[BY_I_WIDE, BY_I_WIDE, hid, hid, hid, KEEP, GIVE, KEEP, GIVE],
        scratch=[
            pltpu.VMEM((FF_OWN, WIDTH), BF),
            pltpu.VMEM((ROWS, WIDTH), BF),
            pltpu.VMEM((ROWS, WIDTH), BF),
        ],
        mib=34,
        flops=12 << 30,
        nbytes=28 << 20,
    )


def flat(v):
    return v.reshape(-1, v.shape[-1])


def turn(i, first):
    return rel_of(i) if first == 1 else i


def grads_call(kernel, info, rows, args, specs, scratch=(), nbytes=0):
    shape = (2, rows, 256)
    return run(
        kernel,
        (sds(shape), sds(shape)),
        (info,),
        args,
        grid=(N_SHARD,),
        in_specs=specs,
        out_specs=[
            pl.BlockSpec((1, rows, 256), lambda i, *_: (jnp.minimum(i, 1), 0, 0)),
            pl.BlockSpec((1, rows, 256), lambda i, *_: (jnp.maximum(i - 2, 0), 0, 0)),
        ],
        scratch=scratch,
        nbytes=nbytes,
    )


def hidden_grads_kernel(info, n2, grad, keep, give):
    halves(pl.program_id(0), dot(grad[...], n2[...], TN).astype(BF), keep, give)


def hidden_grads(info, n2, grad, first):
    span = TEAM * ROWS
    specs = [
        pl.BlockSpec((span, 256), lambda i, info: (0, place(info, turn(i, first)))),
        full(span, FF_OWN),
    ]
    return grads_call(hidden_grads_kernel, info, FF_OWN, (flat(n2), flat(grad)), specs)


def down_grads(info, g, product, first):
    span = TEAM * ROWS

    def kernel(info, g, product, keep, give, dd):
        i = pl.program_id(0)

        @pl.when(i == 0)
        def _():
            for c in range(4):
                dd[c] = dot(product[...], g[:, c * 256 : (c + 1) * 256], TN).astype(BF)

        rows = pl.ds(pl.multiple_of(place(info, turn(i, first)) * FF_PART, 16), FF_PART)
        for c in range(4):
            at = slice(c * FF_PART, (c + 1) * FF_PART)

            @pl.when(i < 2)
            def _():
                keep[0, at] = dd[c, rows]

            @pl.when(i >= 2)
            def _():
                give[0, at] = dd[c, rows]

    specs = [full(span, WIDTH), full(span, FF_OWN)]
    return grads_call(
        kernel, info, FF_OWN, (flat(g), flat(product)), specs, scratch=[pltpu.VMEM((4, FF_OWN, 256), BF)]
    )


def hidden_back_kernel(info, ends, rates, x, ta, tb, ua, ub, g, wo, mixed, pu, q,
                       ga, gpu, gm, qg, gh, state):
    i = pl.program_id(0)
    a = block_abs(i, info)
    att = jnp.where(i < 2, ta[0].astype(F32), tb[0].astype(F32))
    gn2 = jnp.where(i < 2, ua[0].astype(F32), ub[0].astype(F32))
    grad = g[0].astype(F32) + rms_back(x[0].astype(F32) + att, gn2)
    ga[0] = grad.astype(BF)

    @pl.when(i == 0)
    def _():
        gh[...] = grad

    g_gated = dot(ga[0], wo[...], NT)
    for h in range(HEADS_OWN):
        at = slice(h * HEAD, (h + 1) * HEAD)
        m = mixed[0, :, at]
        gpu[0, :, at] = (g_gated[:, at] * rms(m)).astype(BF)
        gmb = rms_back(m, g_gated[:, at] * pu[0, :, at]).astype(BF)
        gm[0, :, at] = gmb
        q_scale, _, _ = scales(a, info, ends, rates, h)
        qs = (q[0, :, at].astype(F32) * q_scale).astype(BF)
        qg[a, h] = dot(qs, gmb, TN)

    @pl.when(i == TEAM - 1)
    def _():
        for h in range(HEADS_OWN):
            total = qg[TEAM - 1, h]
            for b in reversed(range(TEAM - 1)):
                total = passing(b, info, ends, rates, h) * total + qg[b, h]
            state[h] = total.astype(BF)


def hidden_back(scal, x, ta, tb, ua, ub, g, wo, mixed, pu, q):
    block = sds((TEAM, ROWS, COLS))
    return run(
        hidden_back_kernel,
        (
            sds((TEAM, ROWS, WIDTH)), block, block, sds((TEAM, HEADS_OWN, HEAD, HEAD), F32), sds((ROWS, WIDTH), F32),
            sds((HEADS_OWN, HEAD, HEAD)),
        ),
        scal,
        (x, ta, tb, ua, ub, g, wo, mixed, pu, q),
        grid=(TEAM,),
        in_specs=[BY_I_WIDE, KEEP, GIVE, KEEP, GIVE, BY_I_WIDE, full(*wo.shape), BY_ABS, BY_ABS, BY_ABS],
        out_specs=[
            BY_ABS_WIDE, BY_ABS, BY_ABS, full(TEAM, HEADS_OWN, HEAD, HEAD), full(ROWS, WIDTH), full(HEADS_OWN, HEAD, HEAD),
        ],
        flops=1 << 30,
        nbytes=14 << 20,
    )


def scores_back_kernel(info, ends, rates, q, k, v, gm, kv, s_in, gq, gk, gv, dec, states):
    b = pl.program_id(0)

    @pl.when(b == 0)
    def _():
        decay_masks(info, rates, dec)
        run_states(s_in, kv, states, info, ends, rates, range(TEAM))

    same = same_seg(b, info, ends)
    for h in range(HEADS_OWN):
        at = slice(h * HEAD, (h + 1) * HEAD)
        qh, kh, vh, gh = q[0, :, at], k[0, :, at], v[0, :, at], gm[0, :, at]
        q_scale, _, _ = scales(b, info, ends, rates, h)
        mixing = jnp.where(same, dot(qh, kh, NT) * dec[h], 0.0).astype(BF)
        g_scores = jnp.where(same, dot(gh, vh, NT) * dec[h], 0.0).astype(BF)
        gq[0, :, at] = dot(g_scores, kh) + q_scale * dot(gh, states[b, h], NT)
        gk[0, :, at] = dot(g_scores, qh, TN)
        gv[0, :, at] = dot(mixing, gh, TN)


def scores_back(scal, q, k, v, gm, kv, s_in):
    block = sds((TEAM, ROWS, COLS), F32)
    return run(
        scores_back_kernel,
        (block, block, block),
        scal,
        (q, k, v, gm, kv, s_in),
        grid=(TEAM,),
        in_specs=[*[BLOCK_SPEC] * 4, full(*kv.shape), full(*s_in.shape)],
        out_specs=[BLOCK_SPEC] * 3,
        scratch=[
            pltpu.VMEM((HEADS_OWN, BLOCK, BLOCK), F32),
            pltpu.VMEM((TEAM, HEADS_OWN, HEAD, HEAD), BF),
        ],
        flops=3 << 28,
        nbytes=6 << 20,
    )


def silu_slope(p):
    s = jax.nn.sigmoid(p)
    return s * (1.0 + p * (1.0 - s))


def project_back_kernel(info, ends, rates, gq, gk, gv, pq, pk, k, v, gpu, qg, g_in, w0, w1, w2, w3,
                        dqkv, keep, give, states, back):
    i = pl.program_id(0)
    a = block_abs(i, info)

    @pl.when(i == 0)
    def _():
        run_states(g_in, qg, states, info, ends, rates, (3, 2, 1, 0))

    dqkv[0, :, :COLS] = (gq[0] * silu_slope(pq[0])).astype(BF)
    for h in range(HEADS_OWN):
        at = slice(h * HEAD, (h + 1) * HEAD)
        _, k_scale, _ = scales(a, info, ends, rates, h)
        kh, vh = k[0, :, at], v[0, :, at]
        ks = (kh.astype(F32) * k_scale).astype(BF)
        g_k = gk[0, :, at] + k_scale * dot(vh, states[a, h], NT)
        to_k = slice(COLS + h * HEAD, COLS + (h + 1) * HEAD)
        to_v = slice(2 * COLS + h * HEAD, 2 * COLS + (h + 1) * HEAD)
        dqkv[0, :, to_k] = (g_k * silu_slope(pk[0, :, at])).astype(BF)
        dqkv[0, :, to_v] = (gv[0, :, at] + dot(ks, states[a, h])).astype(BF)
    refs = (w0, w1, w2, w3)
    grads = (dqkv[0, :, :COLS], dqkv[0, :, COLS : 2 * COLS], dqkv[0, :, 2 * COLS :], gpu[0])
    for j in range(N_SHARD):
        total = dot(grads[0], weight_at(refs, j, 0), NT)
        for t in (1, 2, 3):
            total = total + dot(grads[t], weight_at(refs, j, t), NT)
        back[:, lanes(j, info)] = total.astype(BF)
    halves(i, back[...], keep, give)


def project_back(scal, gq, gk, gv, pq, pk, k, v, gpu, qg, g_in, pieces):
    return run(
        project_back_kernel,
        (sds((TEAM, ROWS, 3 * COLS)), PAIR, PAIR),
        scal,
        (gq, gk, gv, pq, pk, k, v, gpu, qg, g_in, *pieces),
        grid=(TEAM,),
        in_specs=[*[BY_ABS] * 8, full(*qg.shape), full(*g_in.shape), *[full(*p.shape) for p in pieces]],
        out_specs=[pl.BlockSpec((1, ROWS, 3 * COLS), lambda i, info, *_: (block_abs(i, info), 0, 0)), KEEP, GIVE],
        scratch=[pltpu.VMEM((TEAM, HEADS_OWN, HEAD, HEAD), BF), pltpu.VMEM((ROWS, WIDTH), BF)],
        flops=5 << 29,
        nbytes=14 << 20,
    )


def column_grads(info, pairs, first):
    span = TEAM * ROWS
    args, specs = [], []
    for pair in pairs:
        for v in pair:
            args.append(v.reshape(span, v.shape[-1]))
            wide = v.shape[-1] == WIDTH
            cut = (lambda i, info: (0, place(info, turn(i, first)))) if wide else (lambda i, info: (0, 0))
            specs.append(pl.BlockSpec((span, 256 if wide else v.shape[-1]), cut))
    n = sum(1 if b.shape[-1] == WIDTH else b.shape[-1] // 256 for _, b in pairs)

    def kernel(info, *refs):
        i = pl.program_id(0)
        values = []
        for t in range(len(pairs)):
            value = dot(refs[2 * t][...], refs[2 * t + 1][...], TN).astype(BF)
            values += [value[:, c * 256 : (c + 1) * 256] for c in range(value.shape[1] // 256)]
        for t, value in enumerate(values):
            at = slice(t * 256, (t + 1) * 256)

            @pl.when(i < 2)
            def _():
                refs[-2][0, at] = value

            @pl.when(i >= 2)
            def _():
                refs[-1][0, at] = value

    return grads_call(kernel, info, n * 256, tuple(args), specs)


def hop(parts, first, hold=(), hold_send=()):
    keep, give = parts
    if hold_send:
        give = after(give, *hold_send)
    got = send(give, "shard", first)
    if hold:
        got = after(got, *hold)
    total = keep.astype(F32) + got.astype(F32)
    return total[0].astype(BF), total[1].astype(BF)


def hop_two(own, other, first):
    return own, send(other, "shard", 3 - first)


def joined(terms, hold=()):
    if hold:
        terms = [(own, after(got, *hold)) for own, got in terms]
    return jnp.concatenate([(own.astype(F32) + got.astype(F32)).astype(BF) for own, got in terms], 0)


def over_zh(part, hold=()):
    got = send(part, "zh", 1)
    if hold:
        got = after(got, *hold)
    return (part.astype(F32) + got.astype(F32)).astype(BF)


def fin_out_kernel(info, p0, p1, p2, p3, fin, stack):
    unit = jnp.where(
        lax.broadcasted_iota(jnp.int32, (256, 256), 0) == lax.broadcasted_iota(jnp.int32, (256, 256), 1), 1.0, 0.0
    ).astype(BF)
    for j, p in enumerate((p0, p1, p2, p3)):
        q = info[0] ^ j
        for n in range(2 * N_SHARD):
            start = pl.multiple_of(n * FF_OWN + q * FF_PART, 16)
            stack[pl.ds(start, FF_PART)] = p[n * FF_PART : (n + 1) * FF_PART]
    for n in range(11):
        fin[:, n * 512 : (n + 1) * 512] = dot(unit, stack[n * 512 : (n + 1) * 512], NT)


def fin_out(info, pieces):
    return run(
        fin_out_kernel,
        sds((256, 8 * FF_OWN), F32),
        (info,),
        tuple(pieces),
        in_specs=[full(2 * FF_OWN, 256)] * 4,
        out_specs=full(256, 8 * FF_OWN),
        scratch=[pltpu.VMEM((8 * FF_OWN, 256), BF)],
        mib=24,
        flops=1 << 30,
        nbytes=9 << 20,
    )


def down_out_kernel(info, p0, p1, p2, p3, down):
    for j, p in enumerate((p0, p1, p2, p3)):
        rows = pl.ds(pl.multiple_of((info[0] ^ j) * FF_PART, 16), FF_PART)
        for c in range(4):
            down[rows, c * 256 : (c + 1) * 256] = p[c * FF_PART : (c + 1) * FF_PART].astype(F32)


def down_out(info, pieces):
    return run(
        down_out_kernel,
        sds((FF_OWN, WIDTH), F32),
        (info,),
        tuple(pieces),
        in_specs=[full(*p.shape) for p in pieces],
        out_specs=full(FF_OWN, WIDTH),
        nbytes=5 << 20,
    )


def last_out_kernel(info, q0, q1, q2, q3, d0, d1, d2, d3, o0, o1, o2, o3, g_q, g_k, g_v, g_u, g_out):
    for j, (p, d, o) in enumerate(zip((q0, q1, q2, q3), (d0, d1, d2, d3), (o0, o1, o2, o3))):
        at = pl.ds(pl.multiple_of((info[0] ^ j) * 256, 256), 256)
        for t, out in enumerate((g_q, g_k, g_v)):
            out[:, at] = p[t * 256 : (t + 1) * 256].astype(F32)
        g_u[:, at] = d[FF_OWN + 256 :].astype(F32)
        g_out[:, lanes(j, info)] = o[...].astype(F32)


def last_out(info, pieces):
    return run(
        last_out_kernel,
        (sds((256, WIDTH), F32),) * 5,
        (info,),
        tuple(pieces),
        in_specs=[full(*p.shape) for p in pieces],
        out_specs=[full(256, WIDTH)] * 5,
    )


def finish_kernel(x, gh, here, got, enter, out):
    gn = here[...] + got[...].astype(F32)
    grad = (gh[...] + rms_back(x[0].astype(F32), gn)).astype(BF)
    out[...] = dot(enter[0], grad, TN).astype(BF)


def result_kernel(x, att, here, got, enter, out):
    result = (x[0].astype(F32) + att[0].astype(F32) + here[...] + got[...].astype(F32)).astype(BF)
    out[...] = dot(enter[0], result, TN).astype(BF)


def finish(kernel, x, second, here, got, enter):
    first = lambda v: pl.BlockSpec((1, *v.shape[1:]), lambda _: (0,) * v.ndim) if v.ndim == 3 else full(*v.shape)
    args = (x, second, here, got, enter)
    return run(
        kernel,
        sds((ROWS, WIDTH)),
        (),
        args,
        in_specs=[first(v) for v in args],
        out_specs=full(ROWS, WIDTH),
        flops=1 << 28,
        nbytes=4 << 20,
    )


def unsort_kernel(leave, rows, out):
    out[...] = dot(leave[...], rows[...], TN).astype(BF)


def unsort(leave, rows):
    return run(
        unsort_kernel,
        sds((ROWS, WIDTH)),
        (),
        (leave, rows),
        in_specs=[full(ROWS, ROWS), full(ROWS, WIDTH)],
        out_specs=full(ROWS, WIDTH),
        flops=1 << 28,
        nbytes=2 << 20,
    )


def exchange(rows):
    return lax.all_to_all(rows, ALL, split_axis=0, concat_axis=0, tiled=True)


def team_raw(own):
    pair = send(own, "zl", 1)
    return [own, pair, send(own, "core", 1), send(pair, "core", 1)]


def team_sum(keep, give, hold=()):
    got = send(give, "core", 1)
    half = (keep.astype(F32) + got.astype(F32)).astype(BF)
    other = send(half, "zl", 1)
    if hold:
        other = after(other, *hold)
    ours = (half.astype(F32) + other[::-1].astype(F32)).astype(BF)
    return ours, send(ours, "core", 1), half


def team_own(keep, give, *behind):
    there = keep[1].astype(F32) + send(give[1], "core", 1).astype(F32)
    here = keep[0].astype(F32) + send(give[0], "core", 1).astype(F32)
    there = there.astype(BF)
    if behind:
        there = after(there, *behind)
    return here, send(there, "zl", 1)


def state_in(state, near, whole, cross, hold=()):
    low = [state] + [lax.ppermute(state, "shard", [(i, i ^ j) for i in range(4)]) for j in (1, 2, 3)]
    wide = [v.astype(F32) for v in low]
    hand = sum(whole[j][:, None, None] * wide[j] for j in range(4))
    if hold:
        hand = after(hand, *hold)
    got = send(hand, "zh", 1)
    here = sum(near[j][:, None, None] * wide[j] for j in (1, 2, 3))
    return here + cross[:, None, None] * got, hand


def fast_body(tokens_in, cotangent, deal_order, lengths, decay_rates, w_query, w_key, w_value, w_ugate, w_out, w_ffin, w_ffdown):
    zh, zl, core, shard = (lax.axis_index(a) for a in ALL)
    me = zl * 2 + core
    group = zh * N_SHARD + shard
    device = (zh * TEAM + me) * N_SHARD + shard
    span = TEAM * ROWS
    info = jnp.stack([me, shard, group * span, device, zh, jnp.int32(0), jnp.int32(0), jnp.int32(0)]).astype(jnp.int32)
    ends = jnp.sum(jnp.where(jnp.arange(8)[None, :] <= jnp.arange(8)[:, None], lengths[None, :], 0), axis=1).astype(jnp.int32)
    scal = (info, ends, decay_rates)
    by_device = deal_order.reshape(2, N_SHARD, TEAM, ROWS).transpose(0, 2, 1, 3).reshape(DEVICES, ROWS)

    leave, enter, sent_x, sent_g = exchange_rows(info, by_device, *far(tokens_in, cotangent))
    raw_x = exchange(sent_x)
    quarter = take_quarter(after(info, sent_x), *far(w_query, w_key, w_value, w_ugate))
    w_proj = gather_pieces(quarter)
    bundle = ff_bundle(after(info, quarter), *far(w_ffin, w_ffdown))
    w_ff = lax.all_gather(after(bundle, raw_x), "shard", axis=0)
    wo = gather_out(w_out, me, shard)
    x_raws = team_raw(raw_x)
    g_raws = team_raw(exchange(after(sent_g, raw_x)))

    rates = lax.dynamic_slice_in_dim(decay_rates, me * HEADS_OWN, HEADS_OWN)

    def seg_at(p):
        seg = jnp.sum((p[..., None] >= ends).astype(jnp.int32), axis=-1)
        return jnp.where(p < 0, -1, seg)

    def weigh(flag, gap):
        return jnp.where(flag[..., None], jnp.exp(-(jnp.maximum(gap, 0) * span).astype(F32)[..., None] * rates), 0.0)

    peers = zh * N_SHARD + (shard ^ jnp.arange(4))
    peers_last, peers_before = seg_at((peers + 1) * span - 1), seg_at(peers * span - 1)
    my_last, my_before = peers_last[0], peers_before[0]
    end, start = zh * N_SHARD + 3, zh * N_SHARD
    f_near = weigh((peers < group) & (peers_last == my_before), group - 1 - peers)
    f_whole = weigh(peers_last == seg_at((end + 1) * span - 1), end - peers)
    f_cross = weigh((zh == 1) & (seg_at(start * span - 1) == my_before), shard)
    b_near = weigh((peers > group) & (peers_before == my_last), peers - 1 - group)
    b_whole = weigh(peers_before == seg_at(start * span - 1), peers - start)
    b_cross = weigh((zh == 0) & (seg_at((end + 1) * span - 1) == my_last), 3 - shard)

    x, normed, pq, pk, pu, q, k, v, kv, state = project(scal, enter, far(*x_raws), far(*w_proj))
    s_in, _ = state_in(state, f_near, f_whole, f_cross)
    local = attend_local(scal, q, k, v)
    mixed, gated, a_keep, a_give = carry_in((after(info, g_raws[1]), *scal[1:]), local, q, pu, kv, s_in, wo)
    ta, tb, _ = team_sum(a_keep, a_give, hold=(g_raws[2], g_raws[3]))
    g, n2, product, gg, gu, r_keep, r_give, n_keep, n_give = sglu(info, *far(enter), x, ta, *far(tb), far(*g_raws), *far(w_ff))
    n_got = send(n_give, "core", 1)
    d_gate = hidden_grads(info, n2, gg, 1)
    n_half = (n_keep.astype(F32) + n_got.astype(F32)).astype(BF)
    n_other = send(n_half, "zl", 1)
    d_up = hidden_grads(after(info, n_half), n2, gu, 2)
    d_down = down_grads(after(info, d_up[1]), g, product, 1)
    gate_own, gate_other = hop(d_gate, 1, hold=(d_down[1],))
    n_other = after(n_other, d_down[1], gate_other)
    ua = (n_half.astype(F32) + n_other[::-1].astype(F32)).astype(BF)
    ub = send(ua, "core", 1)
    up_own, up_other = hop(d_up, 2, hold=(ua,))

    ga, gpu, gm, qg, gh, g_state = hidden_back(
        (after(info, up_other), *scal[1:]), x, ta, *far(tb), ua, *far(ub), g, wo, mixed, pu, q
    )
    gate = hop_two(gate_own, gate_other, 1)
    up = hop_two(up_own, up_other, 2)
    gq, gk, gv = scores_back(scal, q, k, v, gm, kv, s_in)
    r_here, r_there = team_own(r_keep, r_give, ua)
    g_in, handed = state_in(g_state, b_near, b_whole, b_cross, hold=(r_there,))
    d_ou = column_grads(after(info, handed), [(gated, ga), (normed, gpu)], 2)
    fin = joined((gate, up), hold=(d_ou[1],))
    dqkv, p_keep, p_give = project_back(
        (after(info, fin), *scal[1:]), gq, gk, gv, pq, pk, k, v, gpu, qg, g_in, far(*w_proj)
    )
    here, there = team_own(p_keep, p_give)
    d_qkv = column_grads(info, [(normed, dqkv)], 1)
    last_sent = finish(finish_kernel, x, gh, here, there, after(enter, d_qkv[1]))
    input_grad = unsort(leave, exchange(last_sent))
    output = unsort(leave, exchange(finish(result_kernel, x, ta, r_here, r_there, after(enter, last_sent))))

    down_own, down_other = hop(d_down, 1, hold=(last_sent,), hold_send=(handed,))
    ou_own, ou_other = hop(d_ou, 2, hold=(down_other,))
    fin_sum = over_zh(fin, hold=(ou_other,))
    fin_pair = send(fin_sum, "zl", 1)
    down_ou = joined((hop_two(down_own, down_other, 1), hop_two(ou_own, ou_other, 2)), hold=(fin_sum,))
    qkv_own, qkv_other = hop(d_qkv, 1, hold=(last_sent,))
    qkv = joined((hop_two(qkv_own, qkv_other, 1),))
    down_sum = over_zh(down_ou, hold=(fin_pair, input_grad))
    down_pair = send(down_sum, "zl", 1)
    fin_all = [fin_sum, send(fin_sum, "core", 1), fin_pair, send(fin_pair, "core", 1)]
    down_all = [down_sum, send(down_sum, "core", 1), down_pair, send(down_pair, "core", 1)]
    grad_fin = fin_out(info, far(*fin_all))
    grad_down = down_out(info, far(*down_all))
    outs = []
    for j in range(4):
        pick = me ^ shard ^ j
        top = [p[FF_OWN : FF_OWN + 256] for p in down_all]
        piece = jnp.where(pick < 2, jnp.where(pick == 0, top[0], top[1]), jnp.where(pick == 2, top[2], top[3]))
        outs.append(piece if j == 0 else send(piece, "shard", j))
    qkv_sum = over_zh(qkv, hold=(down_pair, output, grad_fin))
    qkv_pair = send(qkv_sum, "zl", 1)
    qkv_late = after(qkv_pair, grad_down, *outs[1:])
    qkv_all = [qkv_sum, send(qkv_sum, "core", 1), qkv_late, send(qkv_late, "core", 1)]
    grad_q, grad_k, grad_v, grad_u, grad_out = last_out(info, far(*qkv_all, *down_all, *outs))
    return (output, input_grad, grad_q, grad_k, grad_v, grad_u, grad_out, grad_fin, grad_down)


def solution(mesh):
    rep, shard = mesh.shape["rep"], mesh.shape["shard"]
    team = Mesh(mesh.devices.reshape(rep // TEAM, 2, 2, shard), ALL)
    token, weight = P(ALL, None), P("shard", None)
    return jax.shard_map(
        fast_body if (rep, shard) == (8, 4) else general_body,
        mesh=team,
        in_specs=(token, token, P(), P(), P(), *([weight] * 7)),
        out_specs=(token, token, *([weight] * 7)),
        check_vma=False,
    )
```

```python
import functools

import jax
import jax.numpy as jnp
from jax import lax
from jax.experimental import pallas as pl
from jax.experimental.pallas import tpu as pltpu
from jax.sharding import Mesh, PartitionSpec as P

HEAD = 128
BLOCK = 256
TEAM = 4
EPS = 1e-06
BF = jnp.bfloat16
F32 = jnp.float32
ALL = ("zh", "zl", "core", "shard")


def send(value, axis, mask):
    size = lax.axis_size(axis)
    return lax.ppermute(value, axis, [(i, i ^ mask) for i in range(size)])


def dot(a, b, dims=((1,), (0,))):
    return lax.dot_general(a, b, (dims, ((), ())), preferred_element_type=F32)


def norm_scale(values):
    return lax.rsqrt(jnp.mean(values * values, axis=-1, keepdims=True) + EPS)


def norm_back(values, grad):
    scale = norm_scale(values)
    return scale * grad - values * (scale**3) * jnp.mean(values * grad, axis=-1, keepdims=True)


def in_order(pieces, index):
    pieces = list(pieces)
    bit = 1
    while bit < len(pieces):
        flip = (index & bit) != 0
        pieces = [jnp.where(flip, pieces[j ^ bit], pieces[j]) for j in range(len(pieces))]
        bit *= 2
    return pieces


def gather_shard(part):
    size = lax.axis_size("shard")
    if size != 4:
        every = lax.all_gather(part, "shard", axis=0)
        return [every[j] for j in range(size)]
    half = part.shape[0] // 2
    by_x, by_y = send(part, "shard", 1), send(part, "shard", 2)
    far = jnp.concatenate([send(by_x[:half], "shard", 2), send(by_y[half:], "shard", 1)], 0)
    return in_order([part, by_x, by_y, far], lax.axis_index("shard"))


def scatter_shard(parts):
    size = lax.axis_size("shard")
    if size != 4:
        return lax.psum_scatter(jnp.stack(parts), "shard", scatter_dimension=0, tiled=False)
    rel = in_order(parts, lax.axis_index("shard"))
    total = rel[0].astype(F32)
    for j in (1, 2, 3):
        total = total + send(rel[j].astype(BF), "shard", j).astype(F32)
    return total


def sum_zh(part):
    size = lax.axis_size("zh")
    part = part.astype(BF)
    if size != 2:
        return lax.psum(part.astype(F32), "zh").astype(BF)
    return (part.astype(F32) + send(part, "zh", 1).astype(F32)).astype(BF)


def team_gather(own):
    pair = send(own, "zl", 1)
    return [own, send(own, "core", 1), pair, send(pair, "core", 1)]


def team_reduce(parts):
    low = [p.astype(BF) for p in parts]
    here = parts[0] + send(low[1], "core", 1).astype(F32)
    there = parts[2] + send(low[3], "core", 1).astype(F32)
    return here + send(there.astype(BF), "zl", 1).astype(F32)


def place_mix(state, weights):
    groups = lax.axis_size("zh") * lax.axis_size("shard")
    mine = lax.axis_index("zh") * lax.axis_size("shard") + lax.axis_index("shard")
    low = state.astype(BF)
    if groups != 8:
        every = lax.all_gather(low, ("zh", "shard"), axis=0).astype(F32)
        return jnp.sum(every * weights[:, :, None, None], axis=0)
    total = jnp.zeros_like(state)
    for j in range(1, groups):
        got = lax.ppermute(low, ("zh", "shard"), [(i, i ^ j) for i in range(groups)])
        factor = lax.dynamic_index_in_dim(weights, mine ^ j, 0, keepdims=False)
        total = total + factor[:, None, None] * got.astype(F32)
    return total


def after(value, *others):
    return lax.optimization_barrier((value, *others))[0]


def general_body(tokens_in, cotangent, deal_order, lengths, decay_rates, w_query, w_key, w_value, w_ugate, w_out, w_ffin, w_ffdown):
    rows, width = tokens_in.shape
    n_zh, n_shard = lax.axis_size("zh"), lax.axis_size("shard")
    groups = n_zh * n_shard
    devices = groups * TEAM
    zh, zl, core, shard = (lax.axis_index(a) for a in ALL)
    me = zl * 2 + core
    group = zh * n_shard + shard
    device = (zh * TEAM + me) * n_shard + shard
    heads = width // HEAD // TEAM
    cols = heads * HEAD
    depth = w_query.shape[0]
    ff = w_ffin.shape[1] // 2
    ff_shard = w_ffdown.shape[0]
    ff_own = ff_shard // TEAM
    per_peer = rows // devices
    span = rows * TEAM

    by_device = deal_order.reshape(n_zh, n_shard, TEAM, rows).transpose(0, 2, 1, 3).reshape(-1)
    row_ids = jnp.arange(rows, dtype=jnp.int32)
    key = jnp.sum(
        jnp.where(
            by_device[:, None] == device * rows + row_ids[None, :],
            jnp.arange(by_device.shape[0], dtype=jnp.int32)[:, None],
            0,
        ),
        axis=0,
    )
    rank = jnp.sum((key[:, None] < key[None, :]).astype(jnp.int32), axis=0)
    leave = (row_ids[:, None] == rank[None, :]).astype(BF)
    sent_x = dot(leave, tokens_in).astype(BF)
    sent_g = dot(leave, cotangent).astype(BF)
    got_x = lax.all_to_all(sent_x, ALL, split_axis=0, concat_axis=0, tiled=True)
    own_block = lax.dynamic_slice_in_dim(by_device, device * rows, rows)
    source = own_block // rows
    earlier = row_ids[None, :] < row_ids[:, None]
    own_rank = jnp.sum(((source[:, None] == source[None, :]) & earlier).astype(jnp.int32), axis=1)
    slot = source * per_peer + own_rank
    enter = (slot[:, None] == row_ids[None, :]).astype(BF)
    x_own = dot(enter, got_x).astype(BF)
    got_g = lax.all_to_all(after(sent_g, got_x), ALL, split_axis=0, concat_axis=0, tiled=True)
    g_own = dot(enter, got_g).astype(BF)

    def quarter(w):
        return lax.dynamic_slice_in_dim(w, me * cols, cols, axis=1)

    qkvu_part = jnp.concatenate([quarter(w) for w in (w_query, w_key, w_value, w_ugate)], 1)
    w_qkvu = jnp.concatenate(gather_shard(qkvu_part), 0)
    out_all = jnp.concatenate(gather_shard(after(w_out, w_qkvu)), 0)
    w_o = lax.dynamic_slice_in_dim(out_all, me * cols, cols)
    fin = w_ffin.reshape(depth, 2, n_shard, TEAM, ff_own)
    fin = lax.dynamic_index_in_dim(fin, me, 3, keepdims=False)
    fin = fin.transpose(1, 0, 2, 3).reshape(2 * depth, n_shard * ff_own)
    fin_parts = gather_shard(after(fin, out_all))
    w_gate = jnp.concatenate([p[:depth] for p in fin_parts], 0)
    w_up = jnp.concatenate([p[depth:] for p in fin_parts], 0)
    fdown = lax.dynamic_slice_in_dim(w_ffdown, me * ff_own, ff_own)
    w_down = jnp.concatenate(gather_shard(after(fdown, w_up)), 0)

    ends = jnp.sum(jnp.where(jnp.arange(8)[None, :] <= jnp.arange(8)[:, None], lengths[None, :], 0), axis=1)
    all_last = jnp.arange(1, groups + 1) * span - 1
    last_seg = jnp.sum((all_last[:, None] >= ends[None, :]).astype(jnp.int32), axis=1)
    before_seg = jnp.concatenate([jnp.full((1,), -1, jnp.int32), last_seg[:-1]])
    positions = group * span + jnp.arange(span)
    seg = jnp.sum((positions[:, None] >= ends[None, :]).astype(jnp.int32), axis=1)
    seg_before = before_seg[group]
    blocks = span // BLOCK
    seg_b = seg.reshape(blocks, BLOCK)
    prev_b = jnp.concatenate([seg_before[None], seg_b[:-1, -1]])
    rates = lax.dynamic_slice_in_dim(decay_rates, me * heads, heads)
    idx = jnp.arange(BLOCK).astype(F32)
    dist = idx[:, None] - idx[None, :]
    decay = jnp.where(dist >= 0, jnp.exp(-rates[:, None, None] * jnp.maximum(dist, 0.0)), 0.0)
    same = (seg_b[:, :, None] == seg_b[:, None, :]).astype(F32)
    mask = same[:, None] * decay[None]
    carry = (seg_b == prev_b[:, None]).astype(F32)
    q_scale = jnp.exp(-(idx + 1.0)[None, :, None] * rates) * carry[:, :, None]
    k_scale = jnp.exp(-(BLOCK - 1.0 - idx)[None, :, None] * rates) * (seg_b == seg_b[:, -1:]).astype(F32)[:, :, None]
    passing = (seg_b[:, -1] == prev_b).astype(F32)[:, None] * jnp.exp(-rates * BLOCK)[None]
    ids = jnp.arange(groups)
    gap = jnp.maximum(jnp.abs(ids - group) - 1, 0).astype(F32) * span
    into = (ids < group) & (last_seg == seg_before)
    outof = (ids > group) & (before_seg == last_seg[group])
    fade = jnp.exp(-gap[:, None] * rates[None, :])
    w_into = jnp.where(into[:, None], fade, 0.0)
    w_outof = jnp.where(outof[:, None], fade, 0.0)

    x = in_order(team_gather(x_own), me)
    x_all = jnp.concatenate(x, 0)
    xf = x_all.astype(F32)
    normed = (xf * norm_scale(xf)).astype(BF)
    pre = dot(normed, w_qkvu)
    pre_q, pre_k, pre_v, pre_u = (pre[:, i * cols : (i + 1) * cols] for i in range(4))
    shape = (blocks, BLOCK, heads, HEAD)
    q = jax.nn.silu(pre_q).astype(BF).reshape(shape)
    k = jax.nn.silu(pre_k).astype(BF).reshape(shape)
    v = pre_v.astype(BF).reshape(shape)

    def ein(text, a, b):
        return jnp.einsum(text, a, b, preferred_element_type=F32)

    ks = (k.astype(F32) * k_scale[..., None]).astype(BF)
    qs = (q.astype(F32) * q_scale[..., None]).astype(BF)
    kv = ein("bjhe,bjhf->bhef", ks, v)
    state = jnp.zeros((heads, HEAD, HEAD), F32)
    for b in range(blocks):
        state = passing[b][:, None, None] * state + kv[b]
    state_in = place_mix(state, w_into)
    scores = ein("bihe,bjhe->bhij", q, k)
    mixing = (scores * mask).astype(BF)
    mixed = ein("bhij,bjhf->bihf", mixing, v)
    states = []
    state = state_in
    for b in range(blocks):
        states.append(state)
        state = passing[b][:, None, None] * state + kv[b]
    states = jnp.stack(states).astype(BF)
    mixed = mixed + ein("bihe,bhef->bihf", qs, states)
    m_norm = (mixed * norm_scale(mixed)).reshape(span, cols)
    gated = (pre_u * m_norm).astype(BF)
    part = dot(gated, w_o).reshape(TEAM, rows, width)
    att = team_reduce(in_order([part[j] for j in range(TEAM)], me))
    att = jnp.concatenate(in_order(team_gather(att.astype(BF)), me), 0)
    hidden = xf + att.astype(F32)

    g_all = jnp.concatenate(in_order(team_gather(g_own), me), 0)
    n2 = (hidden * norm_scale(hidden)).astype(BF)
    gate, up = dot(n2, w_gate), dot(n2, w_up)
    product = (gate * up).astype(BF)
    res = dot(product, w_down).reshape(TEAM, rows, width)
    g_product = dot(g_all, w_down, ((1,), (1,)))
    g_gate, g_up = (g_product * up).astype(BF), (g_product * gate).astype(BF)
    gn2 = dot(g_gate, w_gate, ((1,), (1,))) + dot(g_up, w_up, ((1,), (1,)))
    gn2 = gn2.reshape(TEAM, rows, width)
    gn2 = team_reduce(in_order([gn2[j] for j in range(TEAM)], me))
    gn2 = jnp.concatenate(in_order(team_gather(gn2.astype(BF)), me), 0)
    g_hidden = g_all.astype(F32) + norm_back(hidden, gn2.astype(F32))
    ga = g_hidden.astype(BF)

    res = team_reduce(in_order([res[j] for j in range(TEAM)], me))
    my_rows = lambda a: lax.dynamic_slice_in_dim(a, me * rows, rows)
    result = (my_rows(hidden) + res).astype(BF)

    g_gated = dot(ga, w_o, ((1,), (1,)))
    g_pre_u = (g_gated * m_norm).astype(BF)
    gm = norm_back(mixed, (g_gated * pre_u).reshape(shape)).astype(BF)
    qg = ein("bihe,bihf->bhef", qs, gm)
    gs = jnp.zeros((heads, HEAD, HEAD), F32)
    for b in reversed(range(blocks)):
        gs = passing[b][:, None, None] * gs + qg[b]
    gs = place_mix(gs, w_outof)
    g_states = [None] * blocks
    for b in reversed(range(blocks)):
        g_states[b] = gs
        gs = passing[b][:, None, None] * gs + qg[b]
    g_states = jnp.stack(g_states).astype(BF)
    g_mixing = ein("bihf,bjhf->bhij", gm, v)
    g_scores = (g_mixing * mask).astype(BF)
    g_q = ein("bhij,bjhe->bihe", g_scores, k) + q_scale[..., None] * ein("bihf,bhef->bihe", gm, states)
    g_k = ein("bhij,bihe->bjhe", g_scores, q) + k_scale[..., None] * ein("bhef,bjhf->bjhe", g_states, v)
    g_v = ein("bhij,bihf->bjhf", mixing, gm) + ein("bjhe,bhef->bjhf", ks, g_states)

    def silu_back(pre_rows, grad):
        sig = jax.nn.sigmoid(pre_rows)
        return (grad * (sig * (1.0 + pre_rows * (1.0 - sig)))).astype(BF)

    g_pre = jnp.concatenate(
        [
            silu_back(pre_q, g_q.reshape(span, cols)),
            silu_back(pre_k, g_k.reshape(span, cols)),
            g_v.reshape(span, cols).astype(BF),
            g_pre_u,
        ],
        1,
    )
    gn = dot(g_pre, w_qkvu, ((1,), (1,))).reshape(TEAM, rows, width)
    gn = team_reduce(in_order([gn[j] for j in range(TEAM)], me))
    grad_x = (my_rows(g_hidden) + norm_back(x_own.astype(F32), gn)).astype(BF)

    def give_back(rows_own):
        ordered = dot(enter, rows_own, ((0,), (0,))).astype(BF)
        back = lax.all_to_all(ordered, ALL, split_axis=0, concat_axis=0, tiled=True)
        return dot(leave, back, ((0,), (0,))).astype(BF)

    output, input_grad = give_back(result), give_back(grad_x)

    def by_place(grad):
        return list(grad.astype(BF).reshape(n_shard, -1, grad.shape[-1]))

    d_down = dot(product, g_all, ((0,), (0,)))
    d_gate, d_up = dot(n2, g_gate, ((0,), (0,))), dot(n2, g_up, ((0,), (0,)))
    d_out = dot(gated, ga, ((0,), (0,)))
    d_qkvu = dot(normed, g_pre, ((0,), (0,)))

    def collect(parts):
        return in_order(team_gather(sum_zh(scatter_shard(parts))), me)

    down = collect(by_place(d_down))
    grad_down = jnp.concatenate(down, 0).astype(F32)
    fin_grad = [jnp.concatenate([a, b], 0) for a, b in zip(by_place(d_gate), by_place(d_up))]
    fin_grad = jnp.stack(collect(fin_grad), 0).reshape(TEAM, 2, depth, n_shard, ff_own)
    grad_fin = fin_grad.transpose(2, 1, 3, 0, 4).reshape(depth, 2 * ff).astype(F32)
    out_cols = width // n_shard
    d_out_cols = [d_out[:, j * out_cols : (j + 1) * out_cols].astype(BF) for j in range(n_shard)]
    d_out_rows = jnp.concatenate(collect(d_out_cols), 0)
    d_out_rows = lax.all_to_all(
        d_out_rows.reshape(n_shard, depth, out_cols), "shard", split_axis=0, concat_axis=0, tiled=True
    )
    grad_out = d_out_rows.transpose(1, 0, 2).reshape(depth, width).astype(F32)
    qkvu = collect(by_place(d_qkvu))
    grads = [
        jnp.concatenate([p[:, i * cols : (i + 1) * cols] for p in qkvu], 1).astype(F32) for i in range(4)
    ]
    return (output, input_grad, *grads, grad_out, grad_fin, grad_down)


N_SHARD = 4
ROWS = 256
WIDTH = 1024
COLS = 256
HEADS_OWN = 2
FF_PART = 176
FF_OWN = 704
SLOTS = 8
DEVICES = 32
TN = ((0,), (0,))
NT = ((1,), (1,))
NN = ((1,), (0,))
GLOBAL = pl.BlockSpec(memory_space=pltpu.VMEM)


def far(*values):
    return tuple(pltpu.with_memory_space_constraint(v, pltpu.HBM) for v in values)


def rel_of(i):
    return (i & 1) * 2 + (i >> 1)


def hbm(shape, dtype=BF):
    return pltpu.HBM(shape, dtype)


def sds(shape, dtype=BF):
    return jax.ShapeDtypeStruct(shape, dtype)


def run(kernel, out, prefetch, args, grid=None, in_specs=None, out_specs=None, scratch=(), mib=16, flops=0, nbytes=0):
    return pl.pallas_call(
        kernel,
        out_shape=out,
        grid_spec=pltpu.PrefetchScalarGridSpec(
            num_scalar_prefetch=len(prefetch),
            grid=grid or (1,),
            in_specs=in_specs,
            out_specs=out_specs,
            scratch_shapes=list(scratch),
        ),
        compiler_params=pltpu.CompilerParams(
            vmem_limit_bytes=mib << 20, dimension_semantics=("arbitrary",) * len(grid or (1,))
        ),
        cost_estimate=pl.CostEstimate(flops=0, bytes_accessed=0, transcendentals=0),
    )(*prefetch, *args)


def full(*shape):
    return pl.BlockSpec(shape, lambda *_: (0,) * len(shape))


def place(info, j):
    return info[1] ^ j


def block_abs(i, info):
    return info[0] ^ rel_of(i)


def seg_scalar(p, ends):
    total = jnp.int32(0)
    for n in range(8):
        total = total + jnp.where(p >= ends[n], 1, 0)
    return jnp.where(p < 0, -1, total)


def seg_vector(base, shape, dim, ends):
    p = base + lax.broadcasted_iota(jnp.int32, shape, dim)
    total = jnp.zeros(shape, jnp.int32)
    for n in range(8):
        total = total + jnp.where(p >= ends[n], 1, 0)
    return total


def scales(a, info, ends, rates, h):
    base = info[2] + a * BLOCK
    prev = seg_scalar(base - 1, ends)
    last = seg_scalar(base + BLOCK - 1, ends)
    seg = seg_vector(base, (BLOCK, HEAD), 0, ends)
    idx = lax.broadcasted_iota(jnp.int32, (BLOCK, HEAD), 0).astype(F32)
    r = rates[info[0] * HEADS_OWN + h]
    q_scale = jnp.where(seg == prev, jnp.exp(-(idx + 1.0) * r), 0.0)
    k_scale = jnp.where(seg == last, jnp.exp(-(BLOCK - 1.0 - idx) * r), 0.0)
    return q_scale, k_scale, passing(a, info, ends, rates, h)


def passing(a, info, ends, rates, h):
    base = info[2] + a * BLOCK
    same = seg_scalar(base - 1, ends) == seg_scalar(base + BLOCK - 1, ends)
    r = rates[info[0] * HEADS_OWN + h]
    return jnp.exp(jnp.full((1, HEAD), -float(BLOCK), F32) * r) * jnp.where(same, 1.0, 0.0)


def decay_masks(info, rates, out):
    dist = lax.broadcasted_iota(jnp.int32, (BLOCK, BLOCK), 0) - lax.broadcasted_iota(jnp.int32, (BLOCK, BLOCK), 1)
    away = jnp.maximum(dist, 0).astype(F32)
    for h in range(HEADS_OWN):
        r = rates[info[0] * HEADS_OWN + h]
        out[h] = jnp.where(dist >= 0, jnp.exp(-away * r), 0.0)


def same_seg(a, info, ends):
    base = info[2] + a * BLOCK
    return seg_vector(base, (BLOCK, 1), 0, ends) == seg_vector(base, (1, BLOCK), 1, ends)


def rms(v):
    return v * lax.rsqrt(jnp.mean(v * v, axis=-1, keepdims=True) + EPS)


def rms_back(v, g):
    s = lax.rsqrt(jnp.mean(v * v, axis=-1, keepdims=True) + EPS)
    return s * g - v * ((s * s * s) * jnp.mean(v * g, axis=-1, keepdims=True))


def lanes(j, info):
    return pl.ds(pl.multiple_of(place(info, j) * 256, 256), 256)


def rows_kernel(info, deal, tok, cot, leave, enter, sent_x, sent_g):
    dev = info[3]
    d = deal[...]
    owner = lax.shift_right_logical(d, 8)
    mine = owner == dev
    r_i = lax.broadcasted_iota(jnp.int32, (ROWS, ROWS), 0)
    c_i = lax.broadcasted_iota(jnp.int32, (ROWS, ROWS), 1)
    upper = jnp.where(r_i < c_i, 1.0, 0.0).astype(BF)
    count = dot(jnp.where(mine, 1.0, 0.0).astype(BF), upper)
    local = (d - dev * ROWS).astype(F32)
    lane8 = lax.broadcasted_iota(jnp.int32, (DEVICES, 128), 1)
    picked = jnp.zeros((DEVICES, 128), F32)
    for slot in range(SLOTS):
        row = jnp.sum(jnp.where(mine & (count == float(slot)), local, 0.0), axis=1, keepdims=True)
        picked = jnp.where(lane8 == slot, row, picked)
    k_r = lax.broadcasted_iota(jnp.int32, (ROWS, DEVICES), 0)
    k_c = lax.broadcasted_iota(jnp.int32, (ROWS, DEVICES), 1)
    spread = jnp.where(lax.shift_right_logical(k_r, 3) == k_c, 1.0, 0.0).astype(BF)
    wide = dot(spread, picked.astype(BF))
    k8 = lax.broadcasted_iota(jnp.int32, (ROWS, 128), 0) & 7
    l8 = lax.broadcasted_iota(jnp.int32, (ROWS, 128), 1)
    column = jnp.sum(jnp.where(k8 == l8, wide, 0.0), axis=1, keepdims=True)
    lv = jnp.where(column == c_i.astype(F32), 1.0, 0.0).astype(BF)
    leave[...] = lv
    sent_x[...] = dot(lv, tok[...]).astype(BF)
    sent_g[...] = dot(lv, cot[...]).astype(BF)
    for i in range(TEAM):
        a = info[0] ^ rel_of(i)
        at = (info[4] * TEAM + a) * N_SHARD + info[1]
        src = lax.shift_right_logical(deal[pl.ds(at, 1), :], 8)
        src_f = src.astype(F32)
        src_col = jnp.sum(jnp.where(r_i == c_i, src_f, 0.0), axis=1, keepdims=True)
        alike = jnp.where((src_col == src_f) & (c_i < r_i), 1.0, 0.0)
        rank = jnp.sum(alike, axis=1, keepdims=True)
        slot = src_col * float(SLOTS) + rank
        enter[i] = jnp.where(slot == c_i.astype(F32), 1.0, 0.0).astype(BF)


def exchange_rows(info, by_device, tokens_in, cotangent):
    return run(
        rows_kernel,
        (sds((ROWS, ROWS)), sds((TEAM, ROWS, ROWS)), sds((ROWS, WIDTH)), sds((ROWS, WIDTH))),
        (info,),
        (by_device, tokens_in, cotangent),
        in_specs=[full(DEVICES, ROWS), full(ROWS, WIDTH), full(ROWS, WIDTH)],
        out_specs=[full(ROWS, ROWS), full(TEAM, ROWS, ROWS), full(ROWS, WIDTH), full(ROWS, WIDTH)],
        flops=4 << 28,
        nbytes=3 << 20,
    )


def quarter_kernel(info, wq, wk, wv, wu, out):
    for t, w in enumerate((wq, wk, wv, wu)):
        out[t * COLS : (t + 1) * COLS] = w[...]


def take_quarter(info, *weights):
    spec = pl.BlockSpec((256, COLS), lambda i, info: (0, info[0]))
    return run(
        quarter_kernel,
        sds((4 * COLS, COLS)),
        (info,),
        weights,
        in_specs=[spec] * 4,
        out_specs=full(4 * COLS, COLS),
        nbytes=1 << 20,
    )


def ff_bundle_kernel(info, fin, down, out, turned):
    me = info[0]
    unit = jnp.where(
        lax.broadcasted_iota(jnp.int32, (256, 256), 0) == lax.broadcasted_iota(jnp.int32, (256, 256), 1), 1.0, 0.0
    ).astype(BF)
    for n in range(11):
        turned[n * 512 : (n + 1) * 512] = dot(fin[:, n * 512 : (n + 1) * 512], unit, TN).astype(BF)
    for n in range(2 * N_SHARD):
        start = pl.multiple_of(n * FF_OWN + me * FF_PART, 16)
        out[n * FF_PART : (n + 1) * FF_PART] = turned[pl.ds(start, FF_PART)]
    for c in range(4):
        rows = pl.ds(pl.multiple_of(me * FF_PART, 16), FF_PART)
        at = 2 * FF_OWN + c * FF_PART
        out[at : at + FF_PART] = down[rows, c * 256 : (c + 1) * 256]


def ff_bundle(info, fin, down):
    return run(
        ff_bundle_kernel,
        sds((3 * FF_OWN, 256)),
        (info,),
        (fin, down),
        in_specs=[full(*fin.shape), full(*down.shape)],
        out_specs=full(3 * FF_OWN, 256),
        scratch=[pltpu.VMEM((8 * FF_OWN, 256), BF)],
        flops=1 << 30,
        nbytes=6 << 20,
    )


def gather_pieces(part):
    return [part] + [send(part, "shard", j) for j in (1, 2, 3)]


def gather_out(w_out, me, shard):
    axes = ("zl", "core", "shard")
    rel = me ^ shard
    wo = w_out
    for j in (1, 2, 3):
        pairs = [(m * N_SHARD + m, m * N_SHARD + (m ^ j)) for m in range(TEAM)]
        wo = jnp.where(rel == j, lax.ppermute(w_out, axes, pairs), wo)
    return wo


def weight_at(refs, j, t):
    return refs[j][t * 256 : (t + 1) * 256]


def project_kernel(info, ends, rates, enter, r0, r1, r2, r3, w0, w1, w2, w3,
                   x, normed, pq, pk, pu, q, k, v, kv, state, scr):
    i = pl.program_id(0)
    a = block_abs(i, info)
    for t, raw in enumerate((r0, r1, r2, r3)):

        @pl.when(i == t)
        def _():
            x[0] = dot(enter[0], raw[...]).astype(BF)

    scr[...] = rms(x[0].astype(F32)).astype(BF)
    normed[0] = scr[...]
    refs = (w0, w1, w2, w3)
    pre = []
    for t in range(4):
        total = dot(scr[:, lanes(0, info)], weight_at(refs, 0, t))
        for j in (1, 2, 3):
            total = total + dot(scr[:, lanes(j, info)], weight_at(refs, j, t))
        pre.append(total)
    pq[0], pk[0], pu[0] = pre[0], pre[1], pre[3]
    qb = (pre[0] * jax.nn.sigmoid(pre[0])).astype(BF)
    kb = (pre[1] * jax.nn.sigmoid(pre[1])).astype(BF)
    vb = pre[2].astype(BF)
    q[0], k[0], v[0] = qb, kb, vb
    for h in range(HEADS_OWN):
        at = slice(h * HEAD, (h + 1) * HEAD)
        _, k_scale, _ = scales(a, info, ends, rates, h)
        ks = (kb[:, at].astype(F32) * k_scale).astype(BF)
        kv[a, h] = dot(ks, vb[:, at], TN)

    @pl.when(i == TEAM - 1)
    def _():
        for h in range(HEADS_OWN):
            total = kv[0, h]
            for b in range(1, TEAM):
                total = passing(b, info, ends, rates, h) * total + kv[b, h]
            state[h] = total.astype(BF)


def project(scal, enter, raws, pieces):
    info = scal[0]
    by_abs = pl.BlockSpec((1, ROWS, COLS), lambda i, info, *_: (block_abs(i, info), 0, 0))
    by_abs_wide = pl.BlockSpec((1, ROWS, WIDTH), lambda i, info, *_: (block_abs(i, info), 0, 0))
    by_i = pl.BlockSpec((1, ROWS, ROWS), lambda i, *_: (i, 0, 0))
    by_i_wide = pl.BlockSpec((1, ROWS, WIDTH), lambda i, *_: (i, 0, 0))
    f32_block, bf_block = sds((TEAM, ROWS, COLS), F32), sds((TEAM, ROWS, COLS))
    return run(
        project_kernel,
        (
            hbm((TEAM, ROWS, WIDTH)), hbm((TEAM, ROWS, WIDTH)), hbm((TEAM, ROWS, COLS), F32), hbm((TEAM, ROWS, COLS), F32),
            f32_block, bf_block, bf_block,
            bf_block, sds((TEAM, HEADS_OWN, HEAD, HEAD), F32), sds((HEADS_OWN, HEAD, HEAD)),
        ),
        scal,
        (enter, *raws, *pieces),
        grid=(TEAM,),
        in_specs=[by_i, *[full(ROWS, WIDTH)] * 4, *[full(*p.shape) for p in pieces]],
        out_specs=[
            by_i_wide, by_abs_wide, *[by_abs] * 6, full(TEAM, HEADS_OWN, HEAD, HEAD), full(HEADS_OWN, HEAD, HEAD),
        ],
        scratch=[pltpu.VMEM((ROWS, WIDTH), BF)],
        flops=3 << 30,
        nbytes=14 << 20,
    )


def local_kernel(info, ends, rates, q, k, v, mixed, dec):
    b = pl.program_id(0)

    @pl.when(b == 0)
    def _():
        decay_masks(info, rates, dec)

    same = same_seg(b, info, ends)
    for h in range(HEADS_OWN):
        at = slice(h * HEAD, (h + 1) * HEAD)
        scores = dot(q[0, :, at], k[0, :, at], NT)
        mixing = jnp.where(same, scores * dec[h], 0.0).astype(BF)
        mixed[0, :, at] = dot(mixing, v[0, :, at])


BLOCK_SPEC = pl.BlockSpec((1, ROWS, COLS), lambda i, *_: (i, 0, 0))


def attend_local(scal, q, k, v):
    return run(
        local_kernel,
        sds((TEAM, ROWS, COLS), F32),
        scal,
        (q, k, v),
        grid=(TEAM,),
        in_specs=[BLOCK_SPEC] * 3,
        out_specs=BLOCK_SPEC,
        scratch=[pltpu.VMEM((HEADS_OWN, BLOCK, BLOCK), F32)],
        flops=1 << 28,
        nbytes=3 << 20,
    )


def run_states(start, step, out, info, ends, rates, order):
    for h in range(HEADS_OWN):
        now = start[h]
        for b in order:
            out[b, h] = now.astype(BF)
            now = passing(b, info, ends, rates, h) * now + step[b, h]


def halves(i, value, keep, give):
    @pl.when(i < 2)
    def _():
        keep[0] = value

    @pl.when(i >= 2)
    def _():
        give[0] = value


def carry_kernel(info, ends, rates, local, q, pu, kv, s_in, wo, mixed, gated, keep, give, states):
    i = pl.program_id(0)
    a = block_abs(i, info)

    @pl.when(i == 0)
    def _():
        run_states(s_in, kv, states, info, ends, rates, range(TEAM))

    for h in range(HEADS_OWN):
        at = slice(h * HEAD, (h + 1) * HEAD)
        q_scale, _, _ = scales(a, info, ends, rates, h)
        qs = (q[0, :, at].astype(F32) * q_scale).astype(BF)
        m = local[0, :, at] + dot(qs, states[a, h])
        mixed[0, :, at] = m
        gated[0, :, at] = (pu[0, :, at] * rms(m)).astype(BF)
    halves(i, dot(gated[0], wo[...]).astype(BF), keep, give)


KEEP = pl.BlockSpec((1, ROWS, WIDTH), lambda i, *_: (jnp.minimum(i, 1), 0, 0))
GIVE = pl.BlockSpec((1, ROWS, WIDTH), lambda i, *_: (jnp.maximum(i - 2, 0), 0, 0))
BY_ABS = pl.BlockSpec((1, ROWS, COLS), lambda i, info, *_: (block_abs(i, info), 0, 0))
BY_ABS_WIDE = pl.BlockSpec((1, ROWS, WIDTH), lambda i, info, *_: (block_abs(i, info), 0, 0))
BY_I = pl.BlockSpec((1, ROWS, ROWS), lambda i, *_: (i, 0, 0))
BY_I_WIDE = pl.BlockSpec((1, ROWS, WIDTH), lambda i, *_: (i, 0, 0))
PAIR = sds((2, ROWS, WIDTH))


def carry_in(scal, local, q, pu, kv, s_in, wo):
    return run(
        carry_kernel,
        (sds((TEAM, ROWS, COLS), F32), sds((TEAM, ROWS, COLS)), PAIR, PAIR),
        scal,
        (local, q, pu, kv, s_in, wo),
        grid=(TEAM,),
        in_specs=[BY_ABS, BY_ABS, BY_ABS, full(*kv.shape), full(*s_in.shape), full(*wo.shape)],
        out_specs=[BY_ABS, BY_ABS, KEEP, GIVE],
        scratch=[pltpu.VMEM((TEAM, HEADS_OWN, HEAD, HEAD), BF)],
        flops=1 << 29,
        nbytes=8 << 20,
    )


def order_kernel(enter, g0, g1, g2, g3, g):
    i = pl.program_id(0)
    for t, raw in enumerate((g0, g1, g2, g3)):

        @pl.when(i == t)
        def _():
            g[0] = dot(enter[0], raw[...]).astype(BF)


def order(enter, raws):
    return run(
        order_kernel,
        sds((TEAM, ROWS, WIDTH)),
        (),
        (enter, *raws),
        grid=(TEAM,),
        in_specs=[BY_I, *[full(ROWS, WIDTH)] * 4],
        out_specs=BY_I_WIDE,
    )


def sglu_kernel(info, x, ta, tb, g, w,
                n2, product, gg, gu, r_keep, r_give, n_keep, n_give, wd, scr, back):
    i = pl.program_id(0)
    pieces = [w.at[p] for p in range(N_SHARD)]

    @pl.when(i == 0)
    def _():
        for p in range(N_SHARD):
            for c in range(4):
                at = 2 * FF_OWN + c * FF_PART
                wd[p * FF_PART : (p + 1) * FF_PART, c * 256 : (c + 1) * 256] = w[p, at : at + FF_PART]

    att = jnp.where(i < 2, ta[0].astype(F32), tb[0].astype(F32))
    scr[...] = rms(x[0].astype(F32) + att).astype(BF)
    n2[0] = scr[...]
    gate = up = None
    for j in range(N_SHARD):
        rows = scr[:, j * 256 : (j + 1) * 256]
        one, two = dot(rows, pieces[j][:FF_OWN], NT), dot(rows, pieces[j][FF_OWN : 2 * FF_OWN], NT)
        gate, up = (one, two) if j == 0 else (gate + one, up + two)
    prod = (gate * up).astype(BF)
    product[0] = prod
    g_prod = dot(g[0], wd[...], NT)
    one, two = (g_prod * up).astype(BF), (g_prod * gate).astype(BF)
    gg[0], gu[0] = one, two
    for j in range(N_SHARD):
        back[:, j * 256 : (j + 1) * 256] = (dot(one, pieces[j][:FF_OWN]) + dot(two, pieces[j][FF_OWN : 2 * FF_OWN])).astype(BF)
    halves(i, back[...], n_keep, n_give)
    halves(i, dot(prod, wd[...]).astype(BF), r_keep, r_give)


def sglu(info, x, ta, tb, g, w_ff):
    hid = pl.BlockSpec((1, ROWS, FF_OWN), lambda i, *_: (i, 0, 0))
    hid_out = sds((TEAM, ROWS, FF_OWN))
    return run(
        sglu_kernel,
        (sds((TEAM, ROWS, WIDTH)), hid_out, hid_out, hid_out, PAIR, PAIR, PAIR, PAIR),
        (info,),
        (x, ta, tb, g, w_ff),
        grid=(TEAM,),
        in_specs=[BY_I_WIDE, KEEP, GIVE, BY_I_WIDE, full(*w_ff.shape)],
        out_specs=[BY_I_WIDE, hid, hid, hid, KEEP, GIVE, KEEP, GIVE],
        scratch=[pltpu.VMEM((FF_OWN, WIDTH), BF), pltpu.VMEM((ROWS, WIDTH), BF), pltpu.VMEM((ROWS, WIDTH), BF)],
        mib=30,
    )


def flat(v):
    return v.reshape(-1, v.shape[-1])


def turn(i, first):
    return rel_of(i) if first == 1 else i


def grads_call(kernel, info, rows, args, specs, scratch=(), nbytes=0):
    shape = (2, rows, 256)
    return run(
        kernel,
        (sds(shape), sds(shape)),
        (info,),
        args,
        grid=(N_SHARD,),
        in_specs=specs,
        out_specs=[
            pl.BlockSpec((1, rows, 256), lambda i, *_: (jnp.minimum(i, 1), 0, 0)),
            pl.BlockSpec((1, rows, 256), lambda i, *_: (jnp.maximum(i - 2, 0), 0, 0)),
        ],
        scratch=scratch,
        nbytes=nbytes,
    )


def hidden_grads_kernel(info, n2, grad, keep, give):
    halves(pl.program_id(0), dot(grad[...], n2[...], TN).astype(BF), keep, give)


def hidden_grads(info, n2, grad, first):
    span = TEAM * ROWS
    specs = [
        pl.BlockSpec((span, 256), lambda i, info: (0, place(info, turn(i, first)))),
        full(span, FF_OWN),
    ]
    return grads_call(hidden_grads_kernel, info, FF_OWN, (flat(n2), flat(grad)), specs)


def down_grads(info, g, product, first):
    span = TEAM * ROWS

    def kernel(info, g, product, keep, give, dd):
        i = pl.program_id(0)

        @pl.when(i == 0)
        def _():
            for c in range(4):
                dd[c] = dot(product[...], g[:, c * 256 : (c + 1) * 256], TN).astype(BF)

        rows = pl.ds(pl.multiple_of(place(info, turn(i, first)) * FF_PART, 16), FF_PART)
        for c in range(4):
            at = slice(c * FF_PART, (c + 1) * FF_PART)

            @pl.when(i < 2)
            def _():
                keep[0, at] = dd[c, rows]

            @pl.when(i >= 2)
            def _():
                give[0, at] = dd[c, rows]

    specs = [full(span, WIDTH), full(span, FF_OWN)]
    return grads_call(
        kernel, info, FF_OWN, (flat(g), flat(product)), specs, scratch=[pltpu.VMEM((4, FF_OWN, 256), BF)]
    )


def hidden_back_kernel(info, ends, rates, x, ta, tb, ua, ub, g, wo, mixed, pu, q,
                       ga, gpu, gm, qg, gh, state):
    i = pl.program_id(0)
    a = block_abs(i, info)
    att = jnp.where(i < 2, ta[0].astype(F32), tb[0].astype(F32))
    gn2 = jnp.where(i < 2, ua[0].astype(F32), ub[0].astype(F32))
    grad = g[0].astype(F32) + rms_back(x[0].astype(F32) + att, gn2)
    ga[0] = grad.astype(BF)

    @pl.when(i == 0)
    def _():
        gh[...] = grad

    g_gated = dot(ga[0], wo[...], NT)
    for h in range(HEADS_OWN):
        at = slice(h * HEAD, (h + 1) * HEAD)
        m = mixed[0, :, at]
        gpu[0, :, at] = (g_gated[:, at] * rms(m)).astype(BF)
        gmb = rms_back(m, g_gated[:, at] * pu[0, :, at]).astype(BF)
        gm[0, :, at] = gmb
        q_scale, _, _ = scales(a, info, ends, rates, h)
        qs = (q[0, :, at].astype(F32) * q_scale).astype(BF)
        qg[a, h] = dot(qs, gmb, TN)

    @pl.when(i == TEAM - 1)
    def _():
        for h in range(HEADS_OWN):
            total = qg[TEAM - 1, h]
            for b in reversed(range(TEAM - 1)):
                total = passing(b, info, ends, rates, h) * total + qg[b, h]
            state[h] = total.astype(BF)


def hidden_back(scal, x, ta, tb, ua, ub, g, wo, mixed, pu, q):
    block = sds((TEAM, ROWS, COLS))
    return run(
        hidden_back_kernel,
        (
            sds((TEAM, ROWS, WIDTH)), block, block, sds((TEAM, HEADS_OWN, HEAD, HEAD), F32), sds((ROWS, WIDTH), F32),
            sds((HEADS_OWN, HEAD, HEAD)),
        ),
        scal,
        (x, ta, tb, ua, ub, g, wo, mixed, pu, q),
        grid=(TEAM,),
        in_specs=[BY_I_WIDE, KEEP, GIVE, KEEP, GIVE, BY_I_WIDE, full(*wo.shape), BY_ABS, BY_ABS, BY_ABS],
        out_specs=[
            BY_ABS_WIDE, BY_ABS, BY_ABS, full(TEAM, HEADS_OWN, HEAD, HEAD), full(ROWS, WIDTH), full(HEADS_OWN, HEAD, HEAD),
        ],
        flops=1 << 30,
        nbytes=14 << 20,
    )


def scores_back_kernel(info, ends, rates, q, k, v, gm, kv, s_in, gq, gk, gv, dec, states):
    b = pl.program_id(0)

    @pl.when(b == 0)
    def _():
        decay_masks(info, rates, dec)
        run_states(s_in, kv, states, info, ends, rates, range(TEAM))

    same = same_seg(b, info, ends)
    for h in range(HEADS_OWN):
        at = slice(h * HEAD, (h + 1) * HEAD)
        qh, kh, vh, gh = q[0, :, at], k[0, :, at], v[0, :, at], gm[0, :, at]
        q_scale, _, _ = scales(b, info, ends, rates, h)
        mixing = jnp.where(same, dot(qh, kh, NT) * dec[h], 0.0).astype(BF)
        g_scores = jnp.where(same, dot(gh, vh, NT) * dec[h], 0.0).astype(BF)
        gq[0, :, at] = dot(g_scores, kh) + q_scale * dot(gh, states[b, h], NT)
        gk[0, :, at] = dot(g_scores, qh, TN)
        gv[0, :, at] = dot(mixing, gh, TN)


def scores_back(scal, q, k, v, gm, kv, s_in):
    block = sds((TEAM, ROWS, COLS), F32)
    return run(
        scores_back_kernel,
        (block, block, block),
        scal,
        (q, k, v, gm, kv, s_in),
        grid=(TEAM,),
        in_specs=[*[BLOCK_SPEC] * 4, full(*kv.shape), full(*s_in.shape)],
        out_specs=[BLOCK_SPEC] * 3,
        scratch=[
            pltpu.VMEM((HEADS_OWN, BLOCK, BLOCK), F32),
            pltpu.VMEM((TEAM, HEADS_OWN, HEAD, HEAD), BF),
        ],
        flops=3 << 28,
        nbytes=6 << 20,
    )


def silu_slope(p):
    s = jax.nn.sigmoid(p)
    return s * (1.0 + p * (1.0 - s))


def project_back_kernel(info, ends, rates, gq, gk, gv, pq, pk, k, v, gpu, qg, g_in, w0, w1, w2, w3,
                        dqkv, keep, give, states, back):
    i = pl.program_id(0)
    a = block_abs(i, info)

    @pl.when(i == 0)
    def _():
        run_states(g_in, qg, states, info, ends, rates, (3, 2, 1, 0))

    dqkv[0, :, :COLS] = (gq[0] * silu_slope(pq[0])).astype(BF)
    for h in range(HEADS_OWN):
        at = slice(h * HEAD, (h + 1) * HEAD)
        _, k_scale, _ = scales(a, info, ends, rates, h)
        kh, vh = k[0, :, at], v[0, :, at]
        ks = (kh.astype(F32) * k_scale).astype(BF)
        g_k = gk[0, :, at] + k_scale * dot(vh, states[a, h], NT)
        to_k = slice(COLS + h * HEAD, COLS + (h + 1) * HEAD)
        to_v = slice(2 * COLS + h * HEAD, 2 * COLS + (h + 1) * HEAD)
        dqkv[0, :, to_k] = (g_k * silu_slope(pk[0, :, at])).astype(BF)
        dqkv[0, :, to_v] = (gv[0, :, at] + dot(ks, states[a, h])).astype(BF)
    refs = (w0, w1, w2, w3)
    grads = (dqkv[0, :, :COLS], dqkv[0, :, COLS : 2 * COLS], dqkv[0, :, 2 * COLS :], gpu[0])
    for j in range(N_SHARD):
        total = dot(grads[0], weight_at(refs, j, 0), NT)
        for t in (1, 2, 3):
            total = total + dot(grads[t], weight_at(refs, j, t), NT)
        back[:, lanes(j, info)] = total.astype(BF)
    halves(i, back[...], keep, give)


def project_back(scal, gq, gk, gv, pq, pk, k, v, gpu, qg, g_in, pieces):
    return run(
        project_back_kernel,
        (sds((TEAM, ROWS, 3 * COLS)), PAIR, PAIR),
        scal,
        (gq, gk, gv, pq, pk, k, v, gpu, qg, g_in, *pieces),
        grid=(TEAM,),
        in_specs=[*[BY_ABS] * 8, full(*qg.shape), full(*g_in.shape), *[full(*p.shape) for p in pieces]],
        out_specs=[pl.BlockSpec((1, ROWS, 3 * COLS), lambda i, info, *_: (block_abs(i, info), 0, 0)), KEEP, GIVE],
        scratch=[pltpu.VMEM((TEAM, HEADS_OWN, HEAD, HEAD), BF), pltpu.VMEM((ROWS, WIDTH), BF)],
        flops=5 << 29,
        nbytes=14 << 20,
    )


def column_grads(info, pairs, first):
    span = TEAM * ROWS
    args, specs = [], []
    for pair in pairs:
        for v in pair:
            args.append(v.reshape(span, v.shape[-1]))
            wide = v.shape[-1] == WIDTH
            cut = (lambda i, info: (0, place(info, turn(i, first)))) if wide else (lambda i, info: (0, 0))
            specs.append(pl.BlockSpec((span, 256 if wide else v.shape[-1]), cut))
    n = sum(1 if b.shape[-1] == WIDTH else b.shape[-1] // 256 for _, b in pairs)

    def kernel(info, *refs):
        i = pl.program_id(0)
        values = []
        for t in range(len(pairs)):
            value = dot(refs[2 * t][...], refs[2 * t + 1][...], TN).astype(BF)
            values += [value[:, c * 256 : (c + 1) * 256] for c in range(value.shape[1] // 256)]
        for t, value in enumerate(values):
            at = slice(t * 256, (t + 1) * 256)

            @pl.when(i < 2)
            def _():
                refs[-2][0, at] = value

            @pl.when(i >= 2)
            def _():
                refs[-1][0, at] = value

    return grads_call(kernel, info, n * 256, tuple(args), specs)


def hop(parts, first, hold=(), hold_send=()):
    keep, give = parts
    if hold_send:
        give = after(give, *hold_send)
    got = send(give, "shard", first)
    if hold:
        got = after(got, *hold)
    total = keep.astype(F32) + got.astype(F32)
    return total[0].astype(BF), total[1].astype(BF)


def hop_two(own, other, first):
    return own, send(other, "shard", 3 - first)


def joined(terms, hold=()):
    if hold:
        terms = [(own, after(got, *hold)) for own, got in terms]
    return jnp.concatenate([(own.astype(F32) + got.astype(F32)).astype(BF) for own, got in terms], 0)


def over_zh(part, hold=()):
    got = send(part, "zh", 1)
    if hold:
        got = after(got, *hold)
    return (part.astype(F32) + got.astype(F32)).astype(BF)


def fin_out_kernel(info, p0, p1, p2, p3, fin, stack):
    unit = jnp.where(
        lax.broadcasted_iota(jnp.int32, (256, 256), 0) == lax.broadcasted_iota(jnp.int32, (256, 256), 1), 1.0, 0.0
    ).astype(BF)
    for j, p in enumerate((p0, p1, p2, p3)):
        q = info[0] ^ j
        for n in range(2 * N_SHARD):
            start = pl.multiple_of(n * FF_OWN + q * FF_PART, 16)
            stack[pl.ds(start, FF_PART)] = p[n * FF_PART : (n + 1) * FF_PART]
    for n in range(11):
        fin[:, n * 512 : (n + 1) * 512] = dot(unit, stack[n * 512 : (n + 1) * 512], NT)


def fin_out(info, pieces):
    return run(
        fin_out_kernel,
        sds((256, 8 * FF_OWN), F32),
        (info,),
        tuple(pieces),
        in_specs=[full(2 * FF_OWN, 256)] * 4,
        out_specs=full(256, 8 * FF_OWN),
        scratch=[pltpu.VMEM((8 * FF_OWN, 256), BF)],
        mib=24,
        flops=1 << 30,
        nbytes=9 << 20,
    )


def down_out_kernel(info, p0, p1, p2, p3, down):
    for j, p in enumerate((p0, p1, p2, p3)):
        rows = pl.ds(pl.multiple_of((info[0] ^ j) * FF_PART, 16), FF_PART)
        for c in range(4):
            down[rows, c * 256 : (c + 1) * 256] = p[c * FF_PART : (c + 1) * FF_PART].astype(F32)


def down_out(info, pieces):
    return run(
        down_out_kernel,
        sds((FF_OWN, WIDTH), F32),
        (info,),
        tuple(pieces),
        in_specs=[full(*p.shape) for p in pieces],
        out_specs=full(FF_OWN, WIDTH),
        nbytes=5 << 20,
    )


def last_out_kernel(info, q0, q1, q2, q3, d0, d1, d2, d3, o0, o1, o2, o3, g_q, g_k, g_v, g_u, g_out):
    for j, (p, d, o) in enumerate(zip((q0, q1, q2, q3), (d0, d1, d2, d3), (o0, o1, o2, o3))):
        at = pl.ds(pl.multiple_of((info[0] ^ j) * 256, 256), 256)
        for t, out in enumerate((g_q, g_k, g_v)):
            out[:, at] = p[t * 256 : (t + 1) * 256].astype(F32)
        g_u[:, at] = d[FF_OWN + 256 :].astype(F32)
        g_out[:, lanes(j, info)] = o[...].astype(F32)


def last_out(info, pieces):
    return run(
        last_out_kernel,
        (sds((256, WIDTH), F32),) * 5,
        (info,),
        tuple(pieces),
        in_specs=[full(*p.shape) for p in pieces],
        out_specs=[full(256, WIDTH)] * 5,
    )


def finish_kernel(x, gh, here, got, enter, out):
    gn = here[...] + got[...].astype(F32)
    grad = (gh[...] + rms_back(x[0].astype(F32), gn)).astype(BF)
    out[...] = dot(enter[0], grad, TN).astype(BF)


def result_kernel(x, att, here, got, enter, out):
    result = (x[0].astype(F32) + att[0].astype(F32) + here[...] + got[...].astype(F32)).astype(BF)
    out[...] = dot(enter[0], result, TN).astype(BF)


def finish(kernel, x, second, here, got, enter):
    first = lambda v: pl.BlockSpec((1, *v.shape[1:]), lambda _: (0,) * v.ndim) if v.ndim == 3 else full(*v.shape)
    args = (x, second, here, got, enter)
    return run(
        kernel,
        sds((ROWS, WIDTH)),
        (),
        args,
        in_specs=[first(v) for v in args],
        out_specs=full(ROWS, WIDTH),
        flops=1 << 28,
        nbytes=4 << 20,
    )


def unsort_kernel(leave, rows, out):
    out[...] = dot(leave[...], rows[...], TN).astype(BF)


def unsort(leave, rows):
    return run(
        unsort_kernel,
        sds((ROWS, WIDTH)),
        (),
        (leave, rows),
        in_specs=[full(ROWS, ROWS), full(ROWS, WIDTH)],
        out_specs=full(ROWS, WIDTH),
        flops=1 << 28,
        nbytes=2 << 20,
    )


def exchange(rows):
    return lax.all_to_all(rows, ALL, split_axis=0, concat_axis=0, tiled=True)


def team_raw(own):
    pair = send(own, "zl", 1)
    return [own, pair, send(own, "core", 1), send(pair, "core", 1)]


def team_sum(keep, give, hold=()):
    got = send(give, "core", 1)
    half = (keep.astype(F32) + got.astype(F32)).astype(BF)
    other = send(half, "zl", 1)
    if hold:
        other = after(other, *hold)
    ours = (half.astype(F32) + other[::-1].astype(F32)).astype(BF)
    return ours, send(ours, "core", 1), half


def team_own(keep, give, *behind):
    there = keep[1].astype(F32) + send(give[1], "core", 1).astype(F32)
    here = keep[0].astype(F32) + send(give[0], "core", 1).astype(F32)
    there = there.astype(BF)
    if behind:
        there = after(there, *behind)
    return here, send(there, "zl", 1)


def state_in(state, near, whole, cross, hold=()):
    low = [state] + [lax.ppermute(state, "shard", [(i, i ^ j) for i in range(4)]) for j in (1, 2, 3)]
    wide = [v.astype(F32) for v in low]
    hand = sum(whole[j][:, None, None] * wide[j] for j in range(4))
    if hold:
        hand = after(hand, *hold)
    got = send(hand, "zh", 1)
    here = sum(near[j][:, None, None] * wide[j] for j in (1, 2, 3))
    return here + cross[:, None, None] * got, hand


def fast_body(tokens_in, cotangent, deal_order, lengths, decay_rates, w_query, w_key, w_value, w_ugate, w_out, w_ffin, w_ffdown):
    zh, zl, core, shard = (lax.axis_index(a) for a in ALL)
    me = zl * 2 + core
    group = zh * N_SHARD + shard
    device = (zh * TEAM + me) * N_SHARD + shard
    span = TEAM * ROWS
    info = jnp.stack([me, shard, group * span, device, zh, jnp.int32(0), jnp.int32(0), jnp.int32(0)]).astype(jnp.int32)
    ends = jnp.sum(jnp.where(jnp.arange(8)[None, :] <= jnp.arange(8)[:, None], lengths[None, :], 0), axis=1).astype(jnp.int32)
    scal = (info, ends, decay_rates)
    by_device = deal_order.reshape(2, N_SHARD, TEAM, ROWS).transpose(0, 2, 1, 3).reshape(DEVICES, ROWS)

    leave, enter, sent_x, sent_g = exchange_rows(info, by_device, *far(tokens_in, cotangent))
    raw_x = exchange(sent_x)
    quarter = take_quarter(after(info, sent_x), *far(w_query, w_key, w_value, w_ugate))
    w_proj = gather_pieces(quarter)
    bundle = ff_bundle(after(info, quarter), *far(w_ffin, w_ffdown))
    w_ff = lax.all_gather(after(bundle, raw_x), "shard", axis=0)
    wo = gather_out(w_out, me, shard)
    x_raws = team_raw(raw_x)
    g_raws = team_raw(exchange(after(sent_g, raw_x)))

    rates = lax.dynamic_slice_in_dim(decay_rates, me * HEADS_OWN, HEADS_OWN)

    def seg_at(p):
        seg = jnp.sum((p[..., None] >= ends).astype(jnp.int32), axis=-1)
        return jnp.where(p < 0, -1, seg)

    def weigh(flag, gap):
        return jnp.where(flag[..., None], jnp.exp(-(jnp.maximum(gap, 0) * span).astype(F32)[..., None] * rates), 0.0)

    peers = zh * N_SHARD + (shard ^ jnp.arange(4))
    peers_last, peers_before = seg_at((peers + 1) * span - 1), seg_at(peers * span - 1)
    my_last, my_before = peers_last[0], peers_before[0]
    end, start = zh * N_SHARD + 3, zh * N_SHARD
    f_near = weigh((peers < group) & (peers_last == my_before), group - 1 - peers)
    f_whole = weigh(peers_last == seg_at((end + 1) * span - 1), end - peers)
    f_cross = weigh((zh == 1) & (seg_at(start * span - 1) == my_before), shard)
    b_near = weigh((peers > group) & (peers_before == my_last), peers - 1 - group)
    b_whole = weigh(peers_before == seg_at(start * span - 1), peers - start)
    b_cross = weigh((zh == 0) & (seg_at((end + 1) * span - 1) == my_last), 3 - shard)

    x, normed, pq, pk, pu, q, k, v, kv, state = project(scal, enter, far(*x_raws), far(*w_proj))
    s_in, _ = state_in(state, f_near, f_whole, f_cross)
    local = attend_local(scal, q, k, v)
    mixed, gated, a_keep, a_give = carry_in((after(info, g_raws[1]), *scal[1:]), local, q, pu, kv, s_in, wo)
    g = order(*far(enter), far(*g_raws))
    ta, tb, _ = team_sum(a_keep, a_give, hold=(g,))
    n2, product, gg, gu, r_keep, r_give, n_keep, n_give = sglu(info, x, ta, *far(tb, g), *far(w_ff))
    n_got = send(n_give, "core", 1)
    d_gate = hidden_grads(info, n2, gg, 1)
    n_half = (n_keep.astype(F32) + n_got.astype(F32)).astype(BF)
    n_other = send(n_half, "zl", 1)
    d_up = hidden_grads(after(info, n_half), n2, gu, 2)
    d_down = down_grads(after(info, d_up[1]), g, product, 1)
    gate_own, gate_other = hop(d_gate, 1, hold=(d_down[1],))
    n_other = after(n_other, d_down[1], gate_other)
    ua = (n_half.astype(F32) + n_other[::-1].astype(F32)).astype(BF)
    ub = send(ua, "core", 1)
    up_own, up_other = hop(d_up, 2, hold=(ua,))

    ga, gpu, gm, qg, gh, g_state = hidden_back(
        (after(info, up_other), *scal[1:]), x, ta, *far(tb), ua, *far(ub), g, wo, mixed, pu, q
    )
    gate = hop_two(gate_own, gate_other, 1)
    up = hop_two(up_own, up_other, 2)
    gq, gk, gv = scores_back(scal, q, k, v, gm, kv, s_in)
    r_here, r_there = team_own(r_keep, r_give, ua)
    g_in, handed = state_in(g_state, b_near, b_whole, b_cross, hold=(r_there,))
    d_ou = column_grads(after(info, handed), [(gated, ga), (normed, gpu)], 2)
    fin = joined((gate, up), hold=(d_ou[1],))
    dqkv, p_keep, p_give = project_back(
        (after(info, fin), *scal[1:]), gq, gk, gv, pq, pk, k, v, gpu, qg, g_in, far(*w_proj)
    )
    here, there = team_own(p_keep, p_give)
    d_qkv = column_grads(info, [(normed, dqkv)], 1)
    last_sent = finish(finish_kernel, x, gh, here, there, after(enter, d_qkv[1]))
    input_grad = unsort(leave, exchange(last_sent))
    output = unsort(leave, exchange(finish(result_kernel, x, ta, r_here, r_there, after(enter, last_sent))))

    down_own, down_other = hop(d_down, 1, hold=(last_sent,), hold_send=(handed,))
    ou_own, ou_other = hop(d_ou, 2, hold=(down_other,))
    fin_sum = over_zh(fin, hold=(ou_other,))
    fin_pair = send(fin_sum, "zl", 1)
    fin_all = [fin_sum, send(fin_sum, "core", 1), fin_pair, send(fin_pair, "core", 1)]
    down_ou = joined((hop_two(down_own, down_other, 1), hop_two(ou_own, ou_other, 2)), hold=(fin_sum,))
    qkv_own, qkv_other = hop(d_qkv, 1, hold=(last_sent,))
    qkv = joined((hop_two(qkv_own, qkv_other, 1),))
    down_sum = over_zh(down_ou, hold=(fin_pair, input_grad))
    down_pair = send(down_sum, "zl", 1)
    down_all = [down_sum, send(down_sum, "core", 1), down_pair, send(down_pair, "core", 1)]
    grad_fin = fin_out(info, far(*fin_all))
    grad_down = down_out(info, far(*down_all))
    outs = []
    for j in range(4):
        pick = me ^ shard ^ j
        top = [p[FF_OWN : FF_OWN + 256] for p in down_all]
        piece = jnp.where(pick < 2, jnp.where(pick == 0, top[0], top[1]), jnp.where(pick == 2, top[2], top[3]))
        outs.append(piece if j == 0 else send(piece, "shard", j))
    qkv_sum = over_zh(qkv, hold=(down_pair, output, fin_all[3]))
    qkv_pair = send(qkv_sum, "zl", 1)
    qkv_late = after(qkv_pair, grad_fin, grad_down, *outs[1:])
    qkv_all = [qkv_sum, send(qkv_sum, "core", 1), qkv_late, send(qkv_late, "core", 1)]
    grad_q, grad_k, grad_v, grad_u, grad_out = last_out(info, far(*qkv_all, *down_all, *outs))
    return (output, input_grad, grad_q, grad_k, grad_v, grad_u, grad_out, grad_fin, grad_down)


def solution(mesh):
    rep, shard = mesh.shape["rep"], mesh.shape["shard"]
    team = Mesh(mesh.devices.reshape(rep // TEAM, 2, 2, shard), ALL)
    token, weight = P(ALL, None), P("shard", None)
    return jax.shard_map(
        fast_body if (rep, shard) == (8, 4) else general_body,
        mesh=team,
        in_specs=(token, token, P(), P(), P(), *([weight] * 7)),
        out_specs=(token, token, *([weight] * 7)),
        check_vma=False,
    )
```

```python
import functools

import jax
import jax.numpy as jnp
from jax import lax
from jax.experimental import pallas as pl
from jax.experimental.pallas import tpu as pltpu
from jax.sharding import Mesh, PartitionSpec as P

HEAD = 128
BLOCK = 256
TEAM = 4
EPS = 1e-06
BF = jnp.bfloat16
F32 = jnp.float32
ALL = ("zh", "zl", "core", "shard")


def send(value, axis, mask):
    size = lax.axis_size(axis)
    return lax.ppermute(value, axis, [(i, i ^ mask) for i in range(size)])


def dot(a, b, dims=((1,), (0,))):
    return lax.dot_general(a, b, (dims, ((), ())), preferred_element_type=F32)


def norm_scale(values):
    return lax.rsqrt(jnp.mean(values * values, axis=-1, keepdims=True) + EPS)


def norm_back(values, grad):
    scale = norm_scale(values)
    return scale * grad - values * (scale**3) * jnp.mean(values * grad, axis=-1, keepdims=True)


def in_order(pieces, index):
    pieces = list(pieces)
    bit = 1
    while bit < len(pieces):
        flip = (index & bit) != 0
        pieces = [jnp.where(flip, pieces[j ^ bit], pieces[j]) for j in range(len(pieces))]
        bit *= 2
    return pieces


def gather_shard(part):
    size = lax.axis_size("shard")
    if size != 4:
        every = lax.all_gather(part, "shard", axis=0)
        return [every[j] for j in range(size)]
    half = part.shape[0] // 2
    by_x, by_y = send(part, "shard", 1), send(part, "shard", 2)
    far = jnp.concatenate([send(by_x[:half], "shard", 2), send(by_y[half:], "shard", 1)], 0)
    return in_order([part, by_x, by_y, far], lax.axis_index("shard"))


def scatter_shard(parts):
    size = lax.axis_size("shard")
    if size != 4:
        return lax.psum_scatter(jnp.stack(parts), "shard", scatter_dimension=0, tiled=False)
    rel = in_order(parts, lax.axis_index("shard"))
    total = rel[0].astype(F32)
    for j in (1, 2, 3):
        total = total + send(rel[j].astype(BF), "shard", j).astype(F32)
    return total


def sum_zh(part):
    size = lax.axis_size("zh")
    part = part.astype(BF)
    if size != 2:
        return lax.psum(part.astype(F32), "zh").astype(BF)
    return (part.astype(F32) + send(part, "zh", 1).astype(F32)).astype(BF)


def team_gather(own):
    pair = send(own, "zl", 1)
    return [own, send(own, "core", 1), pair, send(pair, "core", 1)]


def team_reduce(parts):
    low = [p.astype(BF) for p in parts]
    here = parts[0] + send(low[1], "core", 1).astype(F32)
    there = parts[2] + send(low[3], "core", 1).astype(F32)
    return here + send(there.astype(BF), "zl", 1).astype(F32)


def place_mix(state, weights):
    groups = lax.axis_size("zh") * lax.axis_size("shard")
    mine = lax.axis_index("zh") * lax.axis_size("shard") + lax.axis_index("shard")
    low = state.astype(BF)
    if groups != 8:
        every = lax.all_gather(low, ("zh", "shard"), axis=0).astype(F32)
        return jnp.sum(every * weights[:, :, None, None], axis=0)
    total = jnp.zeros_like(state)
    for j in range(1, groups):
        got = lax.ppermute(low, ("zh", "shard"), [(i, i ^ j) for i in range(groups)])
        factor = lax.dynamic_index_in_dim(weights, mine ^ j, 0, keepdims=False)
        total = total + factor[:, None, None] * got.astype(F32)
    return total


def after(value, *others):
    return lax.optimization_barrier((value, *others))[0]


def general_body(tokens_in, cotangent, deal_order, lengths, decay_rates, w_query, w_key, w_value, w_ugate, w_out, w_ffin, w_ffdown):
    rows, width = tokens_in.shape
    n_zh, n_shard = lax.axis_size("zh"), lax.axis_size("shard")
    groups = n_zh * n_shard
    devices = groups * TEAM
    zh, zl, core, shard = (lax.axis_index(a) for a in ALL)
    me = zl * 2 + core
    group = zh * n_shard + shard
    device = (zh * TEAM + me) * n_shard + shard
    heads = width // HEAD // TEAM
    cols = heads * HEAD
    depth = w_query.shape[0]
    ff = w_ffin.shape[1] // 2
    ff_shard = w_ffdown.shape[0]
    ff_own = ff_shard // TEAM
    per_peer = rows // devices
    span = rows * TEAM

    by_device = deal_order.reshape(n_zh, n_shard, TEAM, rows).transpose(0, 2, 1, 3).reshape(-1)
    row_ids = jnp.arange(rows, dtype=jnp.int32)
    key = jnp.sum(
        jnp.where(
            by_device[:, None] == device * rows + row_ids[None, :],
            jnp.arange(by_device.shape[0], dtype=jnp.int32)[:, None],
            0,
        ),
        axis=0,
    )
    rank = jnp.sum((key[:, None] < key[None, :]).astype(jnp.int32), axis=0)
    leave = (row_ids[:, None] == rank[None, :]).astype(BF)
    sent_x = dot(leave, tokens_in).astype(BF)
    sent_g = dot(leave, cotangent).astype(BF)
    got_x = lax.all_to_all(sent_x, ALL, split_axis=0, concat_axis=0, tiled=True)
    own_block = lax.dynamic_slice_in_dim(by_device, device * rows, rows)
    source = own_block // rows
    earlier = row_ids[None, :] < row_ids[:, None]
    own_rank = jnp.sum(((source[:, None] == source[None, :]) & earlier).astype(jnp.int32), axis=1)
    slot = source * per_peer + own_rank
    enter = (slot[:, None] == row_ids[None, :]).astype(BF)
    x_own = dot(enter, got_x).astype(BF)
    got_g = lax.all_to_all(after(sent_g, got_x), ALL, split_axis=0, concat_axis=0, tiled=True)
    g_own = dot(enter, got_g).astype(BF)

    def quarter(w):
        return lax.dynamic_slice_in_dim(w, me * cols, cols, axis=1)

    qkvu_part = jnp.concatenate([quarter(w) for w in (w_query, w_key, w_value, w_ugate)], 1)
    w_qkvu = jnp.concatenate(gather_shard(qkvu_part), 0)
    out_all = jnp.concatenate(gather_shard(after(w_out, w_qkvu)), 0)
    w_o = lax.dynamic_slice_in_dim(out_all, me * cols, cols)
    fin = w_ffin.reshape(depth, 2, n_shard, TEAM, ff_own)
    fin = lax.dynamic_index_in_dim(fin, me, 3, keepdims=False)
    fin = fin.transpose(1, 0, 2, 3).reshape(2 * depth, n_shard * ff_own)
    fin_parts = gather_shard(after(fin, out_all))
    w_gate = jnp.concatenate([p[:depth] for p in fin_parts], 0)
    w_up = jnp.concatenate([p[depth:] for p in fin_parts], 0)
    fdown = lax.dynamic_slice_in_dim(w_ffdown, me * ff_own, ff_own)
    w_down = jnp.concatenate(gather_shard(after(fdown, w_up)), 0)

    ends = jnp.sum(jnp.where(jnp.arange(8)[None, :] <= jnp.arange(8)[:, None], lengths[None, :], 0), axis=1)
    all_last = jnp.arange(1, groups + 1) * span - 1
    last_seg = jnp.sum((all_last[:, None] >= ends[None, :]).astype(jnp.int32), axis=1)
    before_seg = jnp.concatenate([jnp.full((1,), -1, jnp.int32), last_seg[:-1]])
    positions = group * span + jnp.arange(span)
    seg = jnp.sum((positions[:, None] >= ends[None, :]).astype(jnp.int32), axis=1)
    seg_before = before_seg[group]
    blocks = span // BLOCK
    seg_b = seg.reshape(blocks, BLOCK)
    prev_b = jnp.concatenate([seg_before[None], seg_b[:-1, -1]])
    rates = lax.dynamic_slice_in_dim(decay_rates, me * heads, heads)
    idx = jnp.arange(BLOCK).astype(F32)
    dist = idx[:, None] - idx[None, :]
    decay = jnp.where(dist >= 0, jnp.exp(-rates[:, None, None] * jnp.maximum(dist, 0.0)), 0.0)
    same = (seg_b[:, :, None] == seg_b[:, None, :]).astype(F32)
    mask = same[:, None] * decay[None]
    carry = (seg_b == prev_b[:, None]).astype(F32)
    q_scale = jnp.exp(-(idx + 1.0)[None, :, None] * rates) * carry[:, :, None]
    k_scale = jnp.exp(-(BLOCK - 1.0 - idx)[None, :, None] * rates) * (seg_b == seg_b[:, -1:]).astype(F32)[:, :, None]
    passing = (seg_b[:, -1] == prev_b).astype(F32)[:, None] * jnp.exp(-rates * BLOCK)[None]
    ids = jnp.arange(groups)
    gap = jnp.maximum(jnp.abs(ids - group) - 1, 0).astype(F32) * span
    into = (ids < group) & (last_seg == seg_before)
    outof = (ids > group) & (before_seg == last_seg[group])
    fade = jnp.exp(-gap[:, None] * rates[None, :])
    w_into = jnp.where(into[:, None], fade, 0.0)
    w_outof = jnp.where(outof[:, None], fade, 0.0)

    x = in_order(team_gather(x_own), me)
    x_all = jnp.concatenate(x, 0)
    xf = x_all.astype(F32)
    normed = (xf * norm_scale(xf)).astype(BF)
    pre = dot(normed, w_qkvu)
    pre_q, pre_k, pre_v, pre_u = (pre[:, i * cols : (i + 1) * cols] for i in range(4))
    shape = (blocks, BLOCK, heads, HEAD)
    q = jax.nn.silu(pre_q).astype(BF).reshape(shape)
    k = jax.nn.silu(pre_k).astype(BF).reshape(shape)
    v = pre_v.astype(BF).reshape(shape)

    def ein(text, a, b):
        return jnp.einsum(text, a, b, preferred_element_type=F32)

    ks = (k.astype(F32) * k_scale[..., None]).astype(BF)
    qs = (q.astype(F32) * q_scale[..., None]).astype(BF)
    kv = ein("bjhe,bjhf->bhef", ks, v)
    state = jnp.zeros((heads, HEAD, HEAD), F32)
    for b in range(blocks):
        state = passing[b][:, None, None] * state + kv[b]
    state_in = place_mix(state, w_into)
    scores = ein("bihe,bjhe->bhij", q, k)
    mixing = (scores * mask).astype(BF)
    mixed = ein("bhij,bjhf->bihf", mixing, v)
    states = []
    state = state_in
    for b in range(blocks):
        states.append(state)
        state = passing[b][:, None, None] * state + kv[b]
    states = jnp.stack(states).astype(BF)
    mixed = mixed + ein("bihe,bhef->bihf", qs, states)
    m_norm = (mixed * norm_scale(mixed)).reshape(span, cols)
    gated = (pre_u * m_norm).astype(BF)
    part = dot(gated, w_o).reshape(TEAM, rows, width)
    att = team_reduce(in_order([part[j] for j in range(TEAM)], me))
    att = jnp.concatenate(in_order(team_gather(att.astype(BF)), me), 0)
    hidden = xf + att.astype(F32)

    g_all = jnp.concatenate(in_order(team_gather(g_own), me), 0)
    n2 = (hidden * norm_scale(hidden)).astype(BF)
    gate, up = dot(n2, w_gate), dot(n2, w_up)
    product = (gate * up).astype(BF)
    res = dot(product, w_down).reshape(TEAM, rows, width)
    g_product = dot(g_all, w_down, ((1,), (1,)))
    g_gate, g_up = (g_product * up).astype(BF), (g_product * gate).astype(BF)
    gn2 = dot(g_gate, w_gate, ((1,), (1,))) + dot(g_up, w_up, ((1,), (1,)))
    gn2 = gn2.reshape(TEAM, rows, width)
    gn2 = team_reduce(in_order([gn2[j] for j in range(TEAM)], me))
    gn2 = jnp.concatenate(in_order(team_gather(gn2.astype(BF)), me), 0)
    g_hidden = g_all.astype(F32) + norm_back(hidden, gn2.astype(F32))
    ga = g_hidden.astype(BF)

    res = team_reduce(in_order([res[j] for j in range(TEAM)], me))
    my_rows = lambda a: lax.dynamic_slice_in_dim(a, me * rows, rows)
    result = (my_rows(hidden) + res).astype(BF)

    g_gated = dot(ga, w_o, ((1,), (1,)))
    g_pre_u = (g_gated * m_norm).astype(BF)
    gm = norm_back(mixed, (g_gated * pre_u).reshape(shape)).astype(BF)
    qg = ein("bihe,bihf->bhef", qs, gm)
    gs = jnp.zeros((heads, HEAD, HEAD), F32)
    for b in reversed(range(blocks)):
        gs = passing[b][:, None, None] * gs + qg[b]
    gs = place_mix(gs, w_outof)
    g_states = [None] * blocks
    for b in reversed(range(blocks)):
        g_states[b] = gs
        gs = passing[b][:, None, None] * gs + qg[b]
    g_states = jnp.stack(g_states).astype(BF)
    g_mixing = ein("bihf,bjhf->bhij", gm, v)
    g_scores = (g_mixing * mask).astype(BF)
    g_q = ein("bhij,bjhe->bihe", g_scores, k) + q_scale[..., None] * ein("bihf,bhef->bihe", gm, states)
    g_k = ein("bhij,bihe->bjhe", g_scores, q) + k_scale[..., None] * ein("bhef,bjhf->bjhe", g_states, v)
    g_v = ein("bhij,bihf->bjhf", mixing, gm) + ein("bjhe,bhef->bjhf", ks, g_states)

    def silu_back(pre_rows, grad):
        sig = jax.nn.sigmoid(pre_rows)
        return (grad * (sig * (1.0 + pre_rows * (1.0 - sig)))).astype(BF)

    g_pre = jnp.concatenate(
        [
            silu_back(pre_q, g_q.reshape(span, cols)),
            silu_back(pre_k, g_k.reshape(span, cols)),
            g_v.reshape(span, cols).astype(BF),
            g_pre_u,
        ],
        1,
    )
    gn = dot(g_pre, w_qkvu, ((1,), (1,))).reshape(TEAM, rows, width)
    gn = team_reduce(in_order([gn[j] for j in range(TEAM)], me))
    grad_x = (my_rows(g_hidden) + norm_back(x_own.astype(F32), gn)).astype(BF)

    def give_back(rows_own):
        ordered = dot(enter, rows_own, ((0,), (0,))).astype(BF)
        back = lax.all_to_all(ordered, ALL, split_axis=0, concat_axis=0, tiled=True)
        return dot(leave, back, ((0,), (0,))).astype(BF)

    output, input_grad = give_back(result), give_back(grad_x)

    def by_place(grad):
        return list(grad.astype(BF).reshape(n_shard, -1, grad.shape[-1]))

    d_down = dot(product, g_all, ((0,), (0,)))
    d_gate, d_up = dot(n2, g_gate, ((0,), (0,))), dot(n2, g_up, ((0,), (0,)))
    d_out = dot(gated, ga, ((0,), (0,)))
    d_qkvu = dot(normed, g_pre, ((0,), (0,)))

    def collect(parts):
        return in_order(team_gather(sum_zh(scatter_shard(parts))), me)

    down = collect(by_place(d_down))
    grad_down = jnp.concatenate(down, 0).astype(F32)
    fin_grad = [jnp.concatenate([a, b], 0) for a, b in zip(by_place(d_gate), by_place(d_up))]
    fin_grad = jnp.stack(collect(fin_grad), 0).reshape(TEAM, 2, depth, n_shard, ff_own)
    grad_fin = fin_grad.transpose(2, 1, 3, 0, 4).reshape(depth, 2 * ff).astype(F32)
    out_cols = width // n_shard
    d_out_cols = [d_out[:, j * out_cols : (j + 1) * out_cols].astype(BF) for j in range(n_shard)]
    d_out_rows = jnp.concatenate(collect(d_out_cols), 0)
    d_out_rows = lax.all_to_all(
        d_out_rows.reshape(n_shard, depth, out_cols), "shard", split_axis=0, concat_axis=0, tiled=True
    )
    grad_out = d_out_rows.transpose(1, 0, 2).reshape(depth, width).astype(F32)
    qkvu = collect(by_place(d_qkvu))
    grads = [
        jnp.concatenate([p[:, i * cols : (i + 1) * cols] for p in qkvu], 1).astype(F32) for i in range(4)
    ]
    return (output, input_grad, *grads, grad_out, grad_fin, grad_down)


N_SHARD = 4
ROWS = 256
WIDTH = 1024
COLS = 256
HEADS_OWN = 2
FF_PART = 176
FF_OWN = 704
SLOTS = 8
DEVICES = 32
TN = ((0,), (0,))
NT = ((1,), (1,))
NN = ((1,), (0,))
GLOBAL = pl.BlockSpec(memory_space=pltpu.VMEM)


def far(*values):
    return tuple(pltpu.with_memory_space_constraint(v, pltpu.HBM) for v in values)


def rel_of(i):
    return (i & 1) * 2 + (i >> 1)


def hbm(shape, dtype=BF):
    return pltpu.HBM(shape, dtype)


def sds(shape, dtype=BF):
    return jax.ShapeDtypeStruct(shape, dtype)


def run(kernel, out, prefetch, args, grid=None, in_specs=None, out_specs=None, scratch=(), mib=16, flops=0, nbytes=0):
    return pl.pallas_call(
        kernel,
        out_shape=out,
        grid_spec=pltpu.PrefetchScalarGridSpec(
            num_scalar_prefetch=len(prefetch),
            grid=grid or (1,),
            in_specs=in_specs,
            out_specs=out_specs,
            scratch_shapes=list(scratch),
        ),
        compiler_params=pltpu.CompilerParams(
            vmem_limit_bytes=mib << 20, dimension_semantics=("arbitrary",) * len(grid or (1,))
        ),
        cost_estimate=pl.CostEstimate(flops=0, bytes_accessed=0, transcendentals=0),
    )(*prefetch, *args)


def full(*shape):
    return pl.BlockSpec(shape, lambda *_: (0,) * len(shape))


def place(info, j):
    return info[1] ^ j


def block_abs(i, info):
    return info[0] ^ rel_of(i)


def seg_scalar(p, ends):
    total = jnp.int32(0)
    for n in range(8):
        total = total + jnp.where(p >= ends[n], 1, 0)
    return jnp.where(p < 0, -1, total)


def seg_vector(base, shape, dim, ends):
    p = base + lax.broadcasted_iota(jnp.int32, shape, dim)
    total = jnp.zeros(shape, jnp.int32)
    for n in range(8):
        total = total + jnp.where(p >= ends[n], 1, 0)
    return total


def scales(a, info, ends, rates, h):
    base = info[2] + a * BLOCK
    prev = seg_scalar(base - 1, ends)
    last = seg_scalar(base + BLOCK - 1, ends)
    seg = seg_vector(base, (BLOCK, HEAD), 0, ends)
    idx = lax.broadcasted_iota(jnp.int32, (BLOCK, HEAD), 0).astype(F32)
    r = rates[info[0] * HEADS_OWN + h]
    q_scale = jnp.where(seg == prev, jnp.exp(-(idx + 1.0) * r), 0.0)
    k_scale = jnp.where(seg == last, jnp.exp(-(BLOCK - 1.0 - idx) * r), 0.0)
    return q_scale, k_scale, passing(a, info, ends, rates, h)


def passing(a, info, ends, rates, h):
    base = info[2] + a * BLOCK
    same = seg_scalar(base - 1, ends) == seg_scalar(base + BLOCK - 1, ends)
    r = rates[info[0] * HEADS_OWN + h]
    return jnp.exp(jnp.full((1, HEAD), -float(BLOCK), F32) * r) * jnp.where(same, 1.0, 0.0)


def decay_masks(info, rates, out):
    dist = lax.broadcasted_iota(jnp.int32, (BLOCK, BLOCK), 0) - lax.broadcasted_iota(jnp.int32, (BLOCK, BLOCK), 1)
    away = jnp.maximum(dist, 0).astype(F32)
    for h in range(HEADS_OWN):
        r = rates[info[0] * HEADS_OWN + h]
        out[h] = jnp.where(dist >= 0, jnp.exp(-away * r), 0.0)


def same_seg(a, info, ends):
    base = info[2] + a * BLOCK
    return seg_vector(base, (BLOCK, 1), 0, ends) == seg_vector(base, (1, BLOCK), 1, ends)


def rms(v):
    return v * lax.rsqrt(jnp.mean(v * v, axis=-1, keepdims=True) + EPS)


def rms_back(v, g):
    s = lax.rsqrt(jnp.mean(v * v, axis=-1, keepdims=True) + EPS)
    return s * g - v * ((s * s * s) * jnp.mean(v * g, axis=-1, keepdims=True))


def lanes(j, info):
    return pl.ds(pl.multiple_of(place(info, j) * 256, 256), 256)


def rows_kernel(info, deal, tok, leave, sent_x):
    dev = info[3]
    d = deal[...]
    owner = lax.shift_right_logical(d, 8)
    mine = owner == dev
    r_i = lax.broadcasted_iota(jnp.int32, (ROWS, ROWS), 0)
    c_i = lax.broadcasted_iota(jnp.int32, (ROWS, ROWS), 1)
    upper = jnp.where(r_i < c_i, 1.0, 0.0).astype(BF)
    count = dot(jnp.where(mine, 1.0, 0.0).astype(BF), upper)
    local = (d - dev * ROWS).astype(F32)
    lane8 = lax.broadcasted_iota(jnp.int32, (DEVICES, 128), 1)
    picked = jnp.zeros((DEVICES, 128), F32)
    for slot in range(SLOTS):
        row = jnp.sum(jnp.where(mine & (count == float(slot)), local, 0.0), axis=1, keepdims=True)
        picked = jnp.where(lane8 == slot, row, picked)
    k_r = lax.broadcasted_iota(jnp.int32, (ROWS, DEVICES), 0)
    k_c = lax.broadcasted_iota(jnp.int32, (ROWS, DEVICES), 1)
    spread = jnp.where(lax.shift_right_logical(k_r, 3) == k_c, 1.0, 0.0).astype(BF)
    wide = dot(spread, picked.astype(BF))
    k8 = lax.broadcasted_iota(jnp.int32, (ROWS, 128), 0) & 7
    l8 = lax.broadcasted_iota(jnp.int32, (ROWS, 128), 1)
    column = jnp.sum(jnp.where(k8 == l8, wide, 0.0), axis=1, keepdims=True)
    lv = jnp.where(column == c_i.astype(F32), 1.0, 0.0).astype(BF)
    leave[...] = lv
    sent_x[...] = dot(lv, tok[...]).astype(BF)


def orders_kernel(info, deal, leave, cot, enter, sent_g):
    sent_g[...] = dot(leave[...], cot[...]).astype(BF)
    r_i = lax.broadcasted_iota(jnp.int32, (ROWS, ROWS), 0)
    c_i = lax.broadcasted_iota(jnp.int32, (ROWS, ROWS), 1)
    for i in range(TEAM):
        a = info[0] ^ rel_of(i)
        at = (info[4] * TEAM + a) * N_SHARD + info[1]
        src = lax.shift_right_logical(deal[pl.ds(at, 1), :], 8)
        src_f = src.astype(F32)
        src_col = jnp.sum(jnp.where(r_i == c_i, src_f, 0.0), axis=1, keepdims=True)
        alike = jnp.where((src_col == src_f) & (c_i < r_i), 1.0, 0.0)
        rank = jnp.sum(alike, axis=1, keepdims=True)
        slot = src_col * float(SLOTS) + rank
        enter[i] = jnp.where(slot == c_i.astype(F32), 1.0, 0.0).astype(BF)


def exchange_rows(info, by_device, tokens_in):
    leave, sent_x = run(
        rows_kernel,
        (sds((ROWS, ROWS)), sds((ROWS, WIDTH))),
        (info,),
        (by_device, tokens_in),
        in_specs=[full(DEVICES, ROWS), full(ROWS, WIDTH)],
        out_specs=[full(ROWS, ROWS), full(ROWS, WIDTH)],
    )
    return leave, sent_x


def exchange_orders(info, by_device, leave, cotangent):
    return run(
        orders_kernel,
        (sds((TEAM, ROWS, ROWS)), sds((ROWS, WIDTH))),
        (info,),
        (by_device, leave, cotangent),
        in_specs=[full(DEVICES, ROWS), full(ROWS, ROWS), full(ROWS, WIDTH)],
        out_specs=[full(TEAM, ROWS, ROWS), full(ROWS, WIDTH)],
    )


def quarter_kernel(info, wq, wk, wv, wu, out):
    for t, w in enumerate((wq, wk, wv, wu)):
        out[t * COLS : (t + 1) * COLS] = w[...]


def take_quarter(info, *weights):
    spec = pl.BlockSpec((256, COLS), lambda i, info: (0, info[0]))
    return run(
        quarter_kernel,
        sds((4 * COLS, COLS)),
        (info,),
        weights,
        in_specs=[spec] * 4,
        out_specs=full(4 * COLS, COLS),
        nbytes=1 << 20,
    )


def ff_bundle_kernel(info, fin, down, out, turned):
    me = info[0]
    unit = jnp.where(
        lax.broadcasted_iota(jnp.int32, (256, 256), 0) == lax.broadcasted_iota(jnp.int32, (256, 256), 1), 1.0, 0.0
    ).astype(BF)
    for n in range(11):
        turned[n * 512 : (n + 1) * 512] = dot(fin[:, n * 512 : (n + 1) * 512], unit, TN).astype(BF)
    for n in range(2 * N_SHARD):
        start = pl.multiple_of(n * FF_OWN + me * FF_PART, 16)
        out[n * FF_PART : (n + 1) * FF_PART] = turned[pl.ds(start, FF_PART)]
    for c in range(4):
        rows = pl.ds(pl.multiple_of(me * FF_PART, 16), FF_PART)
        at = 2 * FF_OWN + c * FF_PART
        out[at : at + FF_PART] = down[rows, c * 256 : (c + 1) * 256]


def ff_bundle(info, fin, down):
    return run(
        ff_bundle_kernel,
        sds((3 * FF_OWN, 256)),
        (info,),
        (fin, down),
        in_specs=[full(*fin.shape), full(*down.shape)],
        out_specs=full(3 * FF_OWN, 256),
        scratch=[pltpu.VMEM((8 * FF_OWN, 256), BF)],
        flops=1 << 30,
        nbytes=6 << 20,
    )


def gather_pieces(part):
    return [part] + [send(part, "shard", j) for j in (1, 2, 3)]


def gather_out(w_out, me, shard):
    axes = ("zl", "core", "shard")
    rel = me ^ shard
    wo = w_out
    for j in (1, 2, 3):
        pairs = [(m * N_SHARD + m, m * N_SHARD + (m ^ j)) for m in range(TEAM)]
        wo = jnp.where(rel == j, lax.ppermute(w_out, axes, pairs), wo)
    return wo


def weight_at(refs, j, t):
    return refs[j][t * 256 : (t + 1) * 256]


def project_kernel(info, ends, rates, enter, r0, r1, r2, r3, w0, w1, w2, w3,
                   x, normed, pq, pk, pu, q, k, v, kv, state, scr):
    i = pl.program_id(0)
    a = block_abs(i, info)
    for t, raw in enumerate((r0, r1, r2, r3)):

        @pl.when(i == t)
        def _():
            x[0] = dot(enter[0], raw[...]).astype(BF)

    scr[...] = rms(x[0].astype(F32)).astype(BF)
    normed[0] = scr[...]
    refs = (w0, w1, w2, w3)
    pre = []
    for t in range(4):
        total = dot(scr[:, lanes(0, info)], weight_at(refs, 0, t))
        for j in (1, 2, 3):
            total = total + dot(scr[:, lanes(j, info)], weight_at(refs, j, t))
        pre.append(total)
    pq[0], pk[0], pu[0] = pre[0], pre[1], pre[3]
    qb = (pre[0] * jax.nn.sigmoid(pre[0])).astype(BF)
    kb = (pre[1] * jax.nn.sigmoid(pre[1])).astype(BF)
    vb = pre[2].astype(BF)
    q[0], k[0], v[0] = qb, kb, vb
    for h in range(HEADS_OWN):
        at = slice(h * HEAD, (h + 1) * HEAD)
        _, k_scale, _ = scales(a, info, ends, rates, h)
        ks = (kb[:, at].astype(F32) * k_scale).astype(BF)
        kv[a, h] = dot(ks, vb[:, at], TN)

    @pl.when(i == TEAM - 1)
    def _():
        for h in range(HEADS_OWN):
            total = kv[0, h]
            for b in range(1, TEAM):
                total = passing(b, info, ends, rates, h) * total + kv[b, h]
            state[h] = total.astype(BF)


def project(scal, enter, raws, pieces):
    info = scal[0]
    by_abs = pl.BlockSpec((1, ROWS, COLS), lambda i, info, *_: (block_abs(i, info), 0, 0))
    by_abs_wide = pl.BlockSpec((1, ROWS, WIDTH), lambda i, info, *_: (block_abs(i, info), 0, 0))
    by_i = pl.BlockSpec((1, ROWS, ROWS), lambda i, *_: (i, 0, 0))
    by_i_wide = pl.BlockSpec((1, ROWS, WIDTH), lambda i, *_: (i, 0, 0))
    f32_block, bf_block = sds((TEAM, ROWS, COLS), F32), sds((TEAM, ROWS, COLS))
    return run(
        project_kernel,
        (
            hbm((TEAM, ROWS, WIDTH)), hbm((TEAM, ROWS, WIDTH)), hbm((TEAM, ROWS, COLS), F32), hbm((TEAM, ROWS, COLS), F32),
            f32_block, bf_block, bf_block,
            bf_block, sds((TEAM, HEADS_OWN, HEAD, HEAD), F32), sds((HEADS_OWN, HEAD, HEAD)),
        ),
        scal,
        (enter, *raws, *pieces),
        grid=(TEAM,),
        in_specs=[by_i, *[full(ROWS, WIDTH)] * 4, *[full(*p.shape) for p in pieces]],
        out_specs=[
            by_i_wide, by_abs_wide, *[by_abs] * 6, full(TEAM, HEADS_OWN, HEAD, HEAD), full(HEADS_OWN, HEAD, HEAD),
        ],
        scratch=[pltpu.VMEM((ROWS, WIDTH), BF)],
        flops=3 << 30,
        nbytes=14 << 20,
    )


def local_kernel(info, ends, rates, q, k, v, mixed, dec):
    b = pl.program_id(0)

    @pl.when(b == 0)
    def _():
        decay_masks(info, rates, dec)

    same = same_seg(b, info, ends)
    for h in range(HEADS_OWN):
        at = slice(h * HEAD, (h + 1) * HEAD)
        scores = dot(q[0, :, at], k[0, :, at], NT)
        mixing = jnp.where(same, scores * dec[h], 0.0).astype(BF)
        mixed[0, :, at] = dot(mixing, v[0, :, at])


BLOCK_SPEC = pl.BlockSpec((1, ROWS, COLS), lambda i, *_: (i, 0, 0))


def attend_local(scal, q, k, v):
    return run(
        local_kernel,
        sds((TEAM, ROWS, COLS), F32),
        scal,
        (q, k, v),
        grid=(TEAM,),
        in_specs=[BLOCK_SPEC] * 3,
        out_specs=BLOCK_SPEC,
        scratch=[pltpu.VMEM((HEADS_OWN, BLOCK, BLOCK), F32)],
        flops=1 << 28,
        nbytes=3 << 20,
    )


def run_states(start, step, out, info, ends, rates, order):
    for h in range(HEADS_OWN):
        now = start[h]
        for b in order:
            out[b, h] = now.astype(BF)
            now = passing(b, info, ends, rates, h) * now + step[b, h]


def halves(i, value, keep, give):
    @pl.when(i < 2)
    def _():
        keep[0] = value

    @pl.when(i >= 2)
    def _():
        give[0] = value


def carry_kernel(info, ends, rates, local, q, pu, kv, s_in, wo, mixed, gated, keep, give, states):
    i = pl.program_id(0)
    a = block_abs(i, info)

    @pl.when(i == 0)
    def _():
        run_states(s_in, kv, states, info, ends, rates, range(TEAM))

    for h in range(HEADS_OWN):
        at = slice(h * HEAD, (h + 1) * HEAD)
        q_scale, _, _ = scales(a, info, ends, rates, h)
        qs = (q[0, :, at].astype(F32) * q_scale).astype(BF)
        m = local[0, :, at] + dot(qs, states[a, h])
        mixed[0, :, at] = m
        gated[0, :, at] = (pu[0, :, at] * rms(m)).astype(BF)
    halves(i, dot(gated[0], wo[...]).astype(BF), keep, give)


KEEP = pl.BlockSpec((1, ROWS, WIDTH), lambda i, *_: (jnp.minimum(i, 1), 0, 0))
GIVE = pl.BlockSpec((1, ROWS, WIDTH), lambda i, *_: (jnp.maximum(i - 2, 0), 0, 0))
BY_ABS = pl.BlockSpec((1, ROWS, COLS), lambda i, info, *_: (block_abs(i, info), 0, 0))
BY_ABS_WIDE = pl.BlockSpec((1, ROWS, WIDTH), lambda i, info, *_: (block_abs(i, info), 0, 0))
BY_I = pl.BlockSpec((1, ROWS, ROWS), lambda i, *_: (i, 0, 0))
BY_I_WIDE = pl.BlockSpec((1, ROWS, WIDTH), lambda i, *_: (i, 0, 0))
PAIR = sds((2, ROWS, WIDTH))


def carry_in(scal, local, q, pu, kv, s_in, wo):
    return run(
        carry_kernel,
        (sds((TEAM, ROWS, COLS), F32), sds((TEAM, ROWS, COLS)), PAIR, PAIR),
        scal,
        (local, q, pu, kv, s_in, wo),
        grid=(TEAM,),
        in_specs=[BY_ABS, BY_ABS, BY_ABS, full(*kv.shape), full(*s_in.shape), full(*wo.shape)],
        out_specs=[BY_ABS, BY_ABS, KEEP, GIVE],
        scratch=[pltpu.VMEM((TEAM, HEADS_OWN, HEAD, HEAD), BF)],
        flops=1 << 29,
        nbytes=8 << 20,
    )


def order_kernel(enter, g0, g1, g2, g3, g):
    i = pl.program_id(0)
    for t, raw in enumerate((g0, g1, g2, g3)):

        @pl.when(i == t)
        def _():
            g[0] = dot(enter[0], raw[...]).astype(BF)


def order(enter, raws):
    return run(
        order_kernel,
        sds((TEAM, ROWS, WIDTH)),
        (),
        (enter, *raws),
        grid=(TEAM,),
        in_specs=[BY_I, *[full(ROWS, WIDTH)] * 4],
        out_specs=BY_I_WIDE,
    )


def sglu_kernel(info, x, ta, tb, g, w,
                n2, product, gg, gu, r_keep, r_give, n_keep, n_give, wd, scr, back):
    i = pl.program_id(0)
    pieces = [w.at[p] for p in range(N_SHARD)]

    @pl.when(i == 0)
    def _():
        for p in range(N_SHARD):
            for c in range(4):
                at = 2 * FF_OWN + c * FF_PART
                wd[p * FF_PART : (p + 1) * FF_PART, c * 256 : (c + 1) * 256] = w[p, at : at + FF_PART]

    att = jnp.where(i < 2, ta[0].astype(F32), tb[0].astype(F32))
    scr[...] = rms(x[0].astype(F32) + att).astype(BF)
    n2[0] = scr[...]
    gate = up = None
    for j in range(N_SHARD):
        rows = scr[:, j * 256 : (j + 1) * 256]
        one, two = dot(rows, pieces[j][:FF_OWN], NT), dot(rows, pieces[j][FF_OWN : 2 * FF_OWN], NT)
        gate, up = (one, two) if j == 0 else (gate + one, up + two)
    prod = (gate * up).astype(BF)
    product[0] = prod
    g_prod = dot(g[0], wd[...], NT)
    one, two = (g_prod * up).astype(BF), (g_prod * gate).astype(BF)
    gg[0], gu[0] = one, two
    for j in range(N_SHARD):
        back[:, j * 256 : (j + 1) * 256] = (dot(one, pieces[j][:FF_OWN]) + dot(two, pieces[j][FF_OWN : 2 * FF_OWN])).astype(BF)
    halves(i, back[...], n_keep, n_give)
    halves(i, dot(prod, wd[...]).astype(BF), r_keep, r_give)


def sglu(info, x, ta, tb, g, w_ff):
    hid = pl.BlockSpec((1, ROWS, FF_OWN), lambda i, *_: (i, 0, 0))
    hid_out = sds((TEAM, ROWS, FF_OWN))
    return run(
        sglu_kernel,
        (sds((TEAM, ROWS, WIDTH)), hid_out, hid_out, hid_out, PAIR, PAIR, PAIR, PAIR),
        (info,),
        (x, ta, tb, g, w_ff),
        grid=(TEAM,),
        in_specs=[BY_I_WIDE, KEEP, GIVE, BY_I_WIDE, full(*w_ff.shape)],
        out_specs=[BY_I_WIDE, hid, hid, hid, KEEP, GIVE, KEEP, GIVE],
        scratch=[pltpu.VMEM((FF_OWN, WIDTH), BF), pltpu.VMEM((ROWS, WIDTH), BF), pltpu.VMEM((ROWS, WIDTH), BF)],
        mib=30,
    )


def flat(v):
    return v.reshape(-1, v.shape[-1])


def turn(i, first):
    return rel_of(i) if first == 1 else i


def grads_call(kernel, info, rows, args, specs, scratch=(), nbytes=0):
    shape = (2, rows, 256)
    return run(
        kernel,
        (sds(shape), sds(shape)),
        (info,),
        args,
        grid=(N_SHARD,),
        in_specs=specs,
        out_specs=[
            pl.BlockSpec((1, rows, 256), lambda i, *_: (jnp.minimum(i, 1), 0, 0)),
            pl.BlockSpec((1, rows, 256), lambda i, *_: (jnp.maximum(i - 2, 0), 0, 0)),
        ],
        scratch=scratch,
        nbytes=nbytes,
    )


def hidden_grads_kernel(info, n2, grad, keep, give):
    halves(pl.program_id(0), dot(grad[...], n2[...], TN).astype(BF), keep, give)


def hidden_grads(info, n2, grad, first):
    span = TEAM * ROWS
    specs = [
        pl.BlockSpec((span, 256), lambda i, info: (0, place(info, turn(i, first)))),
        full(span, FF_OWN),
    ]
    return grads_call(hidden_grads_kernel, info, FF_OWN, (flat(n2), flat(grad)), specs)


def down_grads(info, g, product, first):
    span = TEAM * ROWS

    def kernel(info, g, product, keep, give, dd):
        i = pl.program_id(0)

        @pl.when(i == 0)
        def _():
            for c in range(4):
                dd[c] = dot(product[...], g[:, c * 256 : (c + 1) * 256], TN).astype(BF)

        rows = pl.ds(pl.multiple_of(place(info, turn(i, first)) * FF_PART, 16), FF_PART)
        for c in range(4):
            at = slice(c * FF_PART, (c + 1) * FF_PART)

            @pl.when(i < 2)
            def _():
                keep[0, at] = dd[c, rows]

            @pl.when(i >= 2)
            def _():
                give[0, at] = dd[c, rows]

    specs = [full(span, WIDTH), full(span, FF_OWN)]
    return grads_call(
        kernel, info, FF_OWN, (flat(g), flat(product)), specs, scratch=[pltpu.VMEM((4, FF_OWN, 256), BF)]
    )


def hidden_back_kernel(info, ends, rates, x, ta, tb, ua, ub, g, wo, mixed, pu, q,
                       ga, gpu, gm, qg, gh, state):
    i = pl.program_id(0)
    a = block_abs(i, info)
    att = jnp.where(i < 2, ta[0].astype(F32), tb[0].astype(F32))
    gn2 = jnp.where(i < 2, ua[0].astype(F32), ub[0].astype(F32))
    grad = g[0].astype(F32) + rms_back(x[0].astype(F32) + att, gn2)
    ga[0] = grad.astype(BF)

    @pl.when(i == 0)
    def _():
        gh[...] = grad

    g_gated = dot(ga[0], wo[...], NT)
    for h in range(HEADS_OWN):
        at = slice(h * HEAD, (h + 1) * HEAD)
        m = mixed[0, :, at]
        gpu[0, :, at] = (g_gated[:, at] * rms(m)).astype(BF)
        gmb = rms_back(m, g_gated[:, at] * pu[0, :, at]).astype(BF)
        gm[0, :, at] = gmb
        q_scale, _, _ = scales(a, info, ends, rates, h)
        qs = (q[0, :, at].astype(F32) * q_scale).astype(BF)
        qg[a, h] = dot(qs, gmb, TN)

    @pl.when(i == TEAM - 1)
    def _():
        for h in range(HEADS_OWN):
            total = qg[TEAM - 1, h]
            for b in reversed(range(TEAM - 1)):
                total = passing(b, info, ends, rates, h) * total + qg[b, h]
            state[h] = total.astype(BF)


def hidden_back(scal, x, ta, tb, ua, ub, g, wo, mixed, pu, q):
    block = sds((TEAM, ROWS, COLS))
    return run(
        hidden_back_kernel,
        (
            sds((TEAM, ROWS, WIDTH)), block, block, sds((TEAM, HEADS_OWN, HEAD, HEAD), F32), sds((ROWS, WIDTH), F32),
            sds((HEADS_OWN, HEAD, HEAD)),
        ),
        scal,
        (x, ta, tb, ua, ub, g, wo, mixed, pu, q),
        grid=(TEAM,),
        in_specs=[BY_I_WIDE, KEEP, GIVE, KEEP, GIVE, BY_I_WIDE, full(*wo.shape), BY_ABS, BY_ABS, BY_ABS],
        out_specs=[
            BY_ABS_WIDE, BY_ABS, BY_ABS, full(TEAM, HEADS_OWN, HEAD, HEAD), full(ROWS, WIDTH), full(HEADS_OWN, HEAD, HEAD),
        ],
        flops=1 << 30,
        nbytes=14 << 20,
    )


def scores_back_kernel(info, ends, rates, q, k, v, gm, kv, s_in, gq, gk, gv, dec, states):
    b = pl.program_id(0)

    @pl.when(b == 0)
    def _():
        decay_masks(info, rates, dec)
        run_states(s_in, kv, states, info, ends, rates, range(TEAM))

    same = same_seg(b, info, ends)
    for h in range(HEADS_OWN):
        at = slice(h * HEAD, (h + 1) * HEAD)
        qh, kh, vh, gh = q[0, :, at], k[0, :, at], v[0, :, at], gm[0, :, at]
        q_scale, _, _ = scales(b, info, ends, rates, h)
        mixing = jnp.where(same, dot(qh, kh, NT) * dec[h], 0.0).astype(BF)
        g_scores = jnp.where(same, dot(gh, vh, NT) * dec[h], 0.0).astype(BF)
        gq[0, :, at] = dot(g_scores, kh) + q_scale * dot(gh, states[b, h], NT)
        gk[0, :, at] = dot(g_scores, qh, TN)
        gv[0, :, at] = dot(mixing, gh, TN)


def scores_back(scal, q, k, v, gm, kv, s_in):
    block = sds((TEAM, ROWS, COLS), F32)
    return run(
        scores_back_kernel,
        (block, block, block),
        scal,
        (q, k, v, gm, kv, s_in),
        grid=(TEAM,),
        in_specs=[*[BLOCK_SPEC] * 4, full(*kv.shape), full(*s_in.shape)],
        out_specs=[BLOCK_SPEC] * 3,
        scratch=[
            pltpu.VMEM((HEADS_OWN, BLOCK, BLOCK), F32),
            pltpu.VMEM((TEAM, HEADS_OWN, HEAD, HEAD), BF),
        ],
        flops=3 << 28,
        nbytes=6 << 20,
    )


def silu_slope(p):
    s = jax.nn.sigmoid(p)
    return s * (1.0 + p * (1.0 - s))


def project_back_kernel(info, ends, rates, gq, gk, gv, pq, pk, k, v, gpu, qg, g_in, w0, w1, w2, w3,
                        dqkv, keep, give, states, back):
    i = pl.program_id(0)
    a = block_abs(i, info)

    @pl.when(i == 0)
    def _():
        run_states(g_in, qg, states, info, ends, rates, (3, 2, 1, 0))

    dqkv[0, :, :COLS] = (gq[0] * silu_slope(pq[0])).astype(BF)
    for h in range(HEADS_OWN):
        at = slice(h * HEAD, (h + 1) * HEAD)
        _, k_scale, _ = scales(a, info, ends, rates, h)
        kh, vh = k[0, :, at], v[0, :, at]
        ks = (kh.astype(F32) * k_scale).astype(BF)
        g_k = gk[0, :, at] + k_scale * dot(vh, states[a, h], NT)
        to_k = slice(COLS + h * HEAD, COLS + (h + 1) * HEAD)
        to_v = slice(2 * COLS + h * HEAD, 2 * COLS + (h + 1) * HEAD)
        dqkv[0, :, to_k] = (g_k * silu_slope(pk[0, :, at])).astype(BF)
        dqkv[0, :, to_v] = (gv[0, :, at] + dot(ks, states[a, h])).astype(BF)
    refs = (w0, w1, w2, w3)
    grads = (dqkv[0, :, :COLS], dqkv[0, :, COLS : 2 * COLS], dqkv[0, :, 2 * COLS :], gpu[0])
    for j in range(N_SHARD):
        total = dot(grads[0], weight_at(refs, j, 0), NT)
        for t in (1, 2, 3):
            total = total + dot(grads[t], weight_at(refs, j, t), NT)
        back[:, lanes(j, info)] = total.astype(BF)
    halves(i, back[...], keep, give)


def project_back(scal, gq, gk, gv, pq, pk, k, v, gpu, qg, g_in, pieces):
    return run(
        project_back_kernel,
        (sds((TEAM, ROWS, 3 * COLS)), PAIR, PAIR),
        scal,
        (gq, gk, gv, pq, pk, k, v, gpu, qg, g_in, *pieces),
        grid=(TEAM,),
        in_specs=[*[BY_ABS] * 8, full(*qg.shape), full(*g_in.shape), *[full(*p.shape) for p in pieces]],
        out_specs=[pl.BlockSpec((1, ROWS, 3 * COLS), lambda i, info, *_: (block_abs(i, info), 0, 0)), KEEP, GIVE],
        scratch=[pltpu.VMEM((TEAM, HEADS_OWN, HEAD, HEAD), BF), pltpu.VMEM((ROWS, WIDTH), BF)],
        flops=5 << 29,
        nbytes=14 << 20,
    )


def column_grads(info, pairs, first):
    span = TEAM * ROWS
    args, specs = [], []
    for pair in pairs:
        for v in pair:
            args.append(v.reshape(span, v.shape[-1]))
            wide = v.shape[-1] == WIDTH
            cut = (lambda i, info: (0, place(info, turn(i, first)))) if wide else (lambda i, info: (0, 0))
            specs.append(pl.BlockSpec((span, 256 if wide else v.shape[-1]), cut))
    n = sum(1 if b.shape[-1] == WIDTH else b.shape[-1] // 256 for _, b in pairs)

    def kernel(info, *refs):
        i = pl.program_id(0)
        values = []
        for t in range(len(pairs)):
            value = dot(refs[2 * t][...], refs[2 * t + 1][...], TN).astype(BF)
            values += [value[:, c * 256 : (c + 1) * 256] for c in range(value.shape[1] // 256)]
        for t, value in enumerate(values):
            at = slice(t * 256, (t + 1) * 256)

            @pl.when(i < 2)
            def _():
                refs[-2][0, at] = value

            @pl.when(i >= 2)
            def _():
                refs[-1][0, at] = value

    return grads_call(kernel, info, n * 256, tuple(args), specs)


def hop(parts, first, hold=(), hold_send=()):
    keep, give = parts
    if hold_send:
        give = after(give, *hold_send)
    got = send(give, "shard", first)
    if hold:
        got = after(got, *hold)
    total = keep.astype(F32) + got.astype(F32)
    return total[0].astype(BF), total[1].astype(BF)


def hop_two(own, other, first):
    return own, send(other, "shard", 3 - first)


def joined(terms, hold=()):
    if hold:
        terms = [(own, after(got, *hold)) for own, got in terms]
    return jnp.concatenate([(own.astype(F32) + got.astype(F32)).astype(BF) for own, got in terms], 0)


def over_zh(part, hold=()):
    got = send(part, "zh", 1)
    if hold:
        got = after(got, *hold)
    return (part.astype(F32) + got.astype(F32)).astype(BF)


def fin_out_kernel(info, p0, p1, p2, p3, fin, stack):
    unit = jnp.where(
        lax.broadcasted_iota(jnp.int32, (256, 256), 0) == lax.broadcasted_iota(jnp.int32, (256, 256), 1), 1.0, 0.0
    ).astype(BF)
    for j, p in enumerate((p0, p1, p2, p3)):
        q = info[0] ^ j
        for n in range(2 * N_SHARD):
            start = pl.multiple_of(n * FF_OWN + q * FF_PART, 16)
            stack[pl.ds(start, FF_PART)] = p[n * FF_PART : (n + 1) * FF_PART]
    for n in range(11):
        fin[:, n * 512 : (n + 1) * 512] = dot(unit, stack[n * 512 : (n + 1) * 512], NT)


def fin_out(info, pieces):
    return run(
        fin_out_kernel,
        sds((256, 8 * FF_OWN), F32),
        (info,),
        tuple(pieces),
        in_specs=[full(2 * FF_OWN, 256)] * 4,
        out_specs=full(256, 8 * FF_OWN),
        scratch=[pltpu.VMEM((8 * FF_OWN, 256), BF)],
        mib=24,
        flops=1 << 30,
        nbytes=9 << 20,
    )


def down_out_kernel(info, p0, p1, p2, p3, down):
    for j, p in enumerate((p0, p1, p2, p3)):
        rows = pl.ds(pl.multiple_of((info[0] ^ j) * FF_PART, 16), FF_PART)
        for c in range(4):
            down[rows, c * 256 : (c + 1) * 256] = p[c * FF_PART : (c + 1) * FF_PART].astype(F32)


def down_out(info, pieces):
    return run(
        down_out_kernel,
        sds((FF_OWN, WIDTH), F32),
        (info,),
        tuple(pieces),
        in_specs=[full(*p.shape) for p in pieces],
        out_specs=full(FF_OWN, WIDTH),
        nbytes=5 << 20,
    )


def last_out_kernel(info, q0, q1, q2, q3, d0, d1, d2, d3, o0, o1, o2, o3, g_q, g_k, g_v, g_u, g_out):
    for j, (p, d, o) in enumerate(zip((q0, q1, q2, q3), (d0, d1, d2, d3), (o0, o1, o2, o3))):
        at = pl.ds(pl.multiple_of((info[0] ^ j) * 256, 256), 256)
        for t, out in enumerate((g_q, g_k, g_v)):
            out[:, at] = p[t * 256 : (t + 1) * 256].astype(F32)
        g_u[:, at] = d[FF_OWN + 256 :].astype(F32)
        g_out[:, lanes(j, info)] = o[...].astype(F32)


def last_out(info, pieces):
    return run(
        last_out_kernel,
        (sds((256, WIDTH), F32),) * 5,
        (info,),
        tuple(pieces),
        in_specs=[full(*p.shape) for p in pieces],
        out_specs=[full(256, WIDTH)] * 5,
    )


def finish_kernel(x, gh, here, got, enter, out):
    gn = here[...] + got[...].astype(F32)
    grad = (gh[...] + rms_back(x[0].astype(F32), gn)).astype(BF)
    out[...] = dot(enter[0], grad, TN).astype(BF)


def result_kernel(x, att, here, got, enter, out):
    result = (x[0].astype(F32) + att[0].astype(F32) + here[...] + got[...].astype(F32)).astype(BF)
    out[...] = dot(enter[0], result, TN).astype(BF)


def finish(kernel, x, second, here, got, enter):
    first = lambda v: pl.BlockSpec((1, *v.shape[1:]), lambda _: (0,) * v.ndim) if v.ndim == 3 else full(*v.shape)
    args = (x, second, here, got, enter)
    return run(
        kernel,
        sds((ROWS, WIDTH)),
        (),
        args,
        in_specs=[first(v) for v in args],
        out_specs=full(ROWS, WIDTH),
        flops=1 << 28,
        nbytes=4 << 20,
    )


def unsort_kernel(leave, rows, out):
    out[...] = dot(leave[...], rows[...], TN).astype(BF)


def unsort(leave, rows):
    return run(
        unsort_kernel,
        sds((ROWS, WIDTH)),
        (),
        (leave, rows),
        in_specs=[full(ROWS, ROWS), full(ROWS, WIDTH)],
        out_specs=full(ROWS, WIDTH),
        flops=1 << 28,
        nbytes=2 << 20,
    )


def exchange(rows):
    return lax.all_to_all(rows, ALL, split_axis=0, concat_axis=0, tiled=True)


def team_raw(own):
    pair = send(own, "zl", 1)
    return [own, pair, send(own, "core", 1), send(pair, "core", 1)]


def team_sum(keep, give, hold=()):
    got = send(give, "core", 1)
    half = (keep.astype(F32) + got.astype(F32)).astype(BF)
    other = send(half, "zl", 1)
    if hold:
        other = after(other, *hold)
    ours = (half.astype(F32) + other[::-1].astype(F32)).astype(BF)
    return ours, send(ours, "core", 1), half


def team_own(keep, give, *behind):
    there = keep[1].astype(F32) + send(give[1], "core", 1).astype(F32)
    here = keep[0].astype(F32) + send(give[0], "core", 1).astype(F32)
    there = there.astype(BF)
    if behind:
        there = after(there, *behind)
    return here, send(there, "zl", 1)


def state_in(state, near, whole, cross, hold=()):
    low = [state] + [lax.ppermute(state, "shard", [(i, i ^ j) for i in range(4)]) for j in (1, 2, 3)]
    wide = [v.astype(F32) for v in low]
    hand = sum(whole[j][:, None, None] * wide[j] for j in range(4))
    if hold:
        hand = after(hand, *hold)
    got = send(hand, "zh", 1)
    here = sum(near[j][:, None, None] * wide[j] for j in (1, 2, 3))
    return here + cross[:, None, None] * got, hand


def fast_body(tokens_in, cotangent, deal_order, lengths, decay_rates, w_query, w_key, w_value, w_ugate, w_out, w_ffin, w_ffdown):
    zh, zl, core, shard = (lax.axis_index(a) for a in ALL)
    me = zl * 2 + core
    group = zh * N_SHARD + shard
    device = (zh * TEAM + me) * N_SHARD + shard
    span = TEAM * ROWS
    info = jnp.stack([me, shard, group * span, device, zh, jnp.int32(0), jnp.int32(0), jnp.int32(0)]).astype(jnp.int32)
    ends = jnp.sum(jnp.where(jnp.arange(8)[None, :] <= jnp.arange(8)[:, None], lengths[None, :], 0), axis=1).astype(jnp.int32)
    scal = (info, ends, decay_rates)
    by_device = deal_order.reshape(2, N_SHARD, TEAM, ROWS).transpose(0, 2, 1, 3).reshape(DEVICES, ROWS)

    leave, sent_x = exchange_rows(info, by_device, *far(tokens_in))
    raw_x = exchange(sent_x)
    quarter = take_quarter(after(info, sent_x), *far(w_query, w_key, w_value, w_ugate))
    w_proj = gather_pieces(quarter)
    enter, sent_g = exchange_orders(after(info, quarter), by_device, leave, *far(cotangent))
    bundle = ff_bundle(after(info, quarter), *far(w_ffin, w_ffdown))
    w_ff = lax.all_gather(after(bundle, raw_x), "shard", axis=0)
    wo = gather_out(w_out, me, shard)
    x_raws = team_raw(raw_x)
    g_raws = team_raw(exchange(after(sent_g, raw_x)))

    rates = lax.dynamic_slice_in_dim(decay_rates, me * HEADS_OWN, HEADS_OWN)

    def seg_at(p):
        seg = jnp.sum((p[..., None] >= ends).astype(jnp.int32), axis=-1)
        return jnp.where(p < 0, -1, seg)

    def weigh(flag, gap):
        return jnp.where(flag[..., None], jnp.exp(-(jnp.maximum(gap, 0) * span).astype(F32)[..., None] * rates), 0.0)

    peers = zh * N_SHARD + (shard ^ jnp.arange(4))
    peers_last, peers_before = seg_at((peers + 1) * span - 1), seg_at(peers * span - 1)
    my_last, my_before = peers_last[0], peers_before[0]
    end, start = zh * N_SHARD + 3, zh * N_SHARD
    f_near = weigh((peers < group) & (peers_last == my_before), group - 1 - peers)
    f_whole = weigh(peers_last == seg_at((end + 1) * span - 1), end - peers)
    f_cross = weigh((zh == 1) & (seg_at(start * span - 1) == my_before), shard)
    b_near = weigh((peers > group) & (peers_before == my_last), peers - 1 - group)
    b_whole = weigh(peers_before == seg_at(start * span - 1), peers - start)
    b_cross = weigh((zh == 0) & (seg_at((end + 1) * span - 1) == my_last), 3 - shard)

    x, normed, pq, pk, pu, q, k, v, kv, state = project(scal, enter, far(*x_raws), far(*w_proj))
    s_in, _ = state_in(state, f_near, f_whole, f_cross)
    local = attend_local(scal, q, k, v)
    mixed, gated, a_keep, a_give = carry_in((after(info, g_raws[1]), *scal[1:]), local, q, pu, kv, s_in, wo)
    g = order(*far(enter), far(*g_raws))
    ta, tb, _ = team_sum(a_keep, a_give, hold=(g,))
    n2, product, gg, gu, r_keep, r_give, n_keep, n_give = sglu(info, x, ta, *far(tb, g), *far(w_ff))
    n_got = send(n_give, "core", 1)
    d_gate = hidden_grads(info, n2, gg, 1)
    n_half = (n_keep.astype(F32) + n_got.astype(F32)).astype(BF)
    n_other = send(n_half, "zl", 1)
    d_up = hidden_grads(after(info, n_half), n2, gu, 2)
    d_down = down_grads(after(info, d_up[1]), g, product, 1)
    gate_own, gate_other = hop(d_gate, 1, hold=(d_down[1],))
    n_other = after(n_other, d_down[1], gate_other)
    ua = (n_half.astype(F32) + n_other[::-1].astype(F32)).astype(BF)
    ub = send(ua, "core", 1)
    up_own, up_other = hop(d_up, 2, hold=(ua,))

    ga, gpu, gm, qg, gh, g_state = hidden_back(
        (after(info, up_other), *scal[1:]), x, ta, *far(tb), ua, *far(ub), g, wo, mixed, pu, q
    )
    gate = hop_two(gate_own, gate_other, 1)
    up = hop_two(up_own, up_other, 2)
    gq, gk, gv = scores_back(scal, q, k, v, gm, kv, s_in)
    r_here, r_there = team_own(r_keep, r_give, ua)
    g_in, handed = state_in(g_state, b_near, b_whole, b_cross, hold=(r_there,))
    d_ou = column_grads(after(info, handed), [(gated, ga), (normed, gpu)], 2)
    fin = joined((gate, up), hold=(d_ou[1],))
    dqkv, p_keep, p_give = project_back(
        (after(info, fin), *scal[1:]), gq, gk, gv, pq, pk, k, v, gpu, qg, g_in, far(*w_proj)
    )
    here, there = team_own(p_keep, p_give)
    d_qkv = column_grads(info, [(normed, dqkv)], 1)
    last_sent = finish(finish_kernel, x, gh, here, there, after(enter, d_qkv[1]))
    input_grad = unsort(leave, exchange(last_sent))
    output = unsort(leave, exchange(finish(result_kernel, x, ta, r_here, r_there, after(enter, last_sent))))

    down_own, down_other = hop(d_down, 1, hold=(last_sent,), hold_send=(handed,))
    ou_own, ou_other = hop(d_ou, 2, hold=(down_other,))
    fin_sum = over_zh(fin, hold=(ou_other,))
    fin_pair = send(fin_sum, "zl", 1)
    fin_all = [fin_sum, send(fin_sum, "core", 1), fin_pair, send(fin_pair, "core", 1)]
    down_ou = joined((hop_two(down_own, down_other, 1), hop_two(ou_own, ou_other, 2)), hold=(fin_sum,))
    qkv_own, qkv_other = hop(d_qkv, 1, hold=(last_sent,))
    qkv = joined((hop_two(qkv_own, qkv_other, 1),))
    down_sum = over_zh(down_ou, hold=(fin_pair, input_grad))
    down_pair = send(down_sum, "zl", 1)
    down_all = [down_sum, send(down_sum, "core", 1), down_pair, send(down_pair, "core", 1)]
    grad_fin = fin_out(info, far(*fin_all))
    grad_down = down_out(info, far(*down_all))
    outs = []
    for j in range(4):
        pick = me ^ shard ^ j
        top = [p[FF_OWN : FF_OWN + 256] for p in down_all]
        piece = jnp.where(pick < 2, jnp.where(pick == 0, top[0], top[1]), jnp.where(pick == 2, top[2], top[3]))
        outs.append(piece if j == 0 else send(piece, "shard", j))
    qkv_sum = over_zh(qkv, hold=(down_pair, output, fin_all[3]))
    qkv_pair = send(qkv_sum, "zl", 1)
    qkv_late = after(qkv_pair, grad_fin, grad_down, *outs[1:])
    qkv_all = [qkv_sum, send(qkv_sum, "core", 1), qkv_late, send(qkv_late, "core", 1)]
    grad_q, grad_k, grad_v, grad_u, grad_out = last_out(info, far(*qkv_all, *down_all, *outs))
    return (output, input_grad, grad_q, grad_k, grad_v, grad_u, grad_out, grad_fin, grad_down)


def solution(mesh):
    rep, shard = mesh.shape["rep"], mesh.shape["shard"]
    team = Mesh(mesh.devices.reshape(rep // TEAM, 2, 2, shard), ALL)
    token, weight = P(ALL, None), P("shard", None)
    return jax.shard_map(
        fast_body if (rep, shard) == (8, 4) else general_body,
        mesh=team,
        in_specs=(token, token, P(), P(), P(), *([weight] * 7)),
        out_specs=(token, token, *([weight] * 7)),
        check_vma=False,
    )
```
